256 devices in a mesh: context: 32 (over z, y_hi, core), tensor: 8 (over y_lo, x).
Axes of the slice: x: 4, y: 4 (y_hi: 2, y_lo: 2; y = y_hi * 2 + y_lo), z: 8, core: 2. Of those that a mesh axis runs over, the one named last changes fastest.
Arguments:
- query_proj: bfloat16 [8192, 8192], P('context', 'tensor'), may hold values from -6 to 6
- key_proj: bfloat16 [8192, 8192], P('context', 'tensor'), may hold values from -6 to 6
- value_proj: bfloat16 [8192, 8192], P('context', 'tensor'), may hold values from -6 to 6
- short_taps: float32 [3, 3, 8192], P(None, None, 'tensor'), may hold values from -3 to 3
- long_filter: bfloat16 [8192, 8192], P('tensor', 'context'), may hold values from -0.0625 to 0.0625
- skip_weight: float32 [8192], P('tensor'), may hold values from -4 to 4
- out_weight: bfloat16 [8192, 4096], P('tensor'), may hold values from -0.09375 to 0.09375
- norm_gain: float32 [4096], P('tensor'), may hold values from 0.5 to 1.5
Outputs:
- normed: bfloat16 [8192, 4096], P('context', 'tensor')
The draws below stay inside these ranges and needn't reach their ends.
All inputs are finite; a program needn't handle non-finite values.
Results may differ from the reference program's by a relative error of at most 0.019.
Values may be sent and summed in bfloat16 or wider, within the bound.
A program may use at most 64 MiB of HBM per device.

```python
import jax
import jax.numpy as jnp
from jax import lax

D = 8192
E = 4096
L = 8192
D_DEV = 1024
GROUPS = 8


def strengthened(array, rng, source, target, parts, factor):
    def block_of(axis_at):
        return (jnp.arange(array.shape[axis_at]) // (array.shape[axis_at] // parts)).reshape((-1,) + (1,) * (array.ndim - 1 - axis_at))

    first = jax.random.permutation(rng, parts)[block_of(target)]
    second = (block_of(target) + parts // 2) % parts
    return jnp.where((block_of(source) == first) | (block_of(source) == second), factor * array, array)


def block_scale(rng, extent, pieces, smallest, largest):
    loudness = 1.0
    for axis_at, parts in pieces:
        heights = jax.random.uniform(jax.random.fold_in(jax.random.fold_in(rng, 6), axis_at), (parts,), jnp.float32, smallest / len(pieces), largest / len(pieces))
        loudness = loudness * jnp.repeat(jnp.exp(heights), extent[axis_at] // parts).reshape((-1,) + (1,) * (len(extent) - 1 - axis_at))
    return loudness


def normal_values(stream_key, dims, spread, bound, split=(), kind=jnp.bfloat16):
    loudness = block_scale(stream_key, dims, split, -0.22, 0.18) if split else 1.0
    entries = jax.random.normal(stream_key, dims, jnp.float32) * spread * loudness
    return jnp.minimum(jnp.maximum(entries, -bound), bound).astype(kind)


def gaussian_with(own_key, shape, width, reach, shards, heavy, dtype=jnp.bfloat16):
    entries = width * jax.random.normal(own_key, shape, jnp.float32)
    if shards:
        entries = entries * block_scale(own_key, shape, shards, -0.22, 0.18)
    return jnp.clip(strengthened(entries, jax.random.fold_in(own_key, 3), *heavy), -reach, reach).astype(dtype)


def setup_inputs(seed: int = 0) -> dict:
    seeds = jax.random.split(jax.random.key(seed), 9)
    query_proj = normal_values(seeds[0], (L, D), 1.0, 6.0, ((0, 32), (1, 8)))
    key_proj = normal_values(seeds[1], (L, D), 1.0, 6.0, ((0, 32), (1, 8)))
    value_proj = normal_values(seeds[2], (L, D), 1.0, 6.0, ((0, 32), (1, 8)))
    short_taps = normal_values(seeds[3], (3, 3, D), 0.6, 3.0, ((2, 8),), jnp.float32)
    long_filter = normal_values(seeds[4], (D, L), L ** -0.5, 0.0625, ((0, 8), (1, 32)))
    skip_weight = normal_values(seeds[5], (D,), 1.0, 4.0, ((0, 8),), jnp.float32)
    out_weight = gaussian_with(seeds[6], (D, E), D ** -0.5, 0.09375, ((0, 8),), (0, 1, 8, 2.0))
    norm_gain = jnp.clip(1.0 + 0.1 * jax.random.normal(seeds[7], (E,), jnp.float32), 0.5, 1.5)
    return dict(query_proj=query_proj, key_proj=key_proj, value_proj=value_proj, short_taps=short_taps, long_filter=long_filter, skip_weight=skip_weight, out_weight=out_weight, norm_gain=norm_gain)


def featurize(values, taps):
    lagged_one = jnp.pad(values, ((1, 0), (0, 0)))[:-1]
    lagged_two = jnp.pad(values, ((2, 0), (0, 0)))[:-2]
    return taps[0] * values + taps[1] * lagged_one + taps[2] * lagged_two

def convolve_block(pair):
    signal, kernel = pair
    span = signal.shape[1]
    spectrum = jnp.fft.rfft(signal, n=2 * span, axis=1) * jnp.fft.rfft(kernel, n=2 * span, axis=1)
    return jnp.fft.irfft(spectrum, n=2 * span, axis=1)[:, :span].astype(jnp.float32)

def reference(query_proj, key_proj, value_proj, short_taps, long_filter, skip_weight, out_weight, norm_gain):
    query_feat = featurize(query_proj.astype(jnp.float32), short_taps[0])
    key_feat = featurize(key_proj.astype(jnp.float32), short_taps[1])
    value_feat = featurize(value_proj.astype(jnp.float32), short_taps[2])
    mixed_in = (key_feat * value_feat).astype(jnp.bfloat16)
    mixed_wide = lax.optimization_barrier(mixed_in).astype(jnp.float32)
    block = min(D, 512)
    signal = mixed_wide.T.reshape(D // block, block, L)
    kernel = long_filter.astype(jnp.float32).reshape(D // block, block, L)
    convolved = lax.map(convolve_block, (signal, kernel)).reshape(D, L).T.astype(jnp.bfloat16)
    convolved_wide = lax.optimization_barrier(convolved).astype(jnp.float32)
    gated = (query_feat * (convolved_wide + skip_weight * mixed_wide)).astype(jnp.bfloat16)
    total = jnp.zeros((L, E), jnp.float32)
    for group in range(GROUPS):
        lower = group * D_DEV
        term = jnp.dot(gated[:, lower:lower + D_DEV], out_weight[lower:lower + D_DEV], preferred_element_type=jnp.float32).astype(jnp.bfloat16)
        total = total + lax.optimization_barrier(term).astype(jnp.float32)
    meansq = lax.optimization_barrier(jnp.mean(total * total, axis=1, keepdims=True))
    return (total * lax.rsqrt(meansq + 1e-06) * norm_gain).astype(jnp.bfloat16)
```

```python
import functools
import math

import jax
import jax.numpy as jnp
import ml_dtypes
import numpy as np
from jax import lax
from jax.experimental import pallas as pl
from jax.experimental.pallas import tpu as pltpu
from jax.sharding import PartitionSpec as P

F32, BF16 = jnp.float32, jnp.bfloat16
CTX, TEN = "context", "tensor"
HALO = 16
LANES = 128
PART = 16
SHIFT = 0.25
INNER = 8
TOKENS_PER_PART = 128


def times(z, c):
    re, im = z
    cr, ci = float(c.real), float(c.imag)
    cr = 0.0 if abs(cr) < 1e-12 else cr
    ci = 0.0 if abs(ci) < 1e-12 else ci
    if im is None:
        if ci == 0.0:
            return (re if cr == 1.0 else re * cr, None)
        return (re * cr, re * ci)
    if ci == 0.0:
        return z if cr == 1.0 else (re * cr, im * cr)
    if cr == 0.0:
        return (im * -ci, re * ci)
    if abs(abs(cr) - abs(ci)) < 1e-12:
        plus, minus = re + im, re - im
        if (cr > 0) == (ci > 0):
            return (minus * cr, plus * cr)
        return (plus * cr, minus * ci)
    return (re * cr - im * ci, re * ci + im * cr)


def real_part_times(z, c):
    re, im = z
    cr, ci = float(c.real), float(c.imag)
    if im is None or abs(ci) < 1e-12:
        return re if cr == 1.0 else re * cr
    return re * cr - im * ci


def plus_minus(a, b):
    (ar, ai), (br, bi) = a, b
    if ai is None and bi is None:
        return (ar + br, None), (ar - br, None)
    if ai is None:
        return (ar + br, bi), (ar - br, -bi)
    if bi is None:
        return (ar + br, ai), (ar - br, ai)
    return (ar + br, ai + bi), (ar - br, ai - bi)


def dft(x, sign):
    n = len(x)
    if n == 1:
        return list(x)
    even, odd = dft(x[0::2], sign), dft(x[1::2], sign)
    low, high = [], []
    for k in range(n // 2):
        e, o = even[k], odd[k]
        if 4 * k == n and e[1] is not None and o[1] is not None:
            s = float(sign)
            one = (e[0] - o[1], e[1] + o[0])
            two = (e[0] + o[1], e[1] - o[0])
            a, b = (one, two) if s > 0 else (two, one)
        else:
            a, b = plus_minus(e, times(o, turn(sign * k / n)))
        low.append(a)
        high.append(b)
    return low + high


def turn(x):
    return complex(math.cos(2 * math.pi * x), math.sin(2 * math.pi * x))


def im_of(z):
    return jnp.zeros_like(z[0]) if z[1] is None else z[1]


def split_table(x):
    high = x.astype(ml_dtypes.bfloat16)
    low = (x - high.astype(np.float64)).astype(ml_dtypes.bfloat16)
    return np.stack([high, low])


def tables(blocks):
    length = blocks * LANES
    t = np.arange(LANES)
    phase = np.outer(t, t) % LANES / LANES
    forward = np.exp(-2j * np.pi * phase)
    backward = np.exp(2j * np.pi * phase) / length
    pair = lambda w: np.block([[w.real, w.imag], [-w.imag, w.real]])
    twist = np.exp(-2j * np.pi * np.outer(np.arange(blocks) + SHIFT, t) / length)
    return (
        split_table(pair(forward)),
        split_table(pair(backward)),
        np.stack([twist.real, twist.imag]).astype(np.float32),
    )


def kernel(
    nc,
    nt,
    q_hbm,
    k_hbm,
    v_hbm,
    filt_hbm,
    w_hbm,
    fwd_hbm,
    bwd_hbm,
    taps,
    skip,
    gain,
    twist,
    out,
    qbuf,
    kbuf,
    vbuf,
    wbuf,
    fwd,
    bwd,
    qfeat,
    mixed,
    mixed_t,
    frecv,
    srecv,
    csend,
    crecv,
    mid,
    high,
    low,
    fspec,
    dspec,
    gated,
    psend,
    precv,
    total,
    ssend,
    srow,
    load_sem,
    halo_send,
    halo_recv,
    filt_send,
    filt_recv,
    sig_send,
    sig_recv,
    conv_send,
    conv_recv,
    part_send,
    part_recv,
    row_send,
    row_recv,
):
    me, mt = lax.axis_index(CTX), lax.axis_index(TEN)
    tokens, width = q_hbm.shape
    per = width // nc
    parts = per // PART
    halves = tokens // LANES
    blocks = nc * halves
    outer = blocks // INNER
    step_s = INNER // halves
    share = out.shape[1]
    chunks = tokens // TOKENS_PER_PART

    def partner(j, mine, n):
        step = j // 2 + 1
        odd = j % 2
        return (mine + step * (1 - odd) + (n - step) * odd) % n

    def remote(src, dst, send, recv, device):
        return pltpu.make_async_remote_copy(
            src_ref=src,
            dst_ref=dst,
            send_sem=send,
            recv_sem=recv,
            device_id=device,
            device_id_type=pl.DeviceIdType.MESH,
        )

    body = pl.ds(HALO, tokens)
    loads = [
        pltpu.make_async_copy(src, dst, load_sem.at[i])
        for i, (src, dst) in enumerate(
            (
                (k_hbm, kbuf.at[body, :]),
                (v_hbm, vbuf.at[body, :]),
                (q_hbm, qbuf.at[body, :]),
                (fwd_hbm, fwd),
                (bwd_hbm, bwd),
                (w_hbm, wbuf),
            )
        )
    ]
    for copy in loads:
        copy.start()

    barrier = pltpu.get_barrier_semaphore()

    @pl.loop(0, nc - 1)
    def _(j):
        pl.semaphore_signal(barrier, inc=1, device_id={CTX: partner(j, me, nc)})

    @pl.loop(0, nt - 1)
    def _(j):
        pl.semaphore_signal(barrier, inc=1, device_id={TEN: partner(j, mt, nt)})

    pl.semaphore_wait(barrier, nc - 1 + nt - 1)

    halos = [
        remote(
            src.at[pl.ds(tokens - HALO, HALO), :],
            dst.at[pl.ds(0, HALO), :],
            halo_send.at[i],
            halo_recv.at[i],
            {CTX: (me + 1) % nc},
        )
        for i, (src, dst) in enumerate(((k_hbm, kbuf), (v_hbm, vbuf), (q_hbm, qbuf)))
    ]

    @pl.when(me < nc - 1)
    def _():
        for copy in halos:
            copy.start()

    @pl.when(me == 0)
    def _():
        for buf in (kbuf, vbuf, qbuf):
            buf[pl.ds(0, HALO), :] = jnp.zeros((HALO, width), BF16)

    def filter_copy(p):
        return remote(
            filt_hbm.at[pl.ds(pl.multiple_of(p * per, PART), per), :],
            frecv.at[me],
            filt_send.at[p],
            filt_recv.at[me],
            {CTX: p},
        )

    @pl.loop(0, nc - 1)
    def _(j):
        filter_copy(partner(j, me, nc)).start()

    own_filter = pltpu.make_async_copy(
        filt_hbm.at[pl.ds(pl.multiple_of(me * per, PART), per), :], frecv.at[me], filt_recv.at[me]
    )
    own_filter.start()

    def feature(buf, r, row, lane):
        wide = buf[pl.ds(row, LANES + HALO), lane].astype(F32)[HALO - 8 :]
        one = pltpu.roll(wide, 1, 0)[8:]
        two = pltpu.roll(wide, 2, 0)[8:]
        return (
            taps[r, pl.ds(0, 1), lane] * wide[8:]
            + taps[r, pl.ds(1, 1), lane] * one
            + taps[r, pl.ds(2, 1), lane] * two
        )

    columns = width // LANES

    def place(i):
        row = pl.multiple_of(i // columns * LANES, LANES)
        col = pl.multiple_of(i % columns * LANES, LANES)
        return row, col

    for i in (0, 1):
        loads[i].wait()

    @pl.when(me > 0)
    def _():
        for i in (0, 1):
            halos[i].wait_recv()

    @pl.loop(0, halves * columns)
    def _(i):
        row, col = place(i)
        lane = pl.ds(col, LANES)
        product = feature(kbuf, 1, row, lane) * feature(vbuf, 2, row, lane)
        mixed[pl.ds(row, LANES), lane] = product.astype(BF16)
        mixed_t[pl.ds(col, LANES), pl.ds(row, LANES)] = product.T.astype(BF16)

    def signal_copy(part, p):
        return remote(
            mixed_t.at[pl.ds(pl.multiple_of(p * per + part * PART, PART), PART), :],
            srecv.at[me, pl.ds(part * PART, PART), :],
            sig_send.at[part, p],
            sig_recv.at[part, me],
            {CTX: p},
        )

    for part in range(parts):

        @pl.loop(0, nc - 1)
        def _(j):
            signal_copy(part, partner(j, me, nc)).start()

        pltpu.make_async_copy(
            mixed_t.at[pl.ds(pl.multiple_of(me * per + part * PART, PART), PART), :],
            srecv.at[me, pl.ds(part * PART, PART), :],
            sig_recv.at[part, me],
        ).start()

    loads[2].wait()

    @pl.when(me > 0)
    def _():
        halos[2].wait_recv()

    @pl.loop(0, halves * columns)
    def _(i):
        row, col = place(i)
        lane = pl.ds(col, LANES)
        qfeat[pl.ds(row, LANES), lane] = feature(qbuf, 0, row, lane)

    def block_of(k1):
        return pl.ds(k1 * PART, PART)

    left, right = pl.ds(0, LANES), pl.ds(LANES, LANES)

    def outer_forward(recv, part):
        rows = pl.ds(pl.multiple_of(part * PART, PART), PART)
        for b in range(INNER):
            lane = pl.ds(b % halves * LANES, LANES)
            x = [
                times((recv[step_s * a + b // halves, rows, lane].astype(F32), None), turn(-a * SHIFT / outer))
                for a in range(outer)
            ]
            for q, z in enumerate(dft(x, -1)):
                re, im = times(z, turn(-b * (q + SHIFT) / blocks))
                mid[b, q, 0] = re
                mid[b, q, 1] = jnp.zeros_like(re) if im is None else im
        for q in range(outer):
            y = [(mid[b, q, 0], mid[b, q, 1]) for b in range(INNER)]
            for r, (re, im) in enumerate(dft(y, -1)):
                k1 = q + outer * r
                cos, sin = twist[0, pl.ds(k1, 1), :], twist[1, pl.ds(k1, 1), :]
                put(k1 * PART, re * cos - im * sin, im * cos + re * sin)

    def put(row, re, im):
        rows = pl.ds(row, re.shape[0])
        for lane, x in ((left, re), (right, im)):
            top = x.astype(BF16)
            high[rows, lane] = top
            low[rows, lane] = (x - top.astype(F32)).astype(BF16)

    def product(rows, table):
        a, b = high[rows, :], low[rows, :]
        dot = functools.partial(jnp.dot, preferred_element_type=F32)
        return dot(a, table[0]) + dot(b, table[0]) + dot(a, table[1])

    tall = min(256, blocks * PART)

    @pl.loop(0, nc)
    def _(s):
        pltpu.make_async_copy(frecv.at[s], frecv.at[s], filt_recv.at[s]).wait()

    for i in (3, 4):
        loads[i].wait()

    @pl.loop(0, parts)
    def _(part):
        outer_forward(frecv, part)

        @pl.loop(0, blocks * PART // tall)
        def _(i):
            rows = pl.ds(pl.multiple_of(i * tall, tall), tall)
            fspec[part, rows, :] = product(rows, fwd)

    def conv_copy(part, p):
        return remote(
            csend.at[p, pl.ds(pl.multiple_of(part * PART, PART), PART), :],
            crecv.at[pl.ds(pl.multiple_of(me * per + part * PART, PART), PART), :],
            conv_send.at[part, p],
            conv_recv.at[part, me],
            {CTX: p},
        )

    @pl.loop(0, parts)
    def _(part):
        rows16 = pl.ds(pl.multiple_of(part * PART, PART), PART)

        @pl.loop(0, nc)
        def _(s):
            slot = srecv.at[s, rows16, :]
            pltpu.make_async_copy(slot, slot, sig_recv.at[part, s]).wait()

        outer_forward(srecv, part)

        @pl.loop(0, blocks * PART // tall)
        def _(i):
            start = pl.multiple_of(i * tall, tall)
            rows = pl.ds(start, tall)
            spec = product(rows, fwd)
            re, im = spec[:, :LANES], spec[:, LANES:]
            fre, fim = fspec[part, rows, left], fspec[part, rows, right]
            put(start, re * fre - im * fim, re * fim + im * fre)
            dspec[rows, :] = product(rows, bwd)

        for q in range(outer):
            y = []
            for r in range(INNER):
                k1 = q + outer * r
                cos, sin = twist[0, pl.ds(k1, 1), :], twist[1, pl.ds(k1, 1), :]
                re, im = dspec[block_of(k1), left], dspec[block_of(k1), right]
                y.append((re * cos + im * sin, im * cos - re * sin))
            for b, z in enumerate(dft(y, 1)):
                re, im = times(z, turn(b * (q + SHIFT) / blocks))
                mid[b, q, 0] = re
                mid[b, q, 1] = im
        for b in range(INNER):
            lane = pl.ds(b % halves * LANES, LANES)
            y = [(mid[b, q, 0], mid[b, q, 1]) for q in range(outer)]
            for a, z in enumerate(dft(y, 1)):
                csend[step_s * a + b // halves, rows16, lane] = real_part_times(
                    z, turn(a * SHIFT / outer)
                ).astype(BF16)

        @pl.loop(0, nc - 1)
        def _(j):
            conv_copy(part, partner(j, me, nc)).start()

        pltpu.make_async_copy(
            csend.at[me, rows16, :],
            crecv.at[pl.ds(pl.multiple_of(me * per + part * PART, PART), PART), :],
            conv_recv.at[part, me],
        ).start()

    for part in range(parts):

        @pl.loop(0, nc)
        def _(s):
            slot = crecv.at[pl.ds(pl.multiple_of(s * per + part * PART, PART), PART), :]
            pltpu.make_async_copy(slot, slot, conv_recv.at[part, s]).wait()

    @pl.loop(0, halves * columns)
    def _(i):
        row, col = place(i)
        lane, rows = pl.ds(col, LANES), pl.ds(row, LANES)
        conv = crecv[lane, rows].astype(F32).T
        gated[rows, lane] = (
            qfeat[rows, lane] * (conv + skip[:, lane] * mixed[rows, lane].astype(F32))
        ).astype(BF16)

    loads[5].wait()

    def rows_of(chunk):
        return pl.ds(chunk * TOKENS_PER_PART, TOKENS_PER_PART)

    def term(chunk, p):
        return jnp.dot(
            gated[rows_of(chunk), :],
            wbuf[:, pl.ds(pl.multiple_of(p * share, LANES), share)],
            preferred_element_type=F32,
        ).astype(BF16)

    def part_copy(chunk, p):
        return remote(
            psend.at[p, rows_of(chunk), :],
            precv.at[mt, rows_of(chunk), :],
            part_send.at[chunk, p],
            part_recv.at[chunk, mt],
            {TEN: p},
        )

    for chunk in range(chunks):

        @pl.loop(0, nt - 1)
        def _(j):
            p = partner(j, mt, nt)
            psend[p, rows_of(chunk), :] = term(chunk, p)
            part_copy(chunk, p).start()

        precv[mt, rows_of(chunk), :] = term(chunk, mt)

    def row_copy(chunk, p):
        return remote(
            ssend.at[chunk], srow.at[chunk, mt], row_send.at[chunk, p], row_recv.at[chunk, mt], {TEN: p}
        )

    for chunk in range(chunks):

        @pl.loop(0, nt - 1)
        def _(j):
            p = partner(j, mt, nt)
            slot = precv.at[p, rows_of(chunk), :]
            pltpu.make_async_copy(slot, slot, part_recv.at[chunk, p]).wait()

        here = rows_of(chunk)
        squares = jnp.zeros((TOKENS_PER_PART, LANES), F32)
        for c in range(share // LANES):
            lane = pl.ds(c * LANES, LANES)
            s = precv[0, here, lane].astype(F32)
            for g in range(1, nt):
                s = s + precv[g, here, lane].astype(F32)
            total[here, lane] = s
            squares = squares + s * s
        sums = jnp.sum(squares, axis=1, keepdims=True)
        ssend[chunk] = jnp.broadcast_to(sums, (TOKENS_PER_PART, LANES)).T[:8]
        srow[chunk, mt] = ssend[chunk]

        @pl.loop(0, nt - 1)
        def _(j):
            row_copy(chunk, partner(j, mt, nt)).start()

    for chunk in range(chunks):

        @pl.loop(0, nt - 1)
        def _(j):
            p = partner(j, mt, nt)
            slot = srow.at[chunk, p]
            pltpu.make_async_copy(slot, slot, row_recv.at[chunk, p]).wait()

        here = rows_of(chunk)
        s = srow[chunk, 0]
        for g in range(1, nt):
            s = s + srow[chunk, g]
        scale = lax.rsqrt(s * (1.0 / (share * nt)) + 1e-06)
        scale = jnp.broadcast_to(scale[:1], (LANES, TOKENS_PER_PART)).T
        for c in range(share // LANES):
            lane = pl.ds(c * LANES, LANES)
            out[here, lane] = (total[here, lane] * scale * gain[:, lane]).astype(BF16)

    @pl.when(me < nc - 1)
    def _():
        for copy in halos:
            copy.wait_send()

    @pl.loop(0, nc - 1)
    def _(j):
        p = partner(j, me, nc)
        filter_copy(p).wait_send()
        for part in range(parts):
            signal_copy(part, p).wait_send()
            conv_copy(part, p).wait_send()

    @pl.loop(0, nt - 1)
    def _(j):
        p = partner(j, mt, nt)
        for chunk in range(chunks):
            part_copy(chunk, p).wait_send()
            row_copy(chunk, p).wait_send()


def per_device(
    query_proj, key_proj, value_proj, short_taps, long_filter, skip_weight, out_weight, norm_gain
):
    nc, nt = lax.axis_size(CTX), lax.axis_size(TEN)
    tokens, width = query_proj.shape
    features = out_weight.shape[1]
    share = features // nt
    per = width // nc
    parts = per // PART
    blocks = nc * (tokens // LANES)
    outer = blocks // INNER
    chunks = tokens // TOKENS_PER_PART
    fwd, bwd, twist = (jnp.asarray(x) for x in tables(blocks))
    anywhere = pl.BlockSpec(memory_space=pl.ANY)
    vmem = pl.BlockSpec(memory_space=pltpu.VMEM)
    dma = pltpu.SemaphoreType.DMA
    return pl.pallas_call(
        functools.partial(kernel, nc, nt),
        out_shape=jax.ShapeDtypeStruct((tokens, share), BF16),
        in_specs=[anywhere] * 7 + [vmem] * 4,
        out_specs=vmem,
        scratch_shapes=[
            pltpu.VMEM((tokens + HALO, width), BF16),
            pltpu.VMEM((tokens + HALO, width), BF16),
            pltpu.VMEM((tokens + HALO, width), BF16),
            pltpu.VMEM((width, features), BF16),
            pltpu.VMEM(fwd.shape, BF16),
            pltpu.VMEM(bwd.shape, BF16),
            pltpu.VMEM((tokens, width), F32),
            pltpu.VMEM((tokens, width), BF16),
            pltpu.VMEM((width, tokens), BF16),
            pltpu.VMEM((nc, per, tokens), BF16),
            pltpu.VMEM((nc, per, tokens), BF16),
            pltpu.VMEM((nc, per, tokens), BF16),
            pltpu.VMEM((width, tokens), BF16),
            pltpu.VMEM((INNER, outer, 2, PART, LANES), F32),
            pltpu.VMEM((blocks * PART, 2 * LANES), BF16),
            pltpu.VMEM((blocks * PART, 2 * LANES), BF16),
            pltpu.VMEM((parts, blocks * PART, 2 * LANES), F32),
            pltpu.VMEM((blocks * PART, 2 * LANES), F32),
            pltpu.VMEM((tokens, width), BF16),
            pltpu.VMEM((nt, tokens, share), BF16),
            pltpu.VMEM((nt, tokens, share), BF16),
            pltpu.VMEM((tokens, share), F32),
            pltpu.VMEM((chunks, 8, TOKENS_PER_PART), F32),
            pltpu.VMEM((chunks, nt, 8, TOKENS_PER_PART), F32),
            dma((6,)),
            dma((3,)),
            dma((3,)),
            dma((nc,)),
            dma((nc,)),
            dma((parts, nc)),
            dma((parts, nc)),
            dma((parts, nc)),
            dma((parts, nc)),
            dma((chunks, nt)),
            dma((chunks, nt)),
            dma((chunks, nt)),
            dma((chunks, nt)),
        ],
        compiler_params=pltpu.CompilerParams(
            collective_id=0, has_side_effects=True, vmem_limit_bytes=56 * 1024 * 1024
        ),
    )(
        query_proj,
        key_proj,
        value_proj,
        long_filter,
        out_weight,
        fwd,
        bwd,
        short_taps,
        skip_weight.reshape(1, width),
        norm_gain.reshape(1, share),
        twist,
    )


def solution(mesh):
    placed = (
        P(CTX, TEN),
        P(CTX, TEN),
        P(CTX, TEN),
        P(None, None, TEN),
        P(TEN, CTX),
        P(TEN),
        P(TEN, None),
        P(TEN),
    )
    return jax.shard_map(
        per_device, mesh=mesh, in_specs=placed, out_specs=P(CTX, TEN), check_vma=False
    )
```

```python
import functools
import math

import jax
import jax.numpy as jnp
import ml_dtypes
import numpy as np
from jax import lax
from jax.experimental import pallas as pl
from jax.experimental.pallas import tpu as pltpu
from jax.sharding import PartitionSpec as P

F32, BF16 = jnp.float32, jnp.bfloat16
CTX, TEN = "context", "tensor"
HALO = 16
LANES = 128
PART = 16
SHIFT = 0.25
INNER = 8
RING = 4
PIECE = 64


def times(z, c):
    re, im = z
    cr, ci = float(c.real), float(c.imag)
    cr = 0.0 if abs(cr) < 1e-12 else cr
    ci = 0.0 if abs(ci) < 1e-12 else ci
    if im is None:
        if ci == 0.0:
            return (re if cr == 1.0 else re * cr, None)
        return (re * cr, re * ci)
    if ci == 0.0:
        return z if cr == 1.0 else (re * cr, im * cr)
    if cr == 0.0:
        return (im * -ci, re * ci)
    if abs(abs(cr) - abs(ci)) < 1e-12:
        plus, minus = re + im, re - im
        if (cr > 0) == (ci > 0):
            return (minus * cr, plus * cr)
        return (plus * cr, minus * ci)
    return (re * cr - im * ci, re * ci + im * cr)


def real_part_times(z, c):
    re, im = z
    cr, ci = float(c.real), float(c.imag)
    if im is None or abs(ci) < 1e-12:
        return re if cr == 1.0 else re * cr
    return re * cr - im * ci


def plus_minus(a, b):
    (ar, ai), (br, bi) = a, b
    if ai is None and bi is None:
        return (ar + br, None), (ar - br, None)
    if ai is None:
        return (ar + br, bi), (ar - br, -bi)
    if bi is None:
        return (ar + br, ai), (ar - br, ai)
    return (ar + br, ai + bi), (ar - br, ai - bi)


def dft(x, sign):
    n = len(x)
    if n == 1:
        return list(x)
    even, odd = dft(x[0::2], sign), dft(x[1::2], sign)
    low, high = [], []
    for k in range(n // 2):
        e, o = even[k], odd[k]
        if 4 * k == n and e[1] is not None and o[1] is not None:
            s = float(sign)
            one = (e[0] - o[1], e[1] + o[0])
            two = (e[0] + o[1], e[1] - o[0])
            a, b = (one, two) if s > 0 else (two, one)
        else:
            a, b = plus_minus(e, times(o, turn(sign * k / n)))
        low.append(a)
        high.append(b)
    return low + high


def turn(x):
    return complex(math.cos(2 * math.pi * x), math.sin(2 * math.pi * x))


def im_of(z):
    return jnp.zeros_like(z[0]) if z[1] is None else z[1]


def split_table(x):
    high = x.astype(ml_dtypes.bfloat16)
    low = (x - high.astype(np.float64)).astype(ml_dtypes.bfloat16)
    return np.stack([high, low])


def tables(blocks):
    length = blocks * LANES
    t = np.arange(LANES)
    phase = np.outer(t, t) % LANES / LANES
    forward = np.exp(-2j * np.pi * phase)
    backward = np.exp(2j * np.pi * phase) / length
    pair = lambda w: np.block([[w.real, w.imag], [-w.imag, w.real]])
    twist = np.exp(-2j * np.pi * np.outer(np.arange(blocks) + SHIFT, t) / length)
    return (
        split_table(pair(forward)),
        split_table(pair(backward)),
        np.stack([twist.real, twist.imag]).astype(np.float32),
    )


def kernel(
    nc,
    nt,
    q_hbm,
    k_hbm,
    v_hbm,
    filt_hbm,
    w_hbm,
    fwd_hbm,
    bwd_hbm,
    taps,
    skip,
    gain,
    twist,
    out,
    qbuf,
    kbuf,
    vbuf,
    wbuf,
    fwd,
    bwd,
    qfeat,
    mixed,
    mixed_t,
    frecv,
    srecv,
    csend,
    crecv,
    mid,
    high,
    low,
    fspec,
    dspec,
    gated,
    far,
    relay,
    to_right,
    to_left,
    from_left,
    from_right,
    own,
    to_pair,
    from_pair,
    mine,
    ssend,
    srow,
    load_sem,
    halo_send,
    halo_recv,
    filt_send,
    filt_recv,
    sig_send,
    sig_recv,
    conv_send,
    conv_recv,
    red_send,
    red_recv,
    row_send,
    row_recv,
):
    me, mt = lax.axis_index(CTX), lax.axis_index(TEN)
    tokens, width = q_hbm.shape
    per = width // nc
    parts = per // PART
    halves = tokens // LANES
    blocks = nc * halves
    outer = blocks // INNER
    step_s = INNER // halves
    share = out.shape[1]

    def partner(j, mine, n):
        step = n // 2 - (j + 1) // 2
        odd = j % 2
        return (mine + step * (1 - odd) + (n - step) * odd) % n

    def remote(src, dst, send, recv, device):
        return pltpu.make_async_remote_copy(
            src_ref=src,
            dst_ref=dst,
            send_sem=send,
            recv_sem=recv,
            device_id=device,
            device_id_type=pl.DeviceIdType.MESH,
        )

    body = pl.ds(HALO, tokens)
    loads = [
        pltpu.make_async_copy(src, dst, load_sem.at[i])
        for i, (src, dst) in enumerate(
            (
                (k_hbm, kbuf.at[body, :]),
                (v_hbm, vbuf.at[body, :]),
                (q_hbm, qbuf.at[body, :]),
                (fwd_hbm, fwd),
                (bwd_hbm, bwd),
                (w_hbm, wbuf),
            )
        )
    ]
    for copy in loads:
        copy.start()

    barrier = pltpu.get_barrier_semaphore()

    @pl.loop(0, nc - 1)
    def _(j):
        pl.semaphore_signal(barrier, inc=1, device_id={CTX: partner(j, me, nc)})

    @pl.loop(0, nt - 1)
    def _(j):
        pl.semaphore_signal(barrier, inc=1, device_id={TEN: partner(j, mt, nt)})

    pl.semaphore_wait(barrier, nc - 1 + nt - 1)

    def settle(stage):
        @pl.when(me < nc - 1)
        def _():
            for copy in halos:
                copy.wait_send()

        @pl.loop(0, nc - 1)
        def _(j):
            p = partner(j, me, nc)
            filter_copy(p).wait_send()
            if stage > 2:
                for part in range(parts):
                    signal_copy(part, p).wait_send()
            if stage > 4:
                for group in range(parts + halves - 1):
                    conv_copy(group, p).wait_send()

        if stage > 6:
            for c in range(halves):
                for u in pieces:
                    for kind in range(7):
                        message(kind, c, u).wait_send()

            @pl.loop(0, nt - 1)
            def _(j):
                for c in range(halves):
                    row_copy(c, partner(j, mt, nt)).wait_send()

    halos = [
        remote(
            src.at[pl.ds(tokens - HALO, HALO), :],
            dst.at[pl.ds(0, HALO), :],
            halo_send.at[i],
            halo_recv.at[i],
            {CTX: (me + 1) % nc},
        )
        for i, (src, dst) in enumerate(((k_hbm, kbuf), (v_hbm, vbuf), (q_hbm, qbuf)))
    ]

    @pl.when(me < nc - 1)
    def _():
        for copy in halos:
            copy.start()

    @pl.when(me == 0)
    def _():
        for buf in (kbuf, vbuf, qbuf):
            buf[pl.ds(0, HALO), :] = jnp.zeros((HALO, width), BF16)

    def filter_copy(p):
        return remote(
            filt_hbm.at[pl.ds(pl.multiple_of(p * per, PART), per), :],
            frecv.at[me],
            filt_send.at[p],
            filt_recv.at[me],
            {CTX: p},
        )

    @pl.loop(0, nc - 1)
    def _(j):
        filter_copy(partner(j, me, nc)).start()

    own_filter = pltpu.make_async_copy(
        filt_hbm.at[pl.ds(pl.multiple_of(me * per, PART), per), :], frecv.at[me], filt_recv.at[me]
    )
    own_filter.start()

    def feature(buf, r, row, lane):
        wide = buf[pl.ds(row, LANES + HALO), lane].astype(F32)[HALO - 8 :]
        one = pltpu.roll(wide, 1, 0)[8:]
        two = pltpu.roll(wide, 2, 0)[8:]
        return (
            taps[r, pl.ds(0, 1), lane] * wide[8:]
            + taps[r, pl.ds(1, 1), lane] * one
            + taps[r, pl.ds(2, 1), lane] * two
        )

    columns = width // LANES

    def place(i):
        row = pl.multiple_of(i // columns * LANES, LANES)
        col = pl.multiple_of(i % columns * LANES, LANES)
        return row, col

    for i in (0, 1):
        loads[i].wait()

    @pl.when(me > 0)
    def _():
        for i in (0, 1):
            halos[i].wait_recv()

    @pl.loop(0, halves * columns)
    def _(i):
        row, col = place(i)
        lane = pl.ds(col, LANES)
        product = feature(kbuf, 1, row, lane) * feature(vbuf, 2, row, lane)
        mixed[pl.ds(row, LANES), lane] = product.astype(BF16)
        mixed_t[pl.ds(col, LANES), pl.ds(row, LANES)] = product.T.astype(BF16)

    def signal_copy(part, p):
        return remote(
            mixed_t.at[pl.ds(pl.multiple_of(p * per + part * PART, PART), PART), :],
            srecv.at[me, pl.ds(part * PART, PART), :],
            sig_send.at[part, p],
            sig_recv.at[part, me],
            {CTX: p},
        )

    for part in range(parts):

        @pl.loop(0, nc - 1)
        def _(j):
            signal_copy(part, partner(j, me, nc)).start()

        pltpu.make_async_copy(
            mixed_t.at[pl.ds(pl.multiple_of(me * per + part * PART, PART), PART), :],
            srecv.at[me, pl.ds(part * PART, PART), :],
            sig_recv.at[part, me],
        ).start()

    loads[2].wait()

    @pl.when(me > 0)
    def _():
        halos[2].wait_recv()

    @pl.loop(0, halves * columns)
    def _(i):
        row, col = place(i)
        lane = pl.ds(col, LANES)
        qfeat[pl.ds(row, LANES), lane] = feature(qbuf, 0, row, lane)

    def block_of(k1):
        return pl.ds(k1 * PART, PART)

    left, right = pl.ds(0, LANES), pl.ds(LANES, LANES)

    def outer_forward(recv, part):
        rows = pl.ds(pl.multiple_of(part * PART, PART), PART)
        for b in range(INNER):
            lane = pl.ds(b % halves * LANES, LANES)
            x = [
                times((recv[step_s * a + b // halves, rows, lane].astype(F32), None), turn(-a * SHIFT / outer))
                for a in range(outer)
            ]
            for q, z in enumerate(dft(x, -1)):
                re, im = times(z, turn(-b * (q + SHIFT) / blocks))
                mid[b, q, 0] = re
                mid[b, q, 1] = jnp.zeros_like(re) if im is None else im
        for q in range(outer):
            y = [(mid[b, q, 0], mid[b, q, 1]) for b in range(INNER)]
            for r, (re, im) in enumerate(dft(y, -1)):
                k1 = q + outer * r
                cos, sin = twist[0, pl.ds(k1, 1), :], twist[1, pl.ds(k1, 1), :]
                put(k1 * PART, re * cos - im * sin, im * cos + re * sin)

    def put(row, re, im):
        rows = pl.ds(row, re.shape[0])
        for lane, x in ((left, re), (right, im)):
            top = x.astype(BF16)
            high[rows, lane] = top
            low[rows, lane] = (x - top.astype(F32)).astype(BF16)

    def product(rows, table):
        a, b = high[rows, :], low[rows, :]
        dot = functools.partial(jnp.dot, preferred_element_type=F32)
        return dot(a, table[0]) + dot(b, table[0]) + dot(a, table[1])

    tall = min(256, blocks * PART)

    @pl.loop(0, nc)
    def _(s):
        pltpu.make_async_copy(frecv.at[s], frecv.at[s], filt_recv.at[s]).wait()

    for i in (3, 4):
        loads[i].wait()

    @pl.loop(0, parts)
    def _(part):
        outer_forward(frecv, part)

        @pl.loop(0, blocks * PART // tall)
        def _(i):
            rows = pl.ds(pl.multiple_of(i * tall, tall), tall)
            fspec[part, rows, :] = product(rows, fwd)

    def conv_slice(group, p):
        if isinstance(group, int) and group >= parts:
            return pl.ds(pl.multiple_of(p * per, PART), per), pl.ds((group - parts + 1) * LANES, LANES)
        return pl.ds(pl.multiple_of(p * per + group * PART, PART), PART), left

    def conv_copy(group, p):
        src = csend.at[p, conv_slice(group, 0)[0], conv_slice(group, 0)[1]]
        return remote(
            src, crecv.at[conv_slice(group, me)], conv_send.at[group, p], conv_recv.at[group, me], {CTX: p}
        )

    def send_conv(group):
        @pl.loop(0, nc - 1)
        def _(j):
            conv_copy(group, partner(j, me, nc)).start()

        pltpu.make_async_copy(
            csend.at[me, conv_slice(group, 0)[0], conv_slice(group, 0)[1]],
            crecv.at[conv_slice(group, me)],
            conv_recv.at[group, me],
        ).start()

    def await_conv(group):
        @pl.loop(0, nc)
        def _(s):
            slot = crecv.at[conv_slice(group, s)]
            pltpu.make_async_copy(slot, slot, conv_recv.at[group, s]).wait()

    @pl.loop(0, parts)
    def _(part):
        rows16 = pl.ds(pl.multiple_of(part * PART, PART), PART)

        @pl.loop(0, nc)
        def _(s):
            slot = srecv.at[s, rows16, :]
            pltpu.make_async_copy(slot, slot, sig_recv.at[part, s]).wait()

        outer_forward(srecv, part)

        @pl.loop(0, blocks * PART // tall)
        def _(i):
            start = pl.multiple_of(i * tall, tall)
            rows = pl.ds(start, tall)
            spec = product(rows, fwd)
            re, im = spec[:, :LANES], spec[:, LANES:]
            fre, fim = fspec[part, rows, left], fspec[part, rows, right]
            put(start, re * fre - im * fim, re * fim + im * fre)
            dspec[rows, :] = product(rows, bwd)

        for q in range(outer):
            y = []
            for r in range(INNER):
                k1 = q + outer * r
                cos, sin = twist[0, pl.ds(k1, 1), :], twist[1, pl.ds(k1, 1), :]
                re, im = dspec[block_of(k1), left], dspec[block_of(k1), right]
                y.append((re * cos + im * sin, im * cos - re * sin))
            for b, z in enumerate(dft(y, 1)):
                re, im = times(z, turn(b * (q + SHIFT) / blocks))
                mid[b, q, 0] = re
                mid[b, q, 1] = im
        for b in range(INNER):
            lane = pl.ds(b % halves * LANES, LANES)
            y = [(mid[b, q, 0], mid[b, q, 1]) for q in range(outer)]
            for a, z in enumerate(dft(y, 1)):
                csend[step_s * a + b // halves, rows16, lane] = real_part_times(
                    z, turn(a * SHIFT / outer)
                ).astype(BF16)

        send_conv(part)

    for half in range(1, halves):
        send_conv(parts + half - 1)

    def gate(chunk):
        for group in range(parts) if chunk == 0 else [parts + chunk - 1]:
            await_conv(group)
        rows = rows_of(chunk)

        @pl.loop(0, columns)
        def _(i):
            lane = pl.ds(pl.multiple_of(i * LANES, LANES), LANES)
            conv = crecv[lane, rows].astype(F32).T
            gated[rows, lane] = (
                qfeat[rows, lane] * (conv + skip[:, lane] * mixed[rows, lane].astype(F32))
            ).astype(BF16)

    def rows_of(chunk):
        return pl.ds(chunk * LANES, LANES)

    ring_at, pair_at = mt % RING, mt // RING
    rightward = {TEN: pair_at * RING + (ring_at + 1) % RING}
    leftward = {TEN: pair_at * RING + (ring_at + RING - 1) % RING}
    across = {TEN: (1 - pair_at) * RING + ring_at}

    def term(chunk, pair, ring):
        column = pl.multiple_of((pair * RING + ring) * share, LANES)
        return jnp.dot(gated[rows_of(chunk), :], wbuf[:, pl.ds(column, share)], preferred_element_type=F32)

    def terms(chunk, ring, into):
        @pl.loop(0, 2)
        def _(pair):
            into[chunk, pair] = term(chunk, pair, ring % RING).astype(into.dtype)

    def piece(u):
        return pl.ds(u * PIECE, PIECE)

    def first(u):
        return pl.ds(u * PIECE, PIECE // 2)

    def second(u):
        return pl.ds(u * PIECE + PIECE // 2, PIECE // 2)

    def message(kind, c, u):
        src, dst, device = (
            lambda: (far.at[c, :, first(u)], relay.at[c, :, first(u)], rightward),
            lambda: (far.at[c, :, second(u)], relay.at[c, :, second(u)], leftward),
            lambda: (to_right.at[c, :, second(u)], from_left.at[c, :, second(u)], rightward),
            lambda: (to_left.at[c, :, first(u)], from_right.at[c, :, first(u)], leftward),
            lambda: (to_right.at[c, :, first(u)], from_left.at[c, :, first(u)], rightward),
            lambda: (to_left.at[c, :, second(u)], from_right.at[c, :, second(u)], leftward),
            lambda: (to_pair.at[c, piece(u)], from_pair.at[c, piece(u)], across),
        )[kind]()
        return remote(src, dst, red_send.at[kind, c, u], red_recv.at[kind, c, u], device)

    pieces = range(LANES // PIECE)

    def start_ring(c):
        terms(c, ring_at + 2, far)
        for u in pieces:
            message(0, c, u).start()
            message(1, c, u).start()
        terms(c, ring_at + 1, to_right)
        for u in pieces:
            message(2, c, u).start()
        terms(c, ring_at + RING - 1, to_left)
        for u in pieces:
            message(3, c, u).start()
        terms(c, ring_at, own)

    def pass_on(c):
        for u in pieces:
            for kind, rows, buf in ((0, first(u), to_right), (1, second(u), to_left)):
                message(kind, c, u).wait_recv()
                for pair in range(2):
                    buf[c, pair, rows] = (
                        buf[c, pair, rows].astype(F32) + relay[c, pair, rows].astype(F32)
                    ).astype(BF16)
                message(kind + 4, c, u).start()

    def end_ring(c):
        for u in pieces:
            for kind in (2, 3, 4, 5):
                message(kind, c, u).wait_recv()
            rows = piece(u)

            def ring_sum(pair):
                return (
                    own[c, pair, rows]
                    + from_left[c, pair, rows].astype(F32)
                    + from_right[c, pair, rows].astype(F32)
                )

            to_pair[c, rows] = ring_sum(1 - pair_at).astype(BF16)
            message(6, c, u).start()
            mine[c, rows] = ring_sum(pair_at)

    def row_copy(chunk, p):
        return remote(
            ssend.at[chunk], srow.at[chunk, mt], row_send.at[chunk, p], row_recv.at[chunk, mt], {TEN: p}
        )

    def end_pair(c):
        squares = []
        for u in pieces:
            message(6, c, u).wait_recv()
            rows = piece(u)
            square = jnp.zeros((PIECE, LANES), F32)
            for i in range(share // LANES):
                lane = pl.ds(i * LANES, LANES)
                s = mine[c, rows, lane] + from_pair[c, rows, lane].astype(F32)
                mine[c, rows, lane] = s
                square = square + s * s
            squares.append(jnp.sum(square, axis=1, keepdims=True))
        sums = jnp.concatenate(squares, axis=0)
        ssend[c] = jnp.broadcast_to(sums, (LANES, LANES)).T[:8]
        srow[c, mt] = ssend[c]

        @pl.loop(0, nt - 1)
        def _(j):
            row_copy(c, partner(j, mt, nt)).start()

    def normalize(c):
        @pl.loop(0, nt - 1)
        def _(j):
            p = partner(j, mt, nt)
            slot = srow.at[c, p]
            pltpu.make_async_copy(slot, slot, row_recv.at[c, p]).wait()

        s = srow[c, 0]
        for g in range(1, nt):
            s = s + srow[c, g]
        scale = lax.rsqrt(s * (1.0 / (share * nt)) + 1e-06)
        scale = jnp.broadcast_to(scale[:1], (LANES, LANES)).T
        for i in range(share // LANES):
            lane = pl.ds(i * LANES, LANES)
            out[rows_of(c), lane] = (mine[c, :, lane] * scale * gain[:, lane]).astype(BF16)

    gate(0)
    loads[5].wait()
    start_ring(0)
    pass_on(0)
    gate(1)
    start_ring(1)
    end_ring(0)
    pass_on(1)
    end_pair(0)
    end_ring(1)
    normalize(0)
    end_pair(1)
    normalize(1)

    settle(9)


def per_device(
    query_proj, key_proj, value_proj, short_taps, long_filter, skip_weight, out_weight, norm_gain
):
    nc, nt = lax.axis_size(CTX), lax.axis_size(TEN)
    tokens, width = query_proj.shape
    features = out_weight.shape[1]
    share = features // nt
    per = width // nc
    parts = per // PART
    blocks = nc * (tokens // LANES)
    outer = blocks // INNER
    halves = tokens // LANES
    fwd, bwd, twist = (jnp.asarray(x) for x in tables(blocks))
    anywhere = pl.BlockSpec(memory_space=pl.ANY)
    vmem = pl.BlockSpec(memory_space=pltpu.VMEM)
    dma = pltpu.SemaphoreType.DMA
    return pl.pallas_call(
        functools.partial(kernel, nc, nt),
        out_shape=jax.ShapeDtypeStruct((tokens, share), BF16),
        in_specs=[anywhere] * 7 + [vmem] * 4,
        out_specs=vmem,
        scratch_shapes=[
            pltpu.VMEM((tokens + HALO, width), BF16),
            pltpu.VMEM((tokens + HALO, width), BF16),
            pltpu.VMEM((tokens + HALO, width), BF16),
            pltpu.VMEM((width, features), BF16),
            pltpu.VMEM(fwd.shape, BF16),
            pltpu.VMEM(bwd.shape, BF16),
            pltpu.VMEM((tokens, width), F32),
            pltpu.VMEM((tokens, width), BF16),
            pltpu.VMEM((width, tokens), BF16),
            pltpu.VMEM((nc, per, tokens), BF16),
            pltpu.VMEM((nc, per, tokens), BF16),
            pltpu.VMEM((nc, per, tokens), BF16),
            pltpu.VMEM((width, tokens), BF16),
            pltpu.VMEM((INNER, outer, 2, PART, LANES), F32),
            pltpu.VMEM((blocks * PART, 2 * LANES), BF16),
            pltpu.VMEM((blocks * PART, 2 * LANES), BF16),
            pltpu.VMEM((parts, blocks * PART, 2 * LANES), F32),
            pltpu.VMEM((blocks * PART, 2 * LANES), F32),
            pltpu.VMEM((tokens, width), BF16),
            *[pltpu.VMEM((halves, 2, LANES, share), BF16)] * 6,
            pltpu.VMEM((halves, 2, LANES, share), F32),
            pltpu.VMEM((halves, LANES, share), BF16),
            pltpu.VMEM((halves, LANES, share), BF16),
            pltpu.VMEM((halves, LANES, share), F32),
            pltpu.VMEM((halves, 8, LANES), F32),
            pltpu.VMEM((halves, nt, 8, LANES), F32),
            dma((6,)),
            dma((3,)),
            dma((3,)),
            dma((nc,)),
            dma((nc,)),
            dma((parts, nc)),
            dma((parts, nc)),
            dma((parts + halves - 1, nc)),
            dma((parts + halves - 1, nc)),
            dma((7, halves, LANES // PIECE)),
            dma((7, halves, LANES // PIECE)),
            dma((halves, nt)),
            dma((halves, nt)),
        ],
        compiler_params=pltpu.CompilerParams(
            collective_id=0, has_side_effects=True, vmem_limit_bytes=56 * 1024 * 1024
        ),
    )(
        query_proj,
        key_proj,
        value_proj,
        long_filter,
        out_weight,
        fwd,
        bwd,
        short_taps,
        skip_weight.reshape(1, width),
        norm_gain.reshape(1, share),
        twist,
    )


def solution(mesh):
    placed = (
        P(CTX, TEN),
        P(CTX, TEN),
        P(CTX, TEN),
        P(None, None, TEN),
        P(TEN, CTX),
        P(TEN),
        P(TEN, None),
        P(TEN),
    )
    return jax.shard_map(
        per_device, mesh=mesh, in_specs=placed, out_specs=P(CTX, TEN), check_vma=False
    )
```

```python
import functools
import math

import jax
import jax.numpy as jnp
import ml_dtypes
import numpy as np
from jax import lax
from jax.experimental import pallas as pl
from jax.experimental.pallas import tpu as pltpu
from jax.sharding import PartitionSpec as P

F32, BF16 = jnp.float32, jnp.bfloat16
CTX, TEN = "context", "tensor"
HALO = 16
LANES = 128
PART = 16
SHIFT = 0.25
INNER = 8
RING = 4
PIECE = 64


def times(z, c):
    re, im = z
    cr, ci = float(c.real), float(c.imag)
    cr = 0.0 if abs(cr) < 1e-12 else cr
    ci = 0.0 if abs(ci) < 1e-12 else ci
    if im is None:
        if ci == 0.0:
            return (re if cr == 1.0 else re * cr, None)
        return (re * cr, re * ci)
    if ci == 0.0:
        return z if cr == 1.0 else (re * cr, im * cr)
    if cr == 0.0:
        return (im * -ci, re * ci)
    if abs(abs(cr) - abs(ci)) < 1e-12:
        plus, minus = re + im, re - im
        if (cr > 0) == (ci > 0):
            return (minus * cr, plus * cr)
        return (plus * cr, minus * ci)
    return (re * cr - im * ci, re * ci + im * cr)


def real_part_times(z, c):
    re, im = z
    cr, ci = float(c.real), float(c.imag)
    if im is None or abs(ci) < 1e-12:
        return re if cr == 1.0 else re * cr
    return re * cr - im * ci


def plus_minus(a, b):
    (ar, ai), (br, bi) = a, b
    if ai is None and bi is None:
        return (ar + br, None), (ar - br, None)
    if ai is None:
        return (ar + br, bi), (ar - br, -bi)
    if bi is None:
        return (ar + br, ai), (ar - br, ai)
    return (ar + br, ai + bi), (ar - br, ai - bi)


def dft(x, sign):
    n = len(x)
    if n == 1:
        return list(x)
    even, odd = dft(x[0::2], sign), dft(x[1::2], sign)
    low, high = [], []
    for k in range(n // 2):
        e, o = even[k], odd[k]
        if 4 * k == n and e[1] is not None and o[1] is not None:
            s = float(sign)
            one = (e[0] - o[1], e[1] + o[0])
            two = (e[0] + o[1], e[1] - o[0])
            a, b = (one, two) if s > 0 else (two, one)
        else:
            a, b = plus_minus(e, times(o, turn(sign * k / n)))
        low.append(a)
        high.append(b)
    return low + high


def turn(x):
    return complex(math.cos(2 * math.pi * x), math.sin(2 * math.pi * x))


def im_of(z):
    return jnp.zeros_like(z[0]) if z[1] is None else z[1]


def split_table(x):
    high = x.astype(ml_dtypes.bfloat16)
    low = (x - high.astype(np.float64)).astype(ml_dtypes.bfloat16)
    return np.stack([high, low])


def tables(blocks):
    length = blocks * LANES
    t = np.arange(LANES)
    phase = np.outer(t, t) % LANES / LANES
    forward = np.exp(-2j * np.pi * phase)
    backward = np.exp(2j * np.pi * phase) / length
    pair = lambda w: np.block([[w.real, w.imag], [-w.imag, w.real]])
    twist = np.exp(-2j * np.pi * np.outer(np.arange(blocks) + SHIFT, t) / length)
    return (
        split_table(pair(forward)),
        split_table(pair(backward)),
        np.stack([twist.real, twist.imag]).astype(np.float32),
    )


def kernel(
    nc,
    nt,
    q_hbm,
    k_hbm,
    v_hbm,
    filt_hbm,
    w_hbm,
    fwd_hbm,
    bwd_hbm,
    taps_hbm,
    skip_hbm,
    gain_hbm,
    twist_hbm,
    out,
    taps,
    skip,
    gain,
    twist,
    qbuf,
    kbuf,
    vbuf,
    wbuf,
    fwd,
    bwd,
    qfeat,
    mixed,
    mixed_t,
    frecv,
    srecv,
    csend,
    crecv,
    mid,
    high,
    low,
    fspec,
    dspec,
    gated,
    far,
    relay,
    to_right,
    to_left,
    from_left,
    from_right,
    own,
    to_pair,
    from_pair,
    mine,
    ssend,
    srow,
    load_sem,
    halo_send,
    halo_recv,
    filt_send,
    filt_recv,
    sig_send,
    sig_recv,
    conv_send,
    conv_recv,
    red_send,
    red_recv,
    row_send,
    row_recv,
):
    me, mt = lax.axis_index(CTX), lax.axis_index(TEN)
    tokens, width = q_hbm.shape
    per = width // nc
    parts = per // PART
    halves = tokens // LANES
    blocks = nc * halves
    outer = blocks // INNER
    step_s = INNER // halves
    share = out.shape[1]

    def partner(j, mine, n):
        step = n // 2 - (j + 1) // 2
        odd = j % 2
        return (mine + step * (1 - odd) + (n - step) * odd) % n

    def remote(src, dst, send, recv, device):
        return pltpu.make_async_remote_copy(
            src_ref=src,
            dst_ref=dst,
            send_sem=send,
            recv_sem=recv,
            device_id=device,
            device_id_type=pl.DeviceIdType.MESH,
        )

    barrier = pltpu.get_barrier_semaphore()

    @pl.loop(0, nc - 1)
    def _(j):
        pl.semaphore_signal(barrier, inc=1, device_id={CTX: partner(j, me, nc)})

    @pl.loop(0, nt - 1)
    def _(j):
        pl.semaphore_signal(barrier, inc=1, device_id={TEN: partner(j, mt, nt)})

    body = pl.ds(HALO, tokens)
    loads = [
        pltpu.make_async_copy(src, dst, load_sem.at[i])
        for i, (src, dst) in enumerate(
            (
                (k_hbm, kbuf.at[body, :]),
                (v_hbm, vbuf.at[body, :]),
                (q_hbm, qbuf.at[body, :]),
                (fwd_hbm, fwd),
                (bwd_hbm, bwd),
                (w_hbm, wbuf),
                (taps_hbm, taps),
                (twist_hbm, twist),
                (skip_hbm, skip),
                (gain_hbm, gain),
            )
        )
    ]
    for i in (6, 0, 1, 2, 7, 3, 4, 8, 9, 5):
        loads[i].start()

    pl.semaphore_wait(barrier, nc - 1 + nt - 1)

    def settle(stage):
        @pl.when(me < nc - 1)
        def _():
            for copy in halos:
                copy.wait_send()

        @pl.loop(0, nc - 1)
        def _(j):
            p = partner(j, me, nc)
            filter_copy(p).wait_send()
            if stage > 2:
                for part in range(parts):
                    signal_copy(part, p).wait_send()
            if stage > 4:
                for group in range(parts + halves - 1):
                    conv_copy(group, p).wait_send()

        if stage > 6:
            for c in range(halves):
                for u in pieces:
                    for kind in range(7):
                        message(kind, c, u).wait_send()

            @pl.loop(0, nt - 1)
            def _(j):
                for c in range(halves):
                    row_copy(c, partner(j, mt, nt)).wait_send()

    halos = [
        remote(
            src.at[pl.ds(tokens - HALO, HALO), :],
            dst.at[pl.ds(0, HALO), :],
            halo_send.at[i],
            halo_recv.at[i],
            {CTX: (me + 1) % nc},
        )
        for i, (src, dst) in enumerate(((k_hbm, kbuf), (v_hbm, vbuf), (q_hbm, qbuf)))
    ]

    @pl.when(me < nc - 1)
    def _():
        for copy in halos:
            copy.start()

    @pl.when(me == 0)
    def _():
        for buf in (kbuf, vbuf, qbuf):
            buf[pl.ds(0, HALO), :] = jnp.zeros((HALO, width), BF16)

    def filter_copy(p):
        return remote(
            filt_hbm.at[pl.ds(pl.multiple_of(p * per, PART), per), :],
            frecv.at[me],
            filt_send.at[p],
            filt_recv.at[me],
            {CTX: p},
        )

    @pl.loop(0, nc - 1)
    def _(j):
        filter_copy(partner(j, me, nc)).start()

    own_filter = pltpu.make_async_copy(
        filt_hbm.at[pl.ds(pl.multiple_of(me * per, PART), per), :], frecv.at[me], filt_recv.at[me]
    )
    own_filter.start()

    def feature(buf, r, row, lane):
        wide = buf[pl.ds(row, LANES + HALO), lane].astype(F32)[HALO - 8 :]
        one = pltpu.roll(wide, 1, 0)[8:]
        two = pltpu.roll(wide, 2, 0)[8:]
        return (
            taps[r, pl.ds(0, 1), lane] * wide[8:]
            + taps[r, pl.ds(1, 1), lane] * one
            + taps[r, pl.ds(2, 1), lane] * two
        )

    columns = width // LANES

    def place(i):
        row = pl.multiple_of(i // columns * LANES, LANES)
        col = pl.multiple_of(i % columns * LANES, LANES)
        return row, col

    for i in (6, 0, 1):
        loads[i].wait()

    @pl.when(me > 0)
    def _():
        for i in (0, 1):
            halos[i].wait_recv()

    @pl.loop(0, halves * columns)
    def _(i):
        row, col = place(i)
        lane = pl.ds(col, LANES)
        product = feature(kbuf, 1, row, lane) * feature(vbuf, 2, row, lane)
        mixed[pl.ds(row, LANES), lane] = product.astype(BF16)
        mixed_t[pl.ds(col, LANES), pl.ds(row, LANES)] = product.T.astype(BF16)

    def signal_copy(part, p):
        return remote(
            mixed_t.at[pl.ds(pl.multiple_of(p * per + part * PART, PART), PART), :],
            srecv.at[me, pl.ds(part * PART, PART), :],
            sig_send.at[part, p],
            sig_recv.at[part, me],
            {CTX: p},
        )

    for part in range(parts):

        @pl.loop(0, nc - 1)
        def _(j):
            signal_copy(part, partner(j, me, nc)).start()

        pltpu.make_async_copy(
            mixed_t.at[pl.ds(pl.multiple_of(me * per + part * PART, PART), PART), :],
            srecv.at[me, pl.ds(part * PART, PART), :],
            sig_recv.at[part, me],
        ).start()

    loads[2].wait()

    @pl.when(me > 0)
    def _():
        halos[2].wait_recv()

    @pl.loop(0, halves * columns)
    def _(i):
        row, col = place(i)
        lane = pl.ds(col, LANES)
        qfeat[pl.ds(row, LANES), lane] = feature(qbuf, 0, row, lane)

    def block_of(k1):
        return pl.ds(k1 * PART, PART)

    left, right = pl.ds(0, LANES), pl.ds(LANES, LANES)

    def outer_forward(recv, part):
        rows = pl.ds(pl.multiple_of(part * PART, PART), PART)
        for b in range(INNER):
            lane = pl.ds(b % halves * LANES, LANES)
            x = [
                times((recv[step_s * a + b // halves, rows, lane].astype(F32), None), turn(-a * SHIFT / outer))
                for a in range(outer)
            ]
            for q, z in enumerate(dft(x, -1)):
                re, im = times(z, turn(-b * (q + SHIFT) / blocks))
                mid[b, q, 0] = re
                mid[b, q, 1] = jnp.zeros_like(re) if im is None else im
        for q in range(outer):
            y = [(mid[b, q, 0], mid[b, q, 1]) for b in range(INNER)]
            for r, (re, im) in enumerate(dft(y, -1)):
                k1 = q + outer * r
                cos, sin = twist[0, pl.ds(k1, 1), :], twist[1, pl.ds(k1, 1), :]
                put(k1 * PART, re * cos - im * sin, im * cos + re * sin)

    def put(row, re, im):
        rows = pl.ds(row, re.shape[0])
        for lane, x in ((left, re), (right, im)):
            top = x.astype(BF16)
            high[rows, lane] = top
            low[rows, lane] = (x - top.astype(F32)).astype(BF16)

    def product(rows, table):
        a, b = high[rows, :], low[rows, :]
        dot = functools.partial(jnp.dot, preferred_element_type=F32)
        return dot(a, table[0]) + dot(b, table[0]) + dot(a, table[1])

    tall = min(256, blocks * PART)

    @pl.loop(0, nc)
    def _(s):
        pltpu.make_async_copy(frecv.at[s], frecv.at[s], filt_recv.at[s]).wait()

    for i in (3, 4, 7):
        loads[i].wait()

    @pl.loop(0, parts)
    def _(part):
        outer_forward(frecv, part)

        @pl.loop(0, blocks * PART // tall)
        def _(i):
            rows = pl.ds(pl.multiple_of(i * tall, tall), tall)
            fspec[part, rows, :] = product(rows, fwd)

    def conv_slice(group, p):
        if isinstance(group, int) and group >= parts:
            return pl.ds(pl.multiple_of(p * per, PART), per), pl.ds((group - parts + 1) * LANES, LANES)
        return pl.ds(pl.multiple_of(p * per + group * PART, PART), PART), left

    def conv_copy(group, p):
        src = csend.at[p, conv_slice(group, 0)[0], conv_slice(group, 0)[1]]
        return remote(
            src, crecv.at[conv_slice(group, me)], conv_send.at[group, p], conv_recv.at[group, me], {CTX: p}
        )

    def send_conv(group):
        @pl.loop(0, nc - 1)
        def _(j):
            conv_copy(group, partner(j, me, nc)).start()

        pltpu.make_async_copy(
            csend.at[me, conv_slice(group, 0)[0], conv_slice(group, 0)[1]],
            crecv.at[conv_slice(group, me)],
            conv_recv.at[group, me],
        ).start()

    def await_conv(group):
        @pl.loop(0, nc)
        def _(s):
            slot = crecv.at[conv_slice(group, s)]
            pltpu.make_async_copy(slot, slot, conv_recv.at[group, s]).wait()

    @pl.loop(0, parts)
    def _(part):
        rows16 = pl.ds(pl.multiple_of(part * PART, PART), PART)

        @pl.loop(0, nc)
        def _(s):
            slot = srecv.at[s, rows16, :]
            pltpu.make_async_copy(slot, slot, sig_recv.at[part, s]).wait()

        outer_forward(srecv, part)

        @pl.loop(0, blocks * PART // tall)
        def _(i):
            start = pl.multiple_of(i * tall, tall)
            rows = pl.ds(start, tall)
            spec = product(rows, fwd)
            re, im = spec[:, :LANES], spec[:, LANES:]
            fre, fim = fspec[part, rows, left], fspec[part, rows, right]
            put(start, re * fre - im * fim, re * fim + im * fre)
            dspec[rows, :] = product(rows, bwd)

        for q in range(outer):
            y = []
            for r in range(INNER):
                k1 = q + outer * r
                cos, sin = twist[0, pl.ds(k1, 1), :], twist[1, pl.ds(k1, 1), :]
                re, im = dspec[block_of(k1), left], dspec[block_of(k1), right]
                y.append((re * cos + im * sin, im * cos - re * sin))
            for b, z in enumerate(dft(y, 1)):
                re, im = times(z, turn(b * (q + SHIFT) / blocks))
                mid[b, q, 0] = re
                mid[b, q, 1] = im
        for b in range(INNER):
            lane = pl.ds(b % halves * LANES, LANES)
            y = [(mid[b, q, 0], mid[b, q, 1]) for q in range(outer)]
            for a, z in enumerate(dft(y, 1)):
                csend[step_s * a + b // halves, rows16, lane] = real_part_times(
                    z, turn(a * SHIFT / outer)
                ).astype(BF16)

        send_conv(part)

    for half in range(1, halves):
        send_conv(parts + half - 1)

    def gate(chunk):
        for group in range(parts) if chunk == 0 else [parts + chunk - 1]:
            await_conv(group)
        rows = rows_of(chunk)

        @pl.loop(0, columns)
        def _(i):
            lane = pl.ds(pl.multiple_of(i * LANES, LANES), LANES)
            conv = crecv[lane, rows].astype(F32).T
            gated[rows, lane] = (
                qfeat[rows, lane] * (conv + skip[:, lane] * mixed[rows, lane].astype(F32))
            ).astype(BF16)

    def rows_of(chunk):
        return pl.ds(chunk * LANES, LANES)

    ring_at, pair_at = mt % RING, mt // RING
    rightward = {TEN: pair_at * RING + (ring_at + 1) % RING}
    leftward = {TEN: pair_at * RING + (ring_at + RING - 1) % RING}
    across = {TEN: (1 - pair_at) * RING + ring_at}

    def term(chunk, pair, ring):
        column = pl.multiple_of((pair * RING + ring) * share, LANES)
        return jnp.dot(gated[rows_of(chunk), :], wbuf[:, pl.ds(column, share)], preferred_element_type=F32)

    def terms(chunk, ring, into):
        @pl.loop(0, 2)
        def _(pair):
            into[chunk, pair] = term(chunk, pair, ring % RING).astype(into.dtype)

    def piece(u):
        return pl.ds(u * PIECE, PIECE)

    def first(u):
        return pl.ds(u * PIECE, PIECE // 2)

    def second(u):
        return pl.ds(u * PIECE + PIECE // 2, PIECE // 2)

    def message(kind, c, u):
        src, dst, device = (
            lambda: (far.at[c, :, first(u)], relay.at[c, :, first(u)], rightward),
            lambda: (far.at[c, :, second(u)], relay.at[c, :, second(u)], leftward),
            lambda: (to_right.at[c, :, second(u)], from_left.at[c, :, second(u)], rightward),
            lambda: (to_left.at[c, :, first(u)], from_right.at[c, :, first(u)], leftward),
            lambda: (to_right.at[c, :, first(u)], from_left.at[c, :, first(u)], rightward),
            lambda: (to_left.at[c, :, second(u)], from_right.at[c, :, second(u)], leftward),
            lambda: (to_pair.at[c, piece(u)], from_pair.at[c, piece(u)], across),
        )[kind]()
        return remote(src, dst, red_send.at[kind, c, u], red_recv.at[kind, c, u], device)

    pieces = range(LANES // PIECE)

    def start_ring(c):
        terms(c, ring_at + 2, far)
        for u in pieces:
            message(0, c, u).start()
            message(1, c, u).start()
        terms(c, ring_at + 1, to_right)
        message(2, c, 0).start()
        terms(c, ring_at + RING - 1, to_left)
        message(3, c, 0).start()
        terms(c, ring_at, own)

    def pass_on(c):
        for u in pieces:
            for kind, rows, buf in ((0, first(u), to_right), (1, second(u), to_left)):
                message(kind, c, u).wait_recv()
                for pair in range(2):
                    buf[c, pair, rows] = (
                        buf[c, pair, rows].astype(F32) + relay[c, pair, rows].astype(F32)
                    ).astype(BF16)
                message(kind + 4, c, u).start()
            if u + 1 < len(pieces):
                message(2, c, u + 1).start()
                message(3, c, u + 1).start()

    def end_ring(c):
        for u in pieces:
            for kind in (2, 3, 4, 5):
                message(kind, c, u).wait_recv()
            rows = piece(u)

            def ring_sum(pair):
                return (
                    own[c, pair, rows]
                    + from_left[c, pair, rows].astype(F32)
                    + from_right[c, pair, rows].astype(F32)
                )

            to_pair[c, rows] = ring_sum(1 - pair_at).astype(BF16)
            message(6, c, u).start()
            mine[c, rows] = ring_sum(pair_at)

    def row_copy(chunk, p):
        return remote(
            ssend.at[chunk], srow.at[chunk, mt], row_send.at[chunk, p], row_recv.at[chunk, mt], {TEN: p}
        )

    def end_pair(c):
        squares = []
        for u in pieces:
            message(6, c, u).wait_recv()
            rows = piece(u)
            square = jnp.zeros((PIECE, LANES), F32)
            for i in range(share // LANES):
                lane = pl.ds(i * LANES, LANES)
                s = mine[c, rows, lane] + from_pair[c, rows, lane].astype(F32)
                mine[c, rows, lane] = s
                square = square + s * s
            squares.append(jnp.sum(square, axis=1, keepdims=True))
        sums = jnp.concatenate(squares, axis=0)
        ssend[c] = jnp.broadcast_to(sums, (LANES, LANES)).T[:8]
        srow[c, mt] = ssend[c]

        @pl.loop(0, nt - 1)
        def _(j):
            row_copy(c, partner(j, mt, nt)).start()

    def normalize(c):
        @pl.loop(0, nt - 1)
        def _(j):
            p = partner(j, mt, nt)
            slot = srow.at[c, p]
            pltpu.make_async_copy(slot, slot, row_recv.at[c, p]).wait()

        s = srow[c, 0]
        for g in range(1, nt):
            s = s + srow[c, g]
        scale = lax.rsqrt(s * (1.0 / (share * nt)) + 1e-06)
        scale = jnp.broadcast_to(scale[:1], (LANES, LANES)).T
        for i in range(share // LANES):
            lane = pl.ds(i * LANES, LANES)
            out[rows_of(c), lane] = (mine[c, :, lane] * scale * gain[:, lane]).astype(BF16)

    loads[8].wait()
    gate(0)
    loads[5].wait()
    start_ring(0)
    pass_on(0)
    gate(1)
    start_ring(1)
    end_ring(0)
    pass_on(1)
    end_pair(0)
    end_ring(1)
    loads[9].wait()
    normalize(0)
    end_pair(1)
    normalize(1)

    settle(9)


def per_device(
    query_proj, key_proj, value_proj, short_taps, long_filter, skip_weight, out_weight, norm_gain
):
    nc, nt = lax.axis_size(CTX), lax.axis_size(TEN)
    tokens, width = query_proj.shape
    features = out_weight.shape[1]
    share = features // nt
    per = width // nc
    parts = per // PART
    blocks = nc * (tokens // LANES)
    outer = blocks // INNER
    halves = tokens // LANES
    fwd, bwd, twist = (jnp.asarray(x) for x in tables(blocks))
    anywhere = pl.BlockSpec(memory_space=pl.ANY)
    vmem = pl.BlockSpec(memory_space=pltpu.VMEM)
    dma = pltpu.SemaphoreType.DMA
    return pl.pallas_call(
        functools.partial(kernel, nc, nt),
        out_shape=pltpu.VMEM((tokens, share), BF16),
        in_specs=[anywhere] * 11,
        out_specs=vmem,
        scratch_shapes=[
            pltpu.VMEM(short_taps.shape, F32),
            pltpu.VMEM((1, width), F32),
            pltpu.VMEM((1, share), F32),
            pltpu.VMEM(twist.shape, F32),
            pltpu.VMEM((tokens + HALO, width), BF16),
            pltpu.VMEM((tokens + HALO, width), BF16),
            pltpu.VMEM((tokens + HALO, width), BF16),
            pltpu.VMEM((width, features), BF16),
            pltpu.VMEM(fwd.shape, BF16),
            pltpu.VMEM(bwd.shape, BF16),
            pltpu.VMEM((tokens, width), F32),
            pltpu.VMEM((tokens, width), BF16),
            pltpu.VMEM((width, tokens), BF16),
            pltpu.VMEM((nc, per, tokens), BF16),
            pltpu.VMEM((nc, per, tokens), BF16),
            pltpu.VMEM((nc, per, tokens), BF16),
            pltpu.VMEM((width, tokens), BF16),
            pltpu.VMEM((INNER, outer, 2, PART, LANES), F32),
            pltpu.VMEM((blocks * PART, 2 * LANES), BF16),
            pltpu.VMEM((blocks * PART, 2 * LANES), BF16),
            pltpu.VMEM((parts, blocks * PART, 2 * LANES), F32),
            pltpu.VMEM((blocks * PART, 2 * LANES), F32),
            pltpu.VMEM((tokens, width), BF16),
            *[pltpu.VMEM((halves, 2, LANES, share), BF16)] * 6,
            pltpu.VMEM((halves, 2, LANES, share), F32),
            pltpu.VMEM((halves, LANES, share), BF16),
            pltpu.VMEM((halves, LANES, share), BF16),
            pltpu.VMEM((halves, LANES, share), F32),
            pltpu.VMEM((halves, 8, LANES), F32),
            pltpu.VMEM((halves, nt, 8, LANES), F32),
            dma((10,)),
            dma((3,)),
            dma((3,)),
            dma((nc,)),
            dma((nc,)),
            dma((parts, nc)),
            dma((parts, nc)),
            dma((parts + halves - 1, nc)),
            dma((parts + halves - 1, nc)),
            dma((7, halves, LANES // PIECE)),
            dma((7, halves, LANES // PIECE)),
            dma((halves, nt)),
            dma((halves, nt)),
        ],
        compiler_params=pltpu.CompilerParams(
            collective_id=0, has_side_effects=True, vmem_limit_bytes=56 * 1024 * 1024
        ),
    )(
        query_proj,
        key_proj,
        value_proj,
        long_filter,
        out_weight,
        fwd,
        bwd,
        short_taps,
        skip_weight.reshape(1, width),
        norm_gain.reshape(1, share),
        twist,
    )


def solution(mesh):
    placed = (
        P(CTX, TEN),
        P(CTX, TEN),
        P(CTX, TEN),
        P(None, None, TEN),
        P(TEN, CTX),
        P(TEN),
        P(TEN, None),
        P(TEN),
    )
    return jax.shard_map(
        per_device, mesh=mesh, in_specs=placed, out_specs=P(CTX, TEN), check_vma=False
    )
```

```python
import functools
import math

import jax
import jax.numpy as jnp
import ml_dtypes
import numpy as np
from jax import lax
from jax.experimental import pallas as pl
from jax.experimental.pallas import tpu as pltpu
from jax.sharding import PartitionSpec as P

F32, BF16 = jnp.float32, jnp.bfloat16
CTX, TEN = "context", "tensor"
HALO = 16
LANES = 128
PART = 16
SHIFT = 0.25
INNER = 8
RING = 4
PIECE = LANES // 2


def times(z, c):
    re, im = z
    cr, ci = float(c.real), float(c.imag)
    cr = 0.0 if abs(cr) < 1e-12 else cr
    ci = 0.0 if abs(ci) < 1e-12 else ci
    if im is None:
        if ci == 0.0:
            return (re if cr == 1.0 else re * cr, None)
        return (re * cr, re * ci)
    if ci == 0.0:
        return z if cr == 1.0 else (re * cr, im * cr)
    if cr == 0.0:
        return (im * -ci, re * ci)
    if abs(abs(cr) - abs(ci)) < 1e-12:
        plus, minus = re + im, re - im
        if (cr > 0) == (ci > 0):
            return (minus * cr, plus * cr)
        return (plus * cr, minus * ci)
    return (re * cr - im * ci, re * ci + im * cr)


def real_part_times(z, c):
    re, im = z
    cr, ci = float(c.real), float(c.imag)
    if im is None or abs(ci) < 1e-12:
        return re if cr == 1.0 else re * cr
    return re * cr - im * ci


def plus_minus(a, b):
    (ar, ai), (br, bi) = a, b
    if ai is None and bi is None:
        return (ar + br, None), (ar - br, None)
    if ai is None:
        return (ar + br, bi), (ar - br, -bi)
    if bi is None:
        return (ar + br, ai), (ar - br, ai)
    return (ar + br, ai + bi), (ar - br, ai - bi)


def dft(x, sign):
    n = len(x)
    if n == 1:
        return list(x)
    even, odd = dft(x[0::2], sign), dft(x[1::2], sign)
    low, high = [], []
    for k in range(n // 2):
        e, o = even[k], odd[k]
        if 4 * k == n and e[1] is not None and o[1] is not None:
            s = float(sign)
            one = (e[0] - o[1], e[1] + o[0])
            two = (e[0] + o[1], e[1] - o[0])
            a, b = (one, two) if s > 0 else (two, one)
        else:
            a, b = plus_minus(e, times(o, turn(sign * k / n)))
        low.append(a)
        high.append(b)
    return low + high


def turn(x):
    return complex(math.cos(2 * math.pi * x), math.sin(2 * math.pi * x))


def im_of(z):
    return jnp.zeros_like(z[0]) if z[1] is None else z[1]


def split_table(x):
    high = x.astype(ml_dtypes.bfloat16)
    low = (x - high.astype(np.float64)).astype(ml_dtypes.bfloat16)
    return np.stack([high, low])


def tables(blocks):
    length = blocks * LANES
    t = np.arange(LANES)
    phase = np.outer(t, t) % LANES / LANES
    forward = np.exp(-2j * np.pi * phase)
    backward = np.exp(2j * np.pi * phase) / length
    pair = lambda w: np.block([[w.real, w.imag], [-w.imag, w.real]])
    twist = np.exp(-2j * np.pi * np.outer(np.arange(blocks) + SHIFT, t) / length)
    return (
        split_table(pair(forward)),
        split_table(pair(backward)),
        np.stack([twist.real, twist.imag]).astype(np.float32),
    )


def kernel(
    nc,
    nt,
    q_hbm,
    k_hbm,
    v_hbm,
    filt_hbm,
    w_hbm,
    fwd_hbm,
    bwd_hbm,
    taps_hbm,
    skip_hbm,
    gain_hbm,
    twist_hbm,
    out,
    taps,
    skip,
    gain,
    twist,
    qbuf,
    kbuf,
    vbuf,
    wbuf,
    fwd,
    bwd,
    qfeat,
    mixed,
    mixed_t,
    frecv,
    srecv,
    csend,
    crecv,
    mid,
    high,
    low,
    fspec,
    dspec,
    gated,
    xsend,
    xrecv,
    xown,
    ysend,
    yrecv,
    yown,
    yxsend,
    yxrecv,
    xysend,
    xyrecv,
    mine,
    ssend,
    srow,
    load_sem,
    halo_send,
    halo_recv,
    filt_send,
    filt_recv,
    sig_send,
    sig_recv,
    conv_send,
    conv_recv,
    red_send,
    red_recv,
    row_send,
    row_recv,
):
    me, mt = lax.axis_index(CTX), lax.axis_index(TEN)
    tokens, width = q_hbm.shape
    per = width // nc
    parts = per // PART
    halves = tokens // LANES
    blocks = nc * halves
    outer = blocks // INNER
    step_s = INNER // halves
    share = out.shape[1]

    def partner(j, mine, n):
        step = n // 2 - (j + 1) // 2
        odd = j % 2
        return (mine + step * (1 - odd) + (n - step) * odd) % n

    def remote(src, dst, send, recv, device):
        return pltpu.make_async_remote_copy(
            src_ref=src,
            dst_ref=dst,
            send_sem=send,
            recv_sem=recv,
            device_id=device,
            device_id_type=pl.DeviceIdType.MESH,
        )

    barrier = pltpu.get_barrier_semaphore()

    @pl.loop(0, nc - 1, unroll=True)
    def _(j):
        pl.semaphore_signal(barrier, inc=1, device_id={CTX: partner(j, me, nc)})

    @pl.loop(0, nt - 1, unroll=True)
    def _(j):
        pl.semaphore_signal(barrier, inc=1, device_id={TEN: partner(j, mt, nt)})

    body = pl.ds(HALO, tokens)
    loads = [
        pltpu.make_async_copy(src, dst, load_sem.at[i])
        for i, (src, dst) in enumerate(
            (
                (k_hbm, kbuf.at[body, :]),
                (v_hbm, vbuf.at[body, :]),
                (q_hbm, qbuf.at[body, :]),
                (fwd_hbm, fwd),
                (bwd_hbm, bwd),
                (w_hbm, wbuf),
                (taps_hbm, taps),
                (twist_hbm, twist),
                (skip_hbm, skip),
                (gain_hbm, gain),
            )
        )
    ]
    for i in (0, 1, 6):
        loads[i].start()

    pl.semaphore_wait(barrier, nc - 1 + nt - 1)

    def settle(stage):
        @pl.when(me < nc - 1)
        def _():
            for copy in halos:
                copy.wait_send()

        @pl.loop(0, nc - 1)
        def _(j):
            p = partner(j, me, nc)
            filter_copy(p).wait_send()
            if stage > 2:
                for part in range(parts):
                    signal_copy(part, p).wait_send()
            if stage > 4:
                for group in range(parts, parts + halves - 1):
                    conv_copy(group, p).wait_send()

        if stage > 6:
            for c in range(halves):
                for kind, d in messages:
                    message(kind, c, d).wait_send()

            @pl.loop(0, nt - 1)
            def _(j):
                for c in range(halves):
                    row_copy(c, partner(j, mt, nt)).wait_send()

    halos = [
        remote(
            src.at[pl.ds(tokens - HALO, HALO), :],
            dst.at[pl.ds(0, HALO), :],
            halo_send.at[i],
            halo_recv.at[i],
            {CTX: (me + 1) % nc},
        )
        for i, (src, dst) in enumerate(((k_hbm, kbuf), (v_hbm, vbuf), (q_hbm, qbuf)))
    ]

    @pl.when(me < nc - 1)
    def _():
        for copy in halos:
            copy.start()

    @pl.when(me == 0)
    def _():
        for buf in (kbuf, vbuf, qbuf):
            buf[pl.ds(0, HALO), :] = jnp.zeros((HALO, width), BF16)

    def filter_copy(p):
        return remote(
            filt_hbm.at[pl.ds(pl.multiple_of(p * per, PART), per), :],
            frecv.at[me],
            filt_send.at[p],
            filt_recv.at[me],
            {CTX: p},
        )

    @pl.loop(0, nc - 1, unroll=True)
    def _(j):
        filter_copy(partner(j, me, nc)).start()

    own_filter = pltpu.make_async_copy(
        filt_hbm.at[pl.ds(pl.multiple_of(me * per, PART), per), :], frecv.at[me], filt_recv.at[me]
    )
    own_filter.start()
    for i in (2, 7, 3, 4, 8, 9, 5):
        loads[i].start()

    def feature(buf, r, row, lane):
        wide = buf[pl.ds(row, LANES + HALO), lane].astype(F32)[HALO - 8 :]
        one = pltpu.roll(wide, 1, 0)[8:]
        two = pltpu.roll(wide, 2, 0)[8:]
        return (
            taps[r, pl.ds(0, 1), lane] * wide[8:]
            + taps[r, pl.ds(1, 1), lane] * one
            + taps[r, pl.ds(2, 1), lane] * two
        )

    columns = width // LANES

    def place(i):
        row = pl.multiple_of(i // columns * LANES, LANES)
        col = pl.multiple_of(i % columns * LANES, LANES)
        return row, col

    for i in (6, 0, 1):
        loads[i].wait()

    @pl.when(me > 0)
    def _():
        for i in (0, 1):
            halos[i].wait_recv()

    @pl.loop(0, halves * columns)
    def _(i):
        row, col = place(i)
        lane = pl.ds(col, LANES)
        product = feature(kbuf, 1, row, lane) * feature(vbuf, 2, row, lane)
        mixed[pl.ds(row, LANES), lane] = product.astype(BF16)
        mixed_t[pl.ds(col, LANES), pl.ds(row, LANES)] = product.T.astype(BF16)

    def signal_copy(part, p):
        return remote(
            mixed_t.at[pl.ds(pl.multiple_of(p * per + part * PART, PART), PART), :],
            srecv.at[me, pl.ds(part * PART, PART), :],
            sig_send.at[part, p],
            sig_recv.at[part, me],
            {CTX: p},
        )

    for part in range(parts):

        @pl.loop(0, nc - 1, unroll=True)
        def _(j):
            signal_copy(part, partner(j, me, nc)).start()

        pltpu.make_async_copy(
            mixed_t.at[pl.ds(pl.multiple_of(me * per + part * PART, PART), PART), :],
            srecv.at[me, pl.ds(part * PART, PART), :],
            sig_recv.at[part, me],
        ).start()

    loads[2].wait()

    @pl.when(me > 0)
    def _():
        halos[2].wait_recv()

    @pl.loop(0, halves * columns)
    def _(i):
        row, col = place(i)
        lane = pl.ds(col, LANES)
        qfeat[pl.ds(row, LANES), lane] = feature(qbuf, 0, row, lane)

    def block_of(k1):
        return pl.ds(k1 * PART, PART)

    left, right = pl.ds(0, LANES), pl.ds(LANES, LANES)

    def outer_forward(recv, part):
        rows = pl.ds(pl.multiple_of(part * PART, PART), PART)
        for b in range(INNER):
            lane = pl.ds(b % halves * LANES, LANES)
            x = [
                times((recv[step_s * a + b // halves, rows, lane].astype(F32), None), turn(-a * SHIFT / outer))
                for a in range(outer)
            ]
            for q, z in enumerate(dft(x, -1)):
                re, im = times(z, turn(-b * (q + SHIFT) / blocks))
                mid[b, q, 0] = re
                mid[b, q, 1] = jnp.zeros_like(re) if im is None else im
        for q in range(outer):
            y = [(mid[b, q, 0], mid[b, q, 1]) for b in range(INNER)]
            for r, (re, im) in enumerate(dft(y, -1)):
                k1 = q + outer * r
                cos, sin = twist[0, pl.ds(k1, 1), :], twist[1, pl.ds(k1, 1), :]
                put(k1 * PART, re * cos - im * sin, im * cos + re * sin)

    def put(row, re, im):
        rows = pl.ds(row, re.shape[0])
        for lane, x in ((left, re), (right, im)):
            top = x.astype(BF16)
            high[rows, lane] = top
            low[rows, lane] = (x - top.astype(F32)).astype(BF16)

    def product(rows, table):
        a, b = high[rows, :], low[rows, :]
        dot = functools.partial(jnp.dot, preferred_element_type=F32)
        return dot(a, table[0]) + dot(b, table[0]) + dot(a, table[1])

    tall = min(256, blocks * PART)

    @pl.loop(0, nc)
    def _(s):
        pltpu.make_async_copy(frecv.at[s], frecv.at[s], filt_recv.at[s]).wait()

    for i in (3, 4, 7):
        loads[i].wait()

    @pl.loop(0, parts)
    def _(part):
        outer_forward(frecv, part)

        @pl.loop(0, blocks * PART // tall)
        def _(i):
            rows = pl.ds(pl.multiple_of(i * tall, tall), tall)
            fspec[part, rows, :] = product(rows, fwd)

    def conv_slice(group, p):
        if isinstance(group, int) and group >= parts:
            return pl.ds(pl.multiple_of(p * per, PART), per), pl.ds((group - parts + 1) * LANES, LANES)
        return pl.ds(pl.multiple_of(p * per + group * PART, PART), PART), left

    def conv_copy(group, p):
        src = csend.at[p, conv_slice(group, 0)[0], conv_slice(group, 0)[1]]
        return remote(
            src, crecv.at[conv_slice(group, me)], conv_send.at[group, p], conv_recv.at[group, me], {CTX: p}
        )

    def send_conv(group):
        @pl.loop(0, nc - 1)
        def _(j):
            conv_copy(group, partner(j, me, nc)).start()

        pltpu.make_async_copy(
            csend.at[me, conv_slice(group, 0)[0], conv_slice(group, 0)[1]],
            crecv.at[conv_slice(group, me)],
            conv_recv.at[group, me],
        ).start()

    def await_conv(group):
        @pl.loop(0, nc)
        def _(s):
            slot = crecv.at[conv_slice(group, s)]
            pltpu.make_async_copy(slot, slot, conv_recv.at[group, s]).wait()

    @pl.loop(0, parts)
    def _(part):
        rows16 = pl.ds(pl.multiple_of(part * PART, PART), PART)

        @pl.loop(0, nc)
        def _(s):
            slot = srecv.at[s, rows16, :]
            pltpu.make_async_copy(slot, slot, sig_recv.at[part, s]).wait()

        outer_forward(srecv, part)

        @pl.loop(0, blocks * PART // tall)
        def _(i):
            start = pl.multiple_of(i * tall, tall)
            rows = pl.ds(start, tall)
            spec = product(rows, fwd)
            re, im = spec[:, :LANES], spec[:, LANES:]
            fre, fim = fspec[part, rows, left], fspec[part, rows, right]
            put(start, re * fre - im * fim, re * fim + im * fre)
            dspec[rows, :] = product(rows, bwd)

        for q in range(outer):
            y = []
            for r in range(INNER):
                k1 = q + outer * r
                cos, sin = twist[0, pl.ds(k1, 1), :], twist[1, pl.ds(k1, 1), :]
                re, im = dspec[block_of(k1), left], dspec[block_of(k1), right]
                y.append((re * cos + im * sin, im * cos - re * sin))
            for b, z in enumerate(dft(y, 1)):
                re, im = times(z, turn(b * (q + SHIFT) / blocks))
                mid[b, q, 0] = re
                mid[b, q, 1] = im
        for b in range(INNER):
            lane = pl.ds(b % halves * LANES, LANES)
            y = [(mid[b, q, 0], mid[b, q, 1]) for q in range(outer)]
            for a, z in enumerate(dft(y, 1)):
                csend[step_s * a + b // halves, rows16, lane] = real_part_times(
                    z, turn(a * SHIFT / outer)
                ).astype(BF16)

        send_conv(part)

    @pl.loop(0, nc - 1)
    def _(j):
        for group in range(parts):
            conv_copy(group, partner(j, me, nc)).wait_send()

    for half in range(1, halves):
        send_conv(parts + half - 1)

    def gate(chunk):
        for group in range(parts) if chunk == 0 else [parts + chunk - 1]:
            await_conv(group)
        rows = rows_of(chunk)

        @pl.loop(0, columns)
        def _(i):
            lane = pl.ds(pl.multiple_of(i * LANES, LANES), LANES)
            conv = crecv[lane, rows].astype(F32).T
            gated[rows, lane] = (
                qfeat[rows, lane] * (conv + skip[:, lane] * mixed[rows, lane].astype(F32))
            ).astype(BF16)

    def rows_of(chunk):
        return pl.ds(chunk * LANES, LANES)

    ring_at, pair_at = mt % RING, mt // RING
    across = {TEN: (1 - pair_at) * RING + ring_at}

    def term(chunk, pair, ring):
        column = pl.multiple_of((pair * RING + ring) * share, LANES)
        return jnp.dot(gated[rows_of(chunk), :], wbuf[:, pl.ds(column, share)], preferred_element_type=F32)

    upper, lower = pl.ds(0, PIECE), pl.ds(PIECE, PIECE)
    further = (2, 1, 3)

    def ring_device(d):
        return {TEN: pair_at * RING + (ring_at + d) % RING}

    def message(kind, c, d):
        src, dst, device = {
            "far": lambda: (xsend.at[c, 0, d], xrecv.at[c, 0, d], ring_device(d)),
            "near": lambda: (xsend.at[c, 1, d], xrecv.at[c, 1, d], ring_device(d)),
            "pair": lambda: (ysend.at[c, d], yrecv.at[c, d], across),
            "then_ring": lambda: (yxsend.at[c, d], yxrecv.at[c, d], ring_device(d)),
            "then_pair": lambda: (xysend.at[c], xyrecv.at[c], across),
        }[kind]()
        k = ("far", "near", "pair", "then_ring", "then_pair").index(kind)
        return remote(src, dst, red_send.at[k, c, d], red_recv.at[k, c, d], device)

    messages = [
        (kind, d)
        for kind, ds in (
            ("far", further),
            ("near", further),
            ("pair", (0, 1, 2, 3)),
            ("then_ring", further),
            ("then_pair", (0,)),
        )
        for d in ds
    ]

    def start_sums(c):
        for d in (*further, 0):
            t = term(c, 1 - pair_at, (ring_at + d) % RING)
            ysend[c, d] = t[PIECE:].astype(BF16)
            message("pair", c, d).start()
            if d:
                xsend[c, 0, d] = t[:PIECE].astype(BF16)
                message("far", c, d).start()
            else:
                xown[c, 0] = t[:PIECE]
        for d in (*further, 0):
            t = term(c, pair_at, (ring_at + d) % RING)
            yown[c, d] = t[PIECE:]
            if d:
                xsend[c, 1, d] = t[:PIECE].astype(BF16)
                message("near", c, d).start()
            else:
                xown[c, 1] = t[:PIECE]

    def turn_corner(c):
        for d in further:
            message("far", c, d).wait_recv()
        s = xown[c, 0]
        for d in further:
            s = s + xrecv[c, 0, d].astype(F32)
        xysend[c] = s.astype(BF16)
        message("then_pair", c, 0).start()
        for d in further:
            message("pair", c, d).wait_recv()
            yxsend[c, d] = (yown[c, d] + yrecv[c, d].astype(F32)).astype(BF16)
            message("then_ring", c, d).start()

    def row_copy(chunk, p):
        return remote(
            ssend.at[chunk], srow.at[chunk, mt], row_send.at[chunk, p], row_recv.at[chunk, mt], {TEN: p}
        )

    def end_sums(c):
        squares = []

        def finish(rows, parts_of):
            square = jnp.zeros((PIECE, LANES), F32)
            for i in range(share // LANES):
                lane = pl.ds(i * LANES, LANES)
                s = parts_of[0][:, lane]
                for ref in parts_of[1:]:
                    s = s + ref[:, lane].astype(F32)
                mine[c, rows, lane] = s
                square = square + s * s
            squares.append(jnp.sum(square, axis=1, keepdims=True))

        for d in further:
            message("near", c, d).wait_recv()
        message("then_pair", c, 0).wait_recv()
        finish(upper, [xown.at[c, 1], *(xrecv.at[c, 1, d] for d in further), xyrecv.at[c]])
        message("pair", c, 0).wait_recv()
        for d in further:
            message("then_ring", c, d).wait_recv()
        finish(lower, [yown.at[c, 0], yrecv.at[c, 0], *(yxrecv.at[c, d] for d in further)])
        sums = jnp.concatenate(squares, axis=0)
        ssend[c] = jnp.broadcast_to(sums, (LANES, LANES)).T[:8]
        srow[c, mt] = ssend[c]

        @pl.loop(0, nt - 1, unroll=True)
        def _(j):
            row_copy(c, partner(j, mt, nt)).start()

    def normalize(c):
        @pl.loop(0, nt - 1)
        def _(j):
            p = partner(j, mt, nt)
            slot = srow.at[c, p]
            pltpu.make_async_copy(slot, slot, row_recv.at[c, p]).wait()

        s = srow[c, 0]
        for g in range(1, nt):
            s = s + srow[c, g]
        scale = lax.rsqrt(s * (1.0 / (share * nt)) + 1e-06)
        scale = jnp.broadcast_to(scale[:1], (LANES, LANES)).T
        for i in range(share // LANES):
            lane = pl.ds(i * LANES, LANES)
            out[rows_of(c), lane] = (mine[c, :, lane] * scale * gain[:, lane]).astype(BF16)

    loads[8].wait()
    gate(0)
    loads[5].wait()
    start_sums(0)
    gate(1)
    start_sums(1)
    turn_corner(0)
    turn_corner(1)
    end_sums(0)
    end_sums(1)
    loads[9].wait()
    normalize(0)
    normalize(1)

    settle(9)


def per_device(
    query_proj, key_proj, value_proj, short_taps, long_filter, skip_weight, out_weight, norm_gain
):
    nc, nt = lax.axis_size(CTX), lax.axis_size(TEN)
    tokens, width = query_proj.shape
    features = out_weight.shape[1]
    share = features // nt
    per = width // nc
    parts = per // PART
    blocks = nc * (tokens // LANES)
    outer = blocks // INNER
    halves = tokens // LANES
    fwd, bwd, twist = (jnp.asarray(x) for x in tables(blocks))
    anywhere = pl.BlockSpec(memory_space=pl.ANY)
    vmem = pl.BlockSpec(memory_space=pltpu.VMEM)
    dma = pltpu.SemaphoreType.DMA
    return pl.pallas_call(
        functools.partial(kernel, nc, nt),
        out_shape=pltpu.VMEM((tokens, share), BF16),
        in_specs=[anywhere] * 11,
        out_specs=vmem,
        scratch_shapes=[
            pltpu.VMEM(short_taps.shape, F32),
            pltpu.VMEM((1, width), F32),
            pltpu.VMEM((1, share), F32),
            pltpu.VMEM(twist.shape, F32),
            pltpu.VMEM((tokens + HALO, width), BF16),
            pltpu.VMEM((tokens + HALO, width), BF16),
            pltpu.VMEM((tokens + HALO, width), BF16),
            pltpu.VMEM((width, features), BF16),
            pltpu.VMEM(fwd.shape, BF16),
            pltpu.VMEM(bwd.shape, BF16),
            pltpu.VMEM((tokens, width), F32),
            pltpu.VMEM((tokens, width), BF16),
            pltpu.VMEM((width, tokens), BF16),
            pltpu.VMEM((nc, per, tokens), BF16),
            pltpu.VMEM((nc, per, tokens), BF16),
            pltpu.VMEM((nc, per, tokens), BF16),
            pltpu.VMEM((width, tokens), BF16),
            pltpu.VMEM((INNER, outer, 2, PART, LANES), F32),
            pltpu.VMEM((blocks * PART, 2 * LANES), BF16),
            pltpu.VMEM((blocks * PART, 2 * LANES), BF16),
            pltpu.VMEM((parts, blocks * PART, 2 * LANES), F32),
            pltpu.VMEM((blocks * PART, 2 * LANES), F32),
            pltpu.VMEM((tokens, width), BF16),
            pltpu.VMEM((halves, 2, RING, PIECE, share), BF16),
            pltpu.VMEM((halves, 2, RING, PIECE, share), BF16),
            pltpu.VMEM((halves, 2, PIECE, share), F32),
            pltpu.VMEM((halves, RING, PIECE, share), BF16),
            pltpu.VMEM((halves, RING, PIECE, share), BF16),
            pltpu.VMEM((halves, RING, PIECE, share), F32),
            pltpu.VMEM((halves, RING, PIECE, share), BF16),
            pltpu.VMEM((halves, RING, PIECE, share), BF16),
            pltpu.VMEM((halves, PIECE, share), BF16),
            pltpu.VMEM((halves, PIECE, share), BF16),
            pltpu.VMEM((halves, LANES, share), F32),
            pltpu.VMEM((halves, 8, LANES), F32),
            pltpu.VMEM((halves, nt, 8, LANES), F32),
            dma((10,)),
            dma((3,)),
            dma((3,)),
            dma((nc,)),
            dma((nc,)),
            dma((parts, nc)),
            dma((parts, nc)),
            dma((parts + halves - 1, nc)),
            dma((parts + halves - 1, nc)),
            dma((5, halves, RING)),
            dma((5, halves, RING)),
            dma((halves, nt)),
            dma((halves, nt)),
        ],
        compiler_params=pltpu.CompilerParams(
            collective_id=0, has_side_effects=True, vmem_limit_bytes=56 * 1024 * 1024
        ),
    )(
        query_proj,
        key_proj,
        value_proj,
        long_filter,
        out_weight,
        fwd,
        bwd,
        short_taps,
        skip_weight.reshape(1, width),
        norm_gain.reshape(1, share),
        twist,
    )


def solution(mesh):
    placed = (
        P(CTX, TEN),
        P(CTX, TEN),
        P(CTX, TEN),
        P(None, None, TEN),
        P(TEN, CTX),
        P(TEN),
        P(TEN, None),
        P(TEN),
    )
    return jax.shard_map(
        per_device, mesh=mesh, in_specs=placed, out_specs=P(CTX, TEN), check_vma=False
    )
```

```python
import functools
import math

import jax
import jax.numpy as jnp
import ml_dtypes
import numpy as np
from jax import lax
from jax.experimental import pallas as pl
from jax.experimental.pallas import tpu as pltpu
from jax.sharding import PartitionSpec as P

F32, BF16 = jnp.float32, jnp.bfloat16
CTX, TEN = "context", "tensor"
HALO = 16
LANES = 128
PART = 16
SHIFT = 0.25
GROUP = 2
INNER = 8
RING = 4
PIECE = LANES // 2


def times(z, c):
    re, im = z
    cr, ci = float(c.real), float(c.imag)
    cr = 0.0 if abs(cr) < 1e-12 else cr
    ci = 0.0 if abs(ci) < 1e-12 else ci
    if im is None:
        if ci == 0.0:
            return (re if cr == 1.0 else re * cr, None)
        return (re * cr, re * ci)
    if ci == 0.0:
        return z if cr == 1.0 else (re * cr, im * cr)
    if cr == 0.0:
        return (im * -ci, re * ci)
    if abs(abs(cr) - abs(ci)) < 1e-12:
        plus, minus = re + im, re - im
        if (cr > 0) == (ci > 0):
            return (minus * cr, plus * cr)
        return (plus * cr, minus * ci)
    return (re * cr - im * ci, re * ci + im * cr)


def real_part_times(z, c):
    re, im = z
    cr, ci = float(c.real), float(c.imag)
    if im is None or abs(ci) < 1e-12:
        return re if cr == 1.0 else re * cr
    return re * cr - im * ci


def plus_minus(a, b):
    (ar, ai), (br, bi) = a, b
    if ai is None and bi is None:
        return (ar + br, None), (ar - br, None)
    if ai is None:
        return (ar + br, bi), (ar - br, -bi)
    if bi is None:
        return (ar + br, ai), (ar - br, ai)
    return (ar + br, ai + bi), (ar - br, ai - bi)


def dft(x, sign):
    n = len(x)
    if n == 1:
        return list(x)
    even, odd = dft(x[0::2], sign), dft(x[1::2], sign)
    low, high = [], []
    for k in range(n // 2):
        e, o = even[k], odd[k]
        if 4 * k == n and e[1] is not None and o[1] is not None:
            s = float(sign)
            one = (e[0] - o[1], e[1] + o[0])
            two = (e[0] + o[1], e[1] - o[0])
            a, b = (one, two) if s > 0 else (two, one)
        else:
            a, b = plus_minus(e, times(o, turn(sign * k / n)))
        low.append(a)
        high.append(b)
    return low + high


def turn(x):
    return complex(math.cos(2 * math.pi * x), math.sin(2 * math.pi * x))


def im_of(z):
    return jnp.zeros_like(z[0]) if z[1] is None else z[1]


def split_table(x):
    high = x.astype(ml_dtypes.bfloat16)
    low = (x - high.astype(np.float64)).astype(ml_dtypes.bfloat16)
    return np.stack([high, low])


def tables(blocks):
    length = blocks * LANES
    t = np.arange(LANES)
    phase = np.outer(t, t) % LANES / LANES
    forward = np.exp(-2j * np.pi * phase)
    backward = np.exp(2j * np.pi * phase) / length
    pair = lambda w: np.block([[w.real, w.imag], [-w.imag, w.real]])
    twist = np.exp(-2j * np.pi * np.outer(np.arange(blocks) + SHIFT, t) / length)
    return (
        split_table(pair(forward)),
        split_table(pair(backward)),
        np.stack([twist.real, twist.imag]).astype(np.float32),
    )


def kernel(
    nc,
    nt,
    q_hbm,
    k_hbm,
    v_hbm,
    filt_hbm,
    w_hbm,
    fwd_hbm,
    bwd_hbm,
    taps_hbm,
    skip_hbm,
    gain_hbm,
    twist_hbm,
    out,
    taps,
    skip,
    gain,
    twist,
    qbuf,
    kbuf,
    vbuf,
    wbuf,
    fwd,
    bwd,
    qfeat,
    mixed,
    mixed_t,
    frecv,
    srecv,
    csend,
    crecv,
    mid,
    high,
    low,
    fspec,
    dspec,
    gated,
    xsend,
    xrecv,
    xown,
    ysend,
    yrecv,
    yown,
    yxsend,
    yxrecv,
    xysend,
    xyrecv,
    mine,
    ssend,
    srow,
    load_sem,
    halo_send,
    halo_recv,
    filt_send,
    filt_recv,
    sig_send,
    sig_recv,
    conv_send,
    conv_recv,
    red_send,
    red_recv,
    row_send,
    row_recv,
):
    me, mt = lax.axis_index(CTX), lax.axis_index(TEN)
    tokens, width = q_hbm.shape
    per = width // nc
    parts = per // PART
    halves = tokens // LANES
    blocks = nc * halves
    outer = blocks // INNER
    step_s = INNER // halves
    share = out.shape[1]

    def partner(j, mine, n):
        step = n // 2 - (j + 1) // 2
        odd = j % 2
        return (mine + step * (1 - odd) + (n - step) * odd) % n

    def remote(src, dst, send, recv, device):
        return pltpu.make_async_remote_copy(
            src_ref=src,
            dst_ref=dst,
            send_sem=send,
            recv_sem=recv,
            device_id=device,
            device_id_type=pl.DeviceIdType.MESH,
        )

    barrier = pltpu.get_barrier_semaphore()

    @pl.loop(0, nc - 1, unroll=True)
    def _(j):
        pl.semaphore_signal(barrier, inc=1, device_id={CTX: partner(j, me, nc)})

    @pl.loop(0, nt - 1, unroll=True)
    def _(j):
        pl.semaphore_signal(barrier, inc=1, device_id={TEN: partner(j, mt, nt)})

    body = pl.ds(HALO, tokens)
    loads = [
        pltpu.make_async_copy(src, dst, load_sem.at[i])
        for i, (src, dst) in enumerate(
            (
                (k_hbm, kbuf.at[body, :]),
                (v_hbm, vbuf.at[body, :]),
                (q_hbm, qbuf.at[body, :]),
                (fwd_hbm, fwd),
                (bwd_hbm, bwd),
                (w_hbm, wbuf),
                (taps_hbm, taps),
                (twist_hbm, twist),
                (skip_hbm, skip),
                (gain_hbm, gain),
            )
        )
    ]
    for i in (0, 1, 6):
        loads[i].start()

    pl.semaphore_wait(barrier, nc - 1 + nt - 1)

    def settle(stage):
        @pl.when(me < nc - 1)
        def _():
            for copy in halos:
                copy.wait_send()

        @pl.loop(0, nc - 1)
        def _(j):
            p = partner(j, me, nc)
            filter_copy(p).wait_send()
            if stage > 2:
                for part in range(parts):
                    signal_copy(part, p).wait_send()
            if stage > 4:
                for group in range(parts + halves - 1):
                    conv_copy(group, p).wait_send()

        if stage > 6:
            for c in range(halves):
                for kind, d in messages:
                    message(kind, c, d).wait_send()

            @pl.loop(0, nt - 1)
            def _(j):
                for c in range(halves):
                    row_copy(c, partner(j, mt, nt)).wait_send()

    halos = [
        remote(
            src.at[pl.ds(tokens - HALO, HALO), :],
            dst.at[pl.ds(0, HALO), :],
            halo_send.at[i],
            halo_recv.at[i],
            {CTX: (me + 1) % nc},
        )
        for i, (src, dst) in enumerate(((k_hbm, kbuf), (v_hbm, vbuf), (q_hbm, qbuf)))
    ]

    @pl.when(me < nc - 1)
    def _():
        for copy in halos:
            copy.start()

    @pl.when(me == 0)
    def _():
        for buf in (kbuf, vbuf, qbuf):
            buf[pl.ds(0, HALO), :] = jnp.zeros((HALO, width), BF16)

    def filter_copy(p):
        return remote(
            filt_hbm.at[pl.ds(pl.multiple_of(p * per, PART), per), :],
            frecv.at[me],
            filt_send.at[p],
            filt_recv.at[me],
            {CTX: p},
        )

    @pl.loop(0, nc - 1, unroll=True)
    def _(j):
        filter_copy(partner(j, me, nc)).start()

    own_filter = pltpu.make_async_copy(
        filt_hbm.at[pl.ds(pl.multiple_of(me * per, PART), per), :], frecv.at[me], filt_recv.at[me]
    )
    own_filter.start()
    for i in (2, 7, 3, 4, 8, 9, 5):
        loads[i].start()

    def feature(buf, r, row, lane):
        wide = buf[pl.ds(row, LANES + HALO), lane].astype(F32)[HALO - 8 :]
        one = pltpu.roll(wide, 1, 0)[8:]
        two = pltpu.roll(wide, 2, 0)[8:]
        return (
            taps[r, pl.ds(0, 1), lane] * wide[8:]
            + taps[r, pl.ds(1, 1), lane] * one
            + taps[r, pl.ds(2, 1), lane] * two
        )

    columns = width // LANES

    def place(i):
        row = pl.multiple_of(i // columns * LANES, LANES)
        col = pl.multiple_of(i % columns * LANES, LANES)
        return row, col

    for i in (6, 0, 1):
        loads[i].wait()

    @pl.when(me > 0)
    def _():
        for i in (0, 1):
            halos[i].wait_recv()

    @pl.loop(0, halves * columns)
    def _(i):
        row, col = place(i)
        lane = pl.ds(col, LANES)
        product = feature(kbuf, 1, row, lane) * feature(vbuf, 2, row, lane)
        mixed[pl.ds(row, LANES), lane] = product.astype(BF16)
        mixed_t[pl.ds(col, LANES), pl.ds(row, LANES)] = product.T.astype(BF16)

    def signal_copy(part, p):
        return remote(
            mixed_t.at[pl.ds(pl.multiple_of(p * per + part * PART, PART), PART), :],
            srecv.at[me, pl.ds(part * PART, PART), :],
            sig_send.at[part, p],
            sig_recv.at[part, me],
            {CTX: p},
        )

    for part in range(parts):

        @pl.loop(0, nc - 1, unroll=True)
        def _(j):
            signal_copy(part, partner(j, me, nc)).start()

        pltpu.make_async_copy(
            mixed_t.at[pl.ds(pl.multiple_of(me * per + part * PART, PART), PART), :],
            srecv.at[me, pl.ds(part * PART, PART), :],
            sig_recv.at[part, me],
        ).start()

    loads[2].wait()

    @pl.when(me > 0)
    def _():
        halos[2].wait_recv()

    @pl.loop(0, halves * columns)
    def _(i):
        row, col = place(i)
        lane = pl.ds(col, LANES)
        qfeat[pl.ds(row, LANES), lane] = feature(qbuf, 0, row, lane)

    def row_at(q, r):
        return (q * INNER + r) * PART

    together = min(GROUP, outer)
    groups = [range(q, q + together) for q in range(0, outer, together)]

    def group_rows(qs):
        return pl.ds(row_at(qs[0], 0), together * INNER * PART)

    left, right = pl.ds(0, LANES), pl.ds(LANES, LANES)

    def outer_forward(recv, part):
        rows = pl.ds(pl.multiple_of(part * PART, PART), PART)
        for b in range(INNER):
            lane = pl.ds(b % halves * LANES, LANES)
            x = [
                times((recv[step_s * a + b // halves, rows, lane].astype(F32), None), turn(-a * SHIFT / outer))
                for a in range(outer)
            ]
            for q, z in enumerate(dft(x, -1)):
                re, im = times(z, turn(-b * (q + SHIFT) / blocks))
                mid[b, q, 0] = re
                mid[b, q, 1] = jnp.zeros_like(re) if im is None else im

    def inner_forward(qs):
        for q in qs:
            y = [(mid[b, q, 0], mid[b, q, 1]) for b in range(INNER)]
            for r, (re, im) in enumerate(dft(y, -1)):
                k1 = q + outer * r
                cos, sin = twist[0, pl.ds(k1, 1), :], twist[1, pl.ds(k1, 1), :]
                put(row_at(q, r), re * cos - im * sin, im * cos + re * sin)

    def inner_backward(qs):
        for q in qs:
            y = []
            for r in range(INNER):
                k1, rows = q + outer * r, pl.ds(row_at(q, r), PART)
                cos, sin = twist[0, pl.ds(k1, 1), :], twist[1, pl.ds(k1, 1), :]
                re, im = dspec[rows, left], dspec[rows, right]
                y.append((re * cos + im * sin, im * cos - re * sin))
            for b, z in enumerate(dft(y, 1)):
                re, im = times(z, turn(b * (q + SHIFT) / blocks))
                mid[b, q, 0] = re
                mid[b, q, 1] = im

    def put(row, re, im):
        rows = pl.ds(row, re.shape[0])
        for lane, x in ((left, re), (right, im)):
            top = x.astype(BF16)
            high[rows, lane] = top
            low[rows, lane] = (x - top.astype(F32)).astype(BF16)

    def product(rows, table):
        a, b = high[rows, :], low[rows, :]
        dot = functools.partial(jnp.dot, preferred_element_type=F32)
        return dot(a, table[0]) + dot(b, table[0]) + dot(a, table[1])

    @pl.loop(0, nc)
    def _(s):
        pltpu.make_async_copy(frecv.at[s], frecv.at[s], filt_recv.at[s]).wait()

    for i in (3, 4, 7):
        loads[i].wait()

    @pl.loop(0, parts)
    def _(part):
        outer_forward(frecv, part)
        for qs in groups:
            inner_forward(qs)
            fspec[part, group_rows(qs), :] = product(group_rows(qs), fwd)

    def conv_slice(group, p):
        if isinstance(group, int) and group >= parts:
            return pl.ds(pl.multiple_of(p * per, PART), per), pl.ds((group - parts + 1) * LANES, LANES)
        return pl.ds(pl.multiple_of(p * per + group * PART, PART), PART), left

    def conv_copy(group, p):
        src = csend.at[p, conv_slice(group, 0)[0], conv_slice(group, 0)[1]]
        return remote(
            src, crecv.at[conv_slice(group, me)], conv_send.at[group, p], conv_recv.at[group, me], {CTX: p}
        )

    def send_conv(group):
        @pl.loop(0, nc - 1)
        def _(j):
            conv_copy(group, partner(j, me, nc)).start()

        pltpu.make_async_copy(
            csend.at[me, conv_slice(group, 0)[0], conv_slice(group, 0)[1]],
            crecv.at[conv_slice(group, me)],
            conv_recv.at[group, me],
        ).start()

    def await_conv(group):
        @pl.loop(0, nc)
        def _(s):
            slot = crecv.at[conv_slice(group, s)]
            pltpu.make_async_copy(slot, slot, conv_recv.at[group, s]).wait()

    @pl.loop(0, parts)
    def _(part):
        rows16 = pl.ds(pl.multiple_of(part * PART, PART), PART)

        @pl.loop(0, nc)
        def _(s):
            slot = srecv.at[s, rows16, :]
            pltpu.make_async_copy(slot, slot, sig_recv.at[part, s]).wait()

        outer_forward(srecv, part)

        for qs in groups:
            rows = group_rows(qs)
            inner_forward(qs)
            spec = product(rows, fwd)
            re, im = spec[:, :LANES], spec[:, LANES:]
            fre, fim = fspec[part, rows, left], fspec[part, rows, right]
            put(row_at(qs[0], 0), re * fre - im * fim, re * fim + im * fre)
            dspec[rows, :] = product(rows, bwd)
            inner_backward(qs)

        for b in range(INNER):
            lane = pl.ds(b % halves * LANES, LANES)
            y = [(mid[b, q, 0], mid[b, q, 1]) for q in range(outer)]
            for a, z in enumerate(dft(y, 1)):
                csend[step_s * a + b // halves, rows16, lane] = real_part_times(
                    z, turn(a * SHIFT / outer)
                ).astype(BF16)

        send_conv(part)

    for half in range(1, halves):
        send_conv(parts + half - 1)

    def gate(chunk):
        for group in range(parts) if chunk == 0 else [parts + chunk - 1]:
            await_conv(group)
        rows = rows_of(chunk)

        @pl.loop(0, columns)
        def _(i):
            lane = pl.ds(pl.multiple_of(i * LANES, LANES), LANES)
            conv = crecv[lane, rows].astype(F32).T
            gated[rows, lane] = (
                qfeat[rows, lane] * (conv + skip[:, lane] * mixed[rows, lane].astype(F32))
            ).astype(BF16)

    def rows_of(chunk):
        return pl.ds(chunk * LANES, LANES)

    ring_at, pair_at = mt % RING, mt // RING
    across = {TEN: (1 - pair_at) * RING + ring_at}

    def term(chunk, pair, ring):
        column = pl.multiple_of((pair * RING + ring) * share, LANES)
        return jnp.dot(gated[rows_of(chunk), :], wbuf[:, pl.ds(column, share)], preferred_element_type=F32)

    upper, lower = pl.ds(0, PIECE), pl.ds(PIECE, PIECE)
    further = (2, 1, 3)

    def ring_device(d):
        return {TEN: pair_at * RING + (ring_at + d) % RING}

    def message(kind, c, d):
        src, dst, device = {
            "far": lambda: (xsend.at[c, 0, d], xrecv.at[c, 0, d], ring_device(d)),
            "near": lambda: (xsend.at[c, 1, d], xrecv.at[c, 1, d], ring_device(d)),
            "pair": lambda: (ysend.at[c, d], yrecv.at[c, d], across),
            "then_ring": lambda: (yxsend.at[c, d], yxrecv.at[c, d], ring_device(d)),
            "then_pair": lambda: (xysend.at[c], xyrecv.at[c], across),
        }[kind]()
        k = ("far", "near", "pair", "then_ring", "then_pair").index(kind)
        return remote(src, dst, red_send.at[k, c, d], red_recv.at[k, c, d], device)

    messages = [
        (kind, d)
        for kind, ds in (
            ("far", further),
            ("near", further),
            ("pair", (0, 1, 2, 3)),
            ("then_ring", further),
            ("then_pair", (0,)),
        )
        for d in ds
    ]

    def start_sums(c):
        for d in (*further, 0):
            t = term(c, 1 - pair_at, (ring_at + d) % RING)
            ysend[c, d] = t[PIECE:].astype(BF16)
            message("pair", c, d).start()
            if d:
                xsend[c, 0, d] = t[:PIECE].astype(BF16)
                message("far", c, d).start()
            else:
                xown[c, 0] = t[:PIECE]
        for d in (*further, 0):
            t = term(c, pair_at, (ring_at + d) % RING)
            yown[c, d] = t[PIECE:]
            if d:
                xsend[c, 1, d] = t[:PIECE].astype(BF16)
                message("near", c, d).start()
            else:
                xown[c, 1] = t[:PIECE]

    def turn_corner(c):
        for d in further:
            message("far", c, d).wait_recv()
        s = xown[c, 0]
        for d in further:
            s = s + xrecv[c, 0, d].astype(F32)
        xysend[c] = s.astype(BF16)
        message("then_pair", c, 0).start()
        for d in further:
            message("pair", c, d).wait_recv()
            yxsend[c, d] = (yown[c, d] + yrecv[c, d].astype(F32)).astype(BF16)
            message("then_ring", c, d).start()

    def row_copy(chunk, p):
        return remote(
            ssend.at[chunk], srow.at[chunk, mt], row_send.at[chunk, p], row_recv.at[chunk, mt], {TEN: p}
        )

    def end_sums(c):
        squares = []

        def finish(rows, parts_of):
            square = jnp.zeros((PIECE, LANES), F32)
            for i in range(share // LANES):
                lane = pl.ds(i * LANES, LANES)
                s = parts_of[0][:, lane]
                for ref in parts_of[1:]:
                    s = s + ref[:, lane].astype(F32)
                mine[c, rows, lane] = s
                square = square + s * s
            squares.append(jnp.sum(square, axis=1, keepdims=True))

        for d in further:
            message("near", c, d).wait_recv()
        message("then_pair", c, 0).wait_recv()
        finish(upper, [xown.at[c, 1], *(xrecv.at[c, 1, d] for d in further), xyrecv.at[c]])
        message("pair", c, 0).wait_recv()
        for d in further:
            message("then_ring", c, d).wait_recv()
        finish(lower, [yown.at[c, 0], yrecv.at[c, 0], *(yxrecv.at[c, d] for d in further)])
        sums = jnp.concatenate(squares, axis=0)
        ssend[c] = jnp.broadcast_to(sums, (LANES, LANES)).T[:8]
        srow[c, mt] = ssend[c]

        @pl.loop(0, nt - 1, unroll=True)
        def _(j):
            row_copy(c, partner(j, mt, nt)).start()

    def normalize(c):
        @pl.loop(0, nt - 1)
        def _(j):
            p = partner(j, mt, nt)
            slot = srow.at[c, p]
            pltpu.make_async_copy(slot, slot, row_recv.at[c, p]).wait()

        s = srow[c, 0]
        for g in range(1, nt):
            s = s + srow[c, g]
        scale = lax.rsqrt(s * (1.0 / (share * nt)) + 1e-06)
        scale = jnp.broadcast_to(scale[:1], (LANES, LANES)).T
        for i in range(share // LANES):
            lane = pl.ds(i * LANES, LANES)
            out[rows_of(c), lane] = (mine[c, :, lane] * scale * gain[:, lane]).astype(BF16)

    loads[8].wait()
    gate(0)
    loads[5].wait()
    start_sums(0)
    gate(1)
    start_sums(1)
    turn_corner(0)
    turn_corner(1)
    end_sums(0)
    end_sums(1)
    loads[9].wait()
    normalize(0)
    normalize(1)

    settle(9)


def per_device(
    query_proj, key_proj, value_proj, short_taps, long_filter, skip_weight, out_weight, norm_gain
):
    nc, nt = lax.axis_size(CTX), lax.axis_size(TEN)
    tokens, width = query_proj.shape
    features = out_weight.shape[1]
    share = features // nt
    per = width // nc
    parts = per // PART
    blocks = nc * (tokens // LANES)
    outer = blocks // INNER
    halves = tokens // LANES
    fwd, bwd, twist = (jnp.asarray(x) for x in tables(blocks))
    anywhere = pl.BlockSpec(memory_space=pl.ANY)
    vmem = pl.BlockSpec(memory_space=pltpu.VMEM)
    dma = pltpu.SemaphoreType.DMA
    return pl.pallas_call(
        functools.partial(kernel, nc, nt),
        out_shape=pltpu.VMEM((tokens, share), BF16),
        in_specs=[anywhere] * 11,
        out_specs=vmem,
        scratch_shapes=[
            pltpu.VMEM(short_taps.shape, F32),
            pltpu.VMEM((1, width), F32),
            pltpu.VMEM((1, share), F32),
            pltpu.VMEM(twist.shape, F32),
            pltpu.VMEM((tokens + HALO, width), BF16),
            pltpu.VMEM((tokens + HALO, width), BF16),
            pltpu.VMEM((tokens + HALO, width), BF16),
            pltpu.VMEM((width, features), BF16),
            pltpu.VMEM(fwd.shape, BF16),
            pltpu.VMEM(bwd.shape, BF16),
            pltpu.VMEM((tokens, width), F32),
            pltpu.VMEM((tokens, width), BF16),
            pltpu.VMEM((width, tokens), BF16),
            pltpu.VMEM((nc, per, tokens), BF16),
            pltpu.VMEM((nc, per, tokens), BF16),
            pltpu.VMEM((nc, per, tokens), BF16),
            pltpu.VMEM((width, tokens), BF16),
            pltpu.VMEM((INNER, outer, 2, PART, LANES), F32),
            pltpu.VMEM((blocks * PART, 2 * LANES), BF16),
            pltpu.VMEM((blocks * PART, 2 * LANES), BF16),
            pltpu.VMEM((parts, blocks * PART, 2 * LANES), F32),
            pltpu.VMEM((blocks * PART, 2 * LANES), F32),
            pltpu.VMEM((tokens, width), BF16),
            pltpu.VMEM((halves, 2, RING, PIECE, share), BF16),
            pltpu.VMEM((halves, 2, RING, PIECE, share), BF16),
            pltpu.VMEM((halves, 2, PIECE, share), F32),
            pltpu.VMEM((halves, RING, PIECE, share), BF16),
            pltpu.VMEM((halves, RING, PIECE, share), BF16),
            pltpu.VMEM((halves, RING, PIECE, share), F32),
            pltpu.VMEM((halves, RING, PIECE, share), BF16),
            pltpu.VMEM((halves, RING, PIECE, share), BF16),
            pltpu.VMEM((halves, PIECE, share), BF16),
            pltpu.VMEM((halves, PIECE, share), BF16),
            pltpu.VMEM((halves, LANES, share), F32),
            pltpu.VMEM((halves, 8, LANES), F32),
            pltpu.VMEM((halves, nt, 8, LANES), F32),
            dma((10,)),
            dma((3,)),
            dma((3,)),
            dma((nc,)),
            dma((nc,)),
            dma((parts, nc)),
            dma((parts, nc)),
            dma((parts + halves - 1, nc)),
            dma((parts + halves - 1, nc)),
            dma((5, halves, RING)),
            dma((5, halves, RING)),
            dma((halves, nt)),
            dma((halves, nt)),
        ],
        compiler_params=pltpu.CompilerParams(
            collective_id=0, has_side_effects=True, vmem_limit_bytes=56 * 1024 * 1024
        ),
    )(
        query_proj,
        key_proj,
        value_proj,
        long_filter,
        out_weight,
        fwd,
        bwd,
        short_taps,
        skip_weight.reshape(1, width),
        norm_gain.reshape(1, share),
        twist,
    )


def solution(mesh):
    placed = (
        P(CTX, TEN),
        P(CTX, TEN),
        P(CTX, TEN),
        P(None, None, TEN),
        P(TEN, CTX),
        P(TEN),
        P(TEN, None),
        P(TEN),
    )
    return jax.shard_map(
        per_device, mesh=mesh, in_specs=placed, out_specs=P(CTX, TEN), check_vma=False
    )
```

```python
import functools
import math

import jax
import jax.numpy as jnp
import ml_dtypes
import numpy as np
from jax import lax
from jax.experimental import pallas as pl
from jax.experimental.pallas import tpu as pltpu
from jax.sharding import PartitionSpec as P

F32, BF16 = jnp.float32, jnp.bfloat16
CTX, TEN = "context", "tensor"
HALO = 16
LANES = 128
PART = 16
SHIFT = 0.25
GROUP = 2
INNER = 8
RING = 4
PIECE = LANES // 2


def times(z, c):
    re, im = z
    cr, ci = float(c.real), float(c.imag)
    cr = 0.0 if abs(cr) < 1e-12 else cr
    ci = 0.0 if abs(ci) < 1e-12 else ci
    if im is None:
        if ci == 0.0:
            return (re if cr == 1.0 else re * cr, None)
        return (re * cr, re * ci)
    if ci == 0.0:
        return z if cr == 1.0 else (re * cr, im * cr)
    if cr == 0.0:
        return (im * -ci, re * ci)
    if abs(abs(cr) - abs(ci)) < 1e-12:
        plus, minus = re + im, re - im
        if (cr > 0) == (ci > 0):
            return (minus * cr, plus * cr)
        return (plus * cr, minus * ci)
    return (re * cr - im * ci, re * ci + im * cr)


def real_part_times(z, c):
    re, im = z
    cr, ci = float(c.real), float(c.imag)
    if im is None or abs(ci) < 1e-12:
        return re if cr == 1.0 else re * cr
    return re * cr - im * ci


def plus_minus(a, b):
    (ar, ai), (br, bi) = a, b
    if ai is None and bi is None:
        return (ar + br, None), (ar - br, None)
    if ai is None:
        return (ar + br, bi), (ar - br, -bi)
    if bi is None:
        return (ar + br, ai), (ar - br, ai)
    return (ar + br, ai + bi), (ar - br, ai - bi)


def dft(x, sign):
    n = len(x)
    if n == 1:
        return list(x)
    even, odd = dft(x[0::2], sign), dft(x[1::2], sign)
    low, high = [], []
    for k in range(n // 2):
        e, o = even[k], odd[k]
        if 4 * k == n and e[1] is not None and o[1] is not None:
            s = float(sign)
            one = (e[0] - o[1], e[1] + o[0])
            two = (e[0] + o[1], e[1] - o[0])
            a, b = (one, two) if s > 0 else (two, one)
        else:
            a, b = plus_minus(e, times(o, turn(sign * k / n)))
        low.append(a)
        high.append(b)
    return low + high


def turn(x):
    return complex(math.cos(2 * math.pi * x), math.sin(2 * math.pi * x))


def im_of(z):
    return jnp.zeros_like(z[0]) if z[1] is None else z[1]


def split_table(x):
    high = x.astype(ml_dtypes.bfloat16)
    low = (x - high.astype(np.float64)).astype(ml_dtypes.bfloat16)
    return np.stack([high, low])


def tables(blocks):
    length = blocks * LANES
    t = np.arange(LANES)
    phase = np.outer(t, t) % LANES / LANES
    forward = np.exp(-2j * np.pi * phase)
    backward = np.exp(2j * np.pi * phase) / length
    pair = lambda w: np.block([[w.real, w.imag], [-w.imag, w.real]])
    twist = np.exp(-2j * np.pi * np.outer(np.arange(blocks) + SHIFT, t) / length)
    return (
        split_table(pair(forward)),
        split_table(pair(backward)),
        np.stack([twist.real, twist.imag]).astype(np.float32),
    )


def kernel(
    nc,
    nt,
    q_hbm,
    k_hbm,
    v_hbm,
    filt_hbm,
    w_hbm,
    fwd_hbm,
    bwd_hbm,
    taps_hbm,
    skip_hbm,
    gain_hbm,
    twist_hbm,
    out,
    taps,
    skip,
    gain,
    twist,
    qbuf,
    kbuf,
    vbuf,
    wbuf,
    fwd,
    bwd,
    qfeat,
    mixed,
    mixed_t,
    frecv,
    srecv,
    csend,
    crecv,
    mid,
    high,
    low,
    fspec,
    dspec,
    gated,
    xsend,
    xrecv,
    xown,
    ysend,
    yrecv,
    yown,
    yxsend,
    yxrecv,
    xysend,
    xyrecv,
    mine,
    ssend,
    srow,
    load_sem,
    halo_send,
    halo_recv,
    filt_send,
    filt_recv,
    sig_send,
    sig_recv,
    conv_send,
    conv_recv,
    red_send,
    red_recv,
    row_send,
    row_recv,
):
    me, mt = lax.axis_index(CTX), lax.axis_index(TEN)
    tokens, width = q_hbm.shape
    per = width // nc
    parts = per // PART
    halves = tokens // LANES
    blocks = nc * halves
    outer = blocks // INNER
    step_s = INNER // halves
    share = out.shape[1]

    def partner(j, mine, n):
        step = n // 2 - (j + 1) // 2
        odd = j % 2
        return (mine + step * (1 - odd) + (n - step) * odd) % n

    def remote(src, dst, send, recv, device):
        return pltpu.make_async_remote_copy(
            src_ref=src,
            dst_ref=dst,
            send_sem=send,
            recv_sem=recv,
            device_id=device,
            device_id_type=pl.DeviceIdType.MESH,
        )

    barrier = pltpu.get_barrier_semaphore()

    @pl.loop(0, nc - 1, unroll=True)
    def _(j):
        pl.semaphore_signal(barrier, inc=1, device_id={CTX: partner(j, me, nc)})

    @pl.loop(0, nt - 1, unroll=True)
    def _(j):
        pl.semaphore_signal(barrier, inc=1, device_id={TEN: partner(j, mt, nt)})

    body = pl.ds(HALO, tokens)
    loads = [
        pltpu.make_async_copy(src, dst, load_sem.at[i])
        for i, (src, dst) in enumerate(
            (
                (k_hbm, kbuf.at[body, :]),
                (v_hbm, vbuf.at[body, :]),
                (q_hbm, qbuf.at[body, :]),
                (fwd_hbm, fwd),
                (bwd_hbm, bwd),
                (w_hbm, wbuf),
                (taps_hbm, taps),
                (twist_hbm, twist),
                (skip_hbm, skip),
                (gain_hbm, gain),
            )
        )
    ]
    for i in (0, 1, 6):
        loads[i].start()

    pl.semaphore_wait(barrier, nc - 1 + nt - 1)

    def settle(stage):
        @pl.when(me < nc - 1)
        def _():
            for copy in halos:
                copy.wait_send()

        @pl.loop(0, nc - 1)
        def _(j):
            p = partner(j, me, nc)
            filter_copy(p).wait_send()
            if stage > 2:
                for part in range(parts):
                    signal_copy(part, p).wait_send()
            if stage > 4:
                for group in range(parts + halves - 1):
                    conv_copy(group, p).wait_send()

        if stage > 6:
            for c in range(halves):
                for kind, d in messages:
                    message(kind, c, d).wait_send()

            @pl.loop(0, nt - 1)
            def _(j):
                for c in range(halves):
                    row_copy(c, partner(j, mt, nt)).wait_send()

    halos = [
        remote(
            src.at[pl.ds(tokens - HALO, HALO), :],
            dst.at[pl.ds(0, HALO), :],
            halo_send.at[i],
            halo_recv.at[i],
            {CTX: (me + 1) % nc},
        )
        for i, (src, dst) in enumerate(((k_hbm, kbuf), (v_hbm, vbuf), (q_hbm, qbuf)))
    ]

    @pl.when(me < nc - 1)
    def _():
        for copy in halos:
            copy.start()

    @pl.when(me == 0)
    def _():
        for buf in (kbuf, vbuf, qbuf):
            buf[pl.ds(0, HALO), :] = jnp.zeros((HALO, width), BF16)

    def filter_copy(p):
        return remote(
            filt_hbm.at[pl.ds(pl.multiple_of(p * per, PART), per), :],
            frecv.at[me],
            filt_send.at[p],
            filt_recv.at[me],
            {CTX: p},
        )

    @pl.loop(0, nc - 1, unroll=True)
    def _(j):
        filter_copy(partner(j, me, nc)).start()

    own_filter = pltpu.make_async_copy(
        filt_hbm.at[pl.ds(pl.multiple_of(me * per, PART), per), :], frecv.at[me], filt_recv.at[me]
    )
    own_filter.start()
    for i in (2, 7, 3, 4, 8, 9, 5):
        loads[i].start()

    def feature(buf, r, row, lane):
        wide = buf[pl.ds(row, LANES + HALO), lane].astype(F32)[HALO - 8 :]
        one = pltpu.roll(wide, 1, 0)[8:]
        two = pltpu.roll(wide, 2, 0)[8:]
        return (
            taps[r, pl.ds(0, 1), lane] * wide[8:]
            + taps[r, pl.ds(1, 1), lane] * one
            + taps[r, pl.ds(2, 1), lane] * two
        )

    columns = width // LANES

    def place(i):
        row = pl.multiple_of(i // columns * LANES, LANES)
        col = pl.multiple_of(i % columns * LANES, LANES)
        return row, col

    for i in (6, 0, 1):
        loads[i].wait()

    @pl.when(me > 0)
    def _():
        for i in (0, 1):
            halos[i].wait_recv()

    @pl.loop(0, halves * columns)
    def _(i):
        row, col = place(i)
        lane = pl.ds(col, LANES)
        product = feature(kbuf, 1, row, lane) * feature(vbuf, 2, row, lane)
        mixed[pl.ds(row, LANES), lane] = product.astype(BF16)
        mixed_t[pl.ds(col, LANES), pl.ds(row, LANES)] = product.T.astype(BF16)

    def signal_copy(part, p):
        return remote(
            mixed_t.at[pl.ds(pl.multiple_of(p * per + part * PART, PART), PART), :],
            srecv.at[me, pl.ds(part * PART, PART), :],
            sig_send.at[part, p],
            sig_recv.at[part, me],
            {CTX: p},
        )

    for part in range(parts):

        @pl.loop(0, nc - 1, unroll=True)
        def _(j):
            signal_copy(part, partner(j, me, nc)).start()

        pltpu.make_async_copy(
            mixed_t.at[pl.ds(pl.multiple_of(me * per + part * PART, PART), PART), :],
            srecv.at[me, pl.ds(part * PART, PART), :],
            sig_recv.at[part, me],
        ).start()

    loads[2].wait()

    @pl.when(me > 0)
    def _():
        halos[2].wait_recv()

    @pl.loop(0, halves * columns)
    def _(i):
        row, col = place(i)
        lane = pl.ds(col, LANES)
        qfeat[pl.ds(row, LANES), lane] = feature(qbuf, 0, row, lane)

    def row_at(q, r):
        return (q * INNER + r) * PART

    together = min(GROUP, outer)
    groups = [range(q, q + together) for q in range(0, outer, together)]

    def group_rows(qs):
        return pl.ds(row_at(qs[0], 0), together * INNER * PART)

    left, right = pl.ds(0, LANES), pl.ds(LANES, LANES)

    def outer_forward(recv, part):
        rows = pl.ds(pl.multiple_of(part * PART, PART), PART)
        for b in range(INNER):
            lane = pl.ds(b % halves * LANES, LANES)
            x = [
                times((recv[step_s * a + b // halves, rows, lane].astype(F32), None), turn(-a * SHIFT / outer))
                for a in range(outer)
            ]
            for q, z in enumerate(dft(x, -1)):
                re, im = times(z, turn(-b * (q + SHIFT) / blocks))
                mid[b, q, 0] = re
                mid[b, q, 1] = jnp.zeros_like(re) if im is None else im

    def inner_forward(qs):
        for q in qs:
            y = [(mid[b, q, 0], mid[b, q, 1]) for b in range(INNER)]
            for r, (re, im) in enumerate(dft(y, -1)):
                k1 = q + outer * r
                cos, sin = twist[0, pl.ds(k1, 1), :], twist[1, pl.ds(k1, 1), :]
                put(row_at(q, r), re * cos - im * sin, im * cos + re * sin)

    def inner_backward(qs):
        for q in qs:
            y = []
            for r in range(INNER):
                k1, rows = q + outer * r, pl.ds(row_at(q, r), PART)
                cos, sin = twist[0, pl.ds(k1, 1), :], twist[1, pl.ds(k1, 1), :]
                re, im = dspec[rows, left], dspec[rows, right]
                y.append((re * cos + im * sin, im * cos - re * sin))
            for b, z in enumerate(dft(y, 1)):
                re, im = times(z, turn(b * (q + SHIFT) / blocks))
                mid[b, q, 0] = re
                mid[b, q, 1] = im

    def put(row, re, im):
        rows = pl.ds(row, re.shape[0])
        for lane, x in ((left, re), (right, im)):
            top = x.astype(BF16)
            high[rows, lane] = top
            low[rows, lane] = (x - top.astype(F32)).astype(BF16)

    def product(rows, table):
        a, b = high[rows, :], low[rows, :]
        dot = functools.partial(jnp.dot, preferred_element_type=F32)
        return dot(a, table[0]) + dot(b, table[0]) + dot(a, table[1])

    @pl.loop(0, nc)
    def _(s):
        pltpu.make_async_copy(frecv.at[s], frecv.at[s], filt_recv.at[s]).wait()

    for i in (3, 4, 7):
        loads[i].wait()

    @pl.loop(0, parts)
    def _(part):
        outer_forward(frecv, part)
        for qs in groups:
            inner_forward(qs)
            fspec[part, group_rows(qs), :] = product(group_rows(qs), fwd)

    def conv_slice(group, p):
        if isinstance(group, int) and group >= parts:
            return pl.ds(pl.multiple_of(p * per, PART), per), pl.ds((group - parts + 1) * LANES, LANES)
        return pl.ds(pl.multiple_of(p * per + group * PART, PART), PART), left

    def conv_copy(group, p):
        src = csend.at[p, conv_slice(group, 0)[0], conv_slice(group, 0)[1]]
        return remote(
            src, crecv.at[conv_slice(group, me)], conv_send.at[group, p], conv_recv.at[group, me], {CTX: p}
        )

    def send_conv(group):
        @pl.loop(0, nc - 1)
        def _(j):
            conv_copy(group, partner(j, me, nc)).start()

        pltpu.make_async_copy(
            csend.at[me, conv_slice(group, 0)[0], conv_slice(group, 0)[1]],
            crecv.at[conv_slice(group, me)],
            conv_recv.at[group, me],
        ).start()

    @pl.loop(0, parts)
    def _(part):
        rows16 = pl.ds(pl.multiple_of(part * PART, PART), PART)

        @pl.loop(0, nc)
        def _(s):
            slot = srecv.at[s, rows16, :]
            pltpu.make_async_copy(slot, slot, sig_recv.at[part, s]).wait()

        outer_forward(srecv, part)

        for qs in groups:
            rows = group_rows(qs)
            inner_forward(qs)
            spec = product(rows, fwd)
            re, im = spec[:, :LANES], spec[:, LANES:]
            fre, fim = fspec[part, rows, left], fspec[part, rows, right]
            put(row_at(qs[0], 0), re * fre - im * fim, re * fim + im * fre)
            dspec[rows, :] = product(rows, bwd)
            inner_backward(qs)

        for b in range(INNER):
            lane = pl.ds(b % halves * LANES, LANES)
            y = [(mid[b, q, 0], mid[b, q, 1]) for q in range(outer)]
            for a, z in enumerate(dft(y, 1)):
                csend[step_s * a + b // halves, rows16, lane] = real_part_times(
                    z, turn(a * SHIFT / outer)
                ).astype(BF16)

        send_conv(part)

    for half in range(1, halves):
        send_conv(parts + half - 1)

    def gate(chunk):
        rows = rows_of(chunk)
        sources = LANES // per

        @pl.loop(0, columns)
        def _(i):
            block = partner(i, me // sources, columns)
            for n in range(sources):
                for group in range(parts) if chunk == 0 else [parts + chunk - 1]:
                    slot = crecv.at[conv_slice(group, block * sources + n)]
                    pltpu.make_async_copy(slot, slot, conv_recv.at[group, block * sources + n]).wait()
            lane = pl.ds(pl.multiple_of(block * LANES, LANES), LANES)
            conv = crecv[lane, rows].astype(F32).T
            gated[rows, lane] = (
                qfeat[rows, lane] * (conv + skip[:, lane] * mixed[rows, lane].astype(F32))
            ).astype(BF16)

    def rows_of(chunk):
        return pl.ds(chunk * LANES, LANES)

    ring_at, pair_at = mt % RING, mt // RING
    across = {TEN: (1 - pair_at) * RING + ring_at}

    def term(chunk, pair, ring):
        column = pl.multiple_of((pair * RING + ring) * share, LANES)
        return jnp.dot(gated[rows_of(chunk), :], wbuf[:, pl.ds(column, share)], preferred_element_type=F32)

    upper, lower = pl.ds(0, PIECE), pl.ds(PIECE, PIECE)
    further = (2, 1, 3)

    def ring_device(d):
        return {TEN: pair_at * RING + (ring_at + d) % RING}

    def message(kind, c, d):
        src, dst, device = {
            "far": lambda: (xsend.at[c, 0, d], xrecv.at[c, 0, d], ring_device(d)),
            "near": lambda: (xsend.at[c, 1, d], xrecv.at[c, 1, d], ring_device(d)),
            "pair": lambda: (ysend.at[c, d], yrecv.at[c, d], across),
            "then_ring": lambda: (yxsend.at[c, d], yxrecv.at[c, d], ring_device(d)),
            "then_pair": lambda: (xysend.at[c], xyrecv.at[c], across),
        }[kind]()
        k = ("far", "near", "pair", "then_ring", "then_pair").index(kind)
        return remote(src, dst, red_send.at[k, c, d], red_recv.at[k, c, d], device)

    messages = [
        (kind, d)
        for kind, ds in (
            ("far", further),
            ("near", further),
            ("pair", (0, 1, 2, 3)),
            ("then_ring", further),
            ("then_pair", (0,)),
        )
        for d in ds
    ]

    def start_sums(c):
        for d in (*further, 0):
            t = term(c, 1 - pair_at, (ring_at + d) % RING)
            ysend[c, d] = t[PIECE:].astype(BF16)
            message("pair", c, d).start()
            if d:
                xsend[c, 0, d] = t[:PIECE].astype(BF16)
                message("far", c, d).start()
            else:
                xown[c, 0] = t[:PIECE]
        for d in (*further, 0):
            t = term(c, pair_at, (ring_at + d) % RING)
            yown[c, d] = t[PIECE:]
            if d:
                xsend[c, 1, d] = t[:PIECE].astype(BF16)
                message("near", c, d).start()
            else:
                xown[c, 1] = t[:PIECE]

    def turn_corner(c):
        for d in further:
            message("far", c, d).wait_recv()
        s = xown[c, 0]
        for d in further:
            s = s + xrecv[c, 0, d].astype(F32)
        xysend[c] = s.astype(BF16)
        message("then_pair", c, 0).start()
        for d in further:
            message("pair", c, d).wait_recv()
            yxsend[c, d] = (yown[c, d] + yrecv[c, d].astype(F32)).astype(BF16)
            message("then_ring", c, d).start()

    def row_copy(chunk, p):
        return remote(
            ssend.at[chunk], srow.at[chunk, mt], row_send.at[chunk, p], row_recv.at[chunk, mt], {TEN: p}
        )

    def end_sums(c):
        squares = []

        def finish(rows, parts_of):
            square = jnp.zeros((PIECE, LANES), F32)
            for i in range(share // LANES):
                lane = pl.ds(i * LANES, LANES)
                s = parts_of[0][:, lane]
                for ref in parts_of[1:]:
                    s = s + ref[:, lane].astype(F32)
                mine[c, rows, lane] = s
                square = square + s * s
            squares.append(jnp.sum(square, axis=1, keepdims=True))

        for d in further:
            message("near", c, d).wait_recv()
        message("then_pair", c, 0).wait_recv()
        finish(upper, [xown.at[c, 1], *(xrecv.at[c, 1, d] for d in further), xyrecv.at[c]])
        message("pair", c, 0).wait_recv()
        for d in further:
            message("then_ring", c, d).wait_recv()
        finish(lower, [yown.at[c, 0], yrecv.at[c, 0], *(yxrecv.at[c, d] for d in further)])
        sums = jnp.concatenate(squares, axis=0)
        ssend[c] = jnp.broadcast_to(sums, (LANES, LANES)).T[:8]
        srow[c, mt] = ssend[c]

        @pl.loop(0, nt - 1, unroll=True)
        def _(j):
            row_copy(c, partner(j, mt, nt)).start()

    def normalize(c):
        @pl.loop(0, nt - 1)
        def _(j):
            p = partner(j, mt, nt)
            slot = srow.at[c, p]
            pltpu.make_async_copy(slot, slot, row_recv.at[c, p]).wait()

        s = srow[c, 0]
        for g in range(1, nt):
            s = s + srow[c, g]
        scale = lax.rsqrt(s * (1.0 / (share * nt)) + 1e-06)
        scale = jnp.broadcast_to(scale[:1], (LANES, LANES)).T
        for i in range(share // LANES):
            lane = pl.ds(i * LANES, LANES)
            out[rows_of(c), lane] = (mine[c, :, lane] * scale * gain[:, lane]).astype(BF16)

    loads[8].wait()
    gate(0)
    loads[5].wait()
    start_sums(0)
    gate(1)
    start_sums(1)
    turn_corner(0)
    turn_corner(1)
    end_sums(0)
    end_sums(1)
    loads[9].wait()
    normalize(0)
    normalize(1)

    settle(9)


def per_device(
    query_proj, key_proj, value_proj, short_taps, long_filter, skip_weight, out_weight, norm_gain
):
    nc, nt = lax.axis_size(CTX), lax.axis_size(TEN)
    tokens, width = query_proj.shape
    features = out_weight.shape[1]
    share = features // nt
    per = width // nc
    parts = per // PART
    blocks = nc * (tokens // LANES)
    outer = blocks // INNER
    halves = tokens // LANES
    fwd, bwd, twist = (jnp.asarray(x) for x in tables(blocks))
    anywhere = pl.BlockSpec(memory_space=pl.ANY)
    vmem = pl.BlockSpec(memory_space=pltpu.VMEM)
    dma = pltpu.SemaphoreType.DMA
    return pl.pallas_call(
        functools.partial(kernel, nc, nt),
        out_shape=pltpu.VMEM((tokens, share), BF16),
        in_specs=[anywhere] * 11,
        out_specs=vmem,
        scratch_shapes=[
            pltpu.VMEM(short_taps.shape, F32),
            pltpu.VMEM((1, width), F32),
            pltpu.VMEM((1, share), F32),
            pltpu.VMEM(twist.shape, F32),
            pltpu.VMEM((tokens + HALO, width), BF16),
            pltpu.VMEM((tokens + HALO, width), BF16),
            pltpu.VMEM((tokens + HALO, width), BF16),
            pltpu.VMEM((width, features), BF16),
            pltpu.VMEM(fwd.shape, BF16),
            pltpu.VMEM(bwd.shape, BF16),
            pltpu.VMEM((tokens, width), F32),
            pltpu.VMEM((tokens, width), BF16),
            pltpu.VMEM((width, tokens), BF16),
            pltpu.VMEM((nc, per, tokens), BF16),
            pltpu.VMEM((nc, per, tokens), BF16),
            pltpu.VMEM((nc, per, tokens), BF16),
            pltpu.VMEM((width, tokens), BF16),
            pltpu.VMEM((INNER, outer, 2, PART, LANES), F32),
            pltpu.VMEM((blocks * PART, 2 * LANES), BF16),
            pltpu.VMEM((blocks * PART, 2 * LANES), BF16),
            pltpu.VMEM((parts, blocks * PART, 2 * LANES), F32),
            pltpu.VMEM((blocks * PART, 2 * LANES), F32),
            pltpu.VMEM((tokens, width), BF16),
            pltpu.VMEM((halves, 2, RING, PIECE, share), BF16),
            pltpu.VMEM((halves, 2, RING, PIECE, share), BF16),
            pltpu.VMEM((halves, 2, PIECE, share), F32),
            pltpu.VMEM((halves, RING, PIECE, share), BF16),
            pltpu.VMEM((halves, RING, PIECE, share), BF16),
            pltpu.VMEM((halves, RING, PIECE, share), F32),
            pltpu.VMEM((halves, RING, PIECE, share), BF16),
            pltpu.VMEM((halves, RING, PIECE, share), BF16),
            pltpu.VMEM((halves, PIECE, share), BF16),
            pltpu.VMEM((halves, PIECE, share), BF16),
            pltpu.VMEM((halves, LANES, share), F32),
            pltpu.VMEM((halves, 8, LANES), F32),
            pltpu.VMEM((halves, nt, 8, LANES), F32),
            dma((10,)),
            dma((3,)),
            dma((3,)),
            dma((nc,)),
            dma((nc,)),
            dma((parts, nc)),
            dma((parts, nc)),
            dma((parts + halves - 1, nc)),
            dma((parts + halves - 1, nc)),
            dma((5, halves, RING)),
            dma((5, halves, RING)),
            dma((halves, nt)),
            dma((halves, nt)),
        ],
        compiler_params=pltpu.CompilerParams(
            collective_id=0, has_side_effects=True, vmem_limit_bytes=56 * 1024 * 1024
        ),
    )(
        query_proj,
        key_proj,
        value_proj,
        long_filter,
        out_weight,
        fwd,
        bwd,
        short_taps,
        skip_weight.reshape(1, width),
        norm_gain.reshape(1, share),
        twist,
    )


def solution(mesh):
    placed = (
        P(CTX, TEN),
        P(CTX, TEN),
        P(CTX, TEN),
        P(None, None, TEN),
        P(TEN, CTX),
        P(TEN),
        P(TEN, None),
        P(TEN),
    )
    return jax.shard_map(
        per_device, mesh=mesh, in_specs=placed, out_specs=P(CTX, TEN), check_vma=False
    )
```

```python
import functools
import math

import jax
import jax.numpy as jnp
import ml_dtypes
import numpy as np
from jax import lax
from jax.experimental import pallas as pl
from jax.experimental.pallas import tpu as pltpu
from jax.sharding import PartitionSpec as P

F32, BF16 = jnp.float32, jnp.bfloat16
CTX, TEN = "context", "tensor"
HALO = 16
LANES = 128
PART = 16
SHIFT = 0.25
GROUP = 2
INNER = 8
RING = 4
PIECE = 48


def times(z, c):
    re, im = z
    cr, ci = float(c.real), float(c.imag)
    cr = 0.0 if abs(cr) < 1e-12 else cr
    ci = 0.0 if abs(ci) < 1e-12 else ci
    if im is None:
        if ci == 0.0:
            return (re if cr == 1.0 else re * cr, None)
        return (re * cr, re * ci)
    if ci == 0.0:
        return z if cr == 1.0 else (re * cr, im * cr)
    if cr == 0.0:
        return (im * -ci, re * ci)
    if abs(abs(cr) - abs(ci)) < 1e-12:
        plus, minus = re + im, re - im
        if (cr > 0) == (ci > 0):
            return (minus * cr, plus * cr)
        return (plus * cr, minus * ci)
    return (re * cr - im * ci, re * ci + im * cr)


def real_part_times(z, c):
    re, im = z
    cr, ci = float(c.real), float(c.imag)
    if im is None or abs(ci) < 1e-12:
        return re if cr == 1.0 else re * cr
    return re * cr - im * ci


def plus_minus(a, b):
    (ar, ai), (br, bi) = a, b
    if ai is None and bi is None:
        return (ar + br, None), (ar - br, None)
    if ai is None:
        return (ar + br, bi), (ar - br, -bi)
    if bi is None:
        return (ar + br, ai), (ar - br, ai)
    return (ar + br, ai + bi), (ar - br, ai - bi)


def dft(x, sign):
    n = len(x)
    if n == 1:
        return list(x)
    even, odd = dft(x[0::2], sign), dft(x[1::2], sign)
    low, high = [], []
    for k in range(n // 2):
        e, o = even[k], odd[k]
        if 4 * k == n and e[1] is not None and o[1] is not None:
            s = float(sign)
            one = (e[0] - o[1], e[1] + o[0])
            two = (e[0] + o[1], e[1] - o[0])
            a, b = (one, two) if s > 0 else (two, one)
        else:
            a, b = plus_minus(e, times(o, turn(sign * k / n)))
        low.append(a)
        high.append(b)
    return low + high


def turn(x):
    return complex(math.cos(2 * math.pi * x), math.sin(2 * math.pi * x))


def im_of(z):
    return jnp.zeros_like(z[0]) if z[1] is None else z[1]


def split_table(x):
    high = x.astype(ml_dtypes.bfloat16)
    low = (x - high.astype(np.float64)).astype(ml_dtypes.bfloat16)
    return np.stack([high, low])


def tables(blocks):
    length = blocks * LANES
    t = np.arange(LANES)
    phase = np.outer(t, t) % LANES / LANES
    forward = np.exp(-2j * np.pi * phase)
    backward = np.exp(2j * np.pi * phase) / length
    pair = lambda w: np.block([[w.real, w.imag], [-w.imag, w.real]])
    twist = np.exp(-2j * np.pi * np.outer(np.arange(blocks) + SHIFT, t) / length)
    return (
        split_table(pair(forward)),
        split_table(pair(backward)),
        np.stack([twist.real, twist.imag]).astype(np.float32),
    )


def kernel(
    nc,
    nt,
    q_hbm,
    k_hbm,
    v_hbm,
    filt_hbm,
    w_hbm,
    fwd_hbm,
    bwd_hbm,
    taps_hbm,
    skip_hbm,
    gain_hbm,
    twist_hbm,
    out,
    taps,
    skip,
    gain,
    twist,
    qbuf,
    kbuf,
    vbuf,
    wbuf,
    fwd,
    bwd,
    qfeat,
    mixed,
    mixed_t,
    frecv,
    srecv,
    csend,
    crecv,
    mid,
    high,
    low,
    fspec,
    dspec,
    gated,
    xsend,
    xrecv,
    xown,
    ysend,
    yrecv,
    yown,
    yxsend,
    yxrecv,
    xysend,
    xyrecv,
    mine,
    ssend,
    srow,
    load_sem,
    halo_send,
    halo_recv,
    filt_send,
    filt_recv,
    sig_send,
    sig_recv,
    conv_send,
    conv_recv,
    red_send,
    red_recv,
    row_send,
    row_recv,
):
    me, mt = lax.axis_index(CTX), lax.axis_index(TEN)
    tokens, width = q_hbm.shape
    per = width // nc
    parts = per // PART
    halves = tokens // LANES
    blocks = nc * halves
    outer = blocks // INNER
    step_s = INNER // halves
    share = out.shape[1]

    def partner(j, mine, n):
        step = n // 2 - (j + 1) // 2
        odd = j % 2
        return (mine + step * (1 - odd) + (n - step) * odd) % n

    def remote(src, dst, send, recv, device):
        return pltpu.make_async_remote_copy(
            src_ref=src,
            dst_ref=dst,
            send_sem=send,
            recv_sem=recv,
            device_id=device,
            device_id_type=pl.DeviceIdType.MESH,
        )

    barrier = pltpu.get_barrier_semaphore()

    @pl.loop(0, nc - 1, unroll=True)
    def _(j):
        pl.semaphore_signal(barrier, inc=1, device_id={CTX: partner(j, me, nc)})

    @pl.loop(0, nt - 1, unroll=True)
    def _(j):
        pl.semaphore_signal(barrier, inc=1, device_id={TEN: partner(j, mt, nt)})

    body = pl.ds(HALO, tokens)
    loads = [
        pltpu.make_async_copy(src, dst, load_sem.at[i])
        for i, (src, dst) in enumerate(
            (
                (k_hbm, kbuf.at[body, :]),
                (v_hbm, vbuf.at[body, :]),
                (q_hbm, qbuf.at[body, :]),
                (fwd_hbm, fwd),
                (bwd_hbm, bwd),
                (w_hbm, wbuf),
                (taps_hbm, taps),
                (twist_hbm, twist),
                (skip_hbm, skip),
                (gain_hbm, gain),
            )
        )
    ]
    for i in (0, 1, 6):
        loads[i].start()

    pl.semaphore_wait(barrier, nc - 1 + nt - 1)

    def settle_inputs():
        @pl.when(me < nc - 1)
        def _():
            for copy in halos:
                copy.wait_send()

        @pl.loop(0, nc - 1)
        def _(j):
            p = partner(j, me, nc)
            filter_copy(p).wait_send()
            for part in range(parts):
                signal_copy(part, p).wait_send()

    def settle_conv():
        @pl.loop(0, nc - 1)
        def _(j):
            for group in range(parts + halves - 1):
                conv_copy(group, partner(j, me, nc)).wait_send()

    def settle_sums():
        for c in range(halves):
            for kind, d in messages:
                message(kind, c, d).wait_send()

    def settle_rows():
        @pl.loop(0, nt - 1)
        def _(j):
            for c in range(halves):
                row_copy(c, partner(j, mt, nt)).wait_send()

    halos = [
        remote(
            src.at[pl.ds(tokens - HALO, HALO), :],
            dst.at[pl.ds(0, HALO), :],
            halo_send.at[i],
            halo_recv.at[i],
            {CTX: (me + 1) % nc},
        )
        for i, (src, dst) in enumerate(((k_hbm, kbuf), (v_hbm, vbuf), (q_hbm, qbuf)))
    ]

    @pl.when(me < nc - 1)
    def _():
        for copy in halos:
            copy.start()

    @pl.when(me == 0)
    def _():
        for buf in (kbuf, vbuf, qbuf):
            buf[pl.ds(0, HALO), :] = jnp.zeros((HALO, width), BF16)

    def filter_copy(p):
        return remote(
            filt_hbm.at[pl.ds(pl.multiple_of(p * per, PART), per), :],
            frecv.at[me],
            filt_send.at[p],
            filt_recv.at[me],
            {CTX: p},
        )

    @pl.loop(0, nc - 1, unroll=True)
    def _(j):
        filter_copy(partner(j, me, nc)).start()

    own_filter = pltpu.make_async_copy(
        filt_hbm.at[pl.ds(pl.multiple_of(me * per, PART), per), :], frecv.at[me], filt_recv.at[me]
    )
    own_filter.start()
    for i in (2, 7, 3, 4, 8, 9, 5):
        loads[i].start()

    def feature(buf, r, row, lane):
        wide = buf[pl.ds(row, LANES + HALO), lane].astype(F32)[HALO - 8 :]
        one = pltpu.roll(wide, 1, 0)[8:]
        two = pltpu.roll(wide, 2, 0)[8:]
        return (
            taps[r, pl.ds(0, 1), lane] * wide[8:]
            + taps[r, pl.ds(1, 1), lane] * one
            + taps[r, pl.ds(2, 1), lane] * two
        )

    columns = width // LANES

    def place(i):
        row = pl.multiple_of(i // columns * LANES, LANES)
        col = pl.multiple_of(i % columns * LANES, LANES)
        return row, col

    for i in (6, 0, 1):
        loads[i].wait()

    @pl.when(me > 0)
    def _():
        for i in (0, 1):
            halos[i].wait_recv()

    @pl.loop(0, halves * columns)
    def _(i):
        row, col = place(i)
        lane = pl.ds(col, LANES)
        product = feature(kbuf, 1, row, lane) * feature(vbuf, 2, row, lane)
        mixed[pl.ds(row, LANES), lane] = product.astype(BF16)
        mixed_t[pl.ds(col, LANES), pl.ds(row, LANES)] = product.T.astype(BF16)

    def signal_copy(part, p):
        return remote(
            mixed_t.at[pl.ds(pl.multiple_of(p * per + part * PART, PART), PART), :],
            srecv.at[me, pl.ds(part * PART, PART), :],
            sig_send.at[part, p],
            sig_recv.at[part, me],
            {CTX: p},
        )

    for part in range(parts):

        @pl.loop(0, nc - 1, unroll=True)
        def _(j):
            signal_copy(part, partner(j, me, nc)).start()

        pltpu.make_async_copy(
            mixed_t.at[pl.ds(pl.multiple_of(me * per + part * PART, PART), PART), :],
            srecv.at[me, pl.ds(part * PART, PART), :],
            sig_recv.at[part, me],
        ).start()

    loads[2].wait()

    @pl.when(me > 0)
    def _():
        halos[2].wait_recv()

    @pl.loop(0, halves * columns)
    def _(i):
        row, col = place(i)
        lane = pl.ds(col, LANES)
        qfeat[pl.ds(row, LANES), lane] = feature(qbuf, 0, row, lane)

    def row_at(q, r):
        return (q * INNER + r) * PART

    together = min(GROUP, outer)
    groups = [range(q, q + together) for q in range(0, outer, together)]

    def group_rows(qs):
        return pl.ds(row_at(qs[0], 0), together * INNER * PART)

    left, right = pl.ds(0, LANES), pl.ds(LANES, LANES)

    def outer_forward(recv, part):
        rows = pl.ds(pl.multiple_of(part * PART, PART), PART)
        for b in range(INNER):
            lane = pl.ds(b % halves * LANES, LANES)
            x = [
                times((recv[step_s * a + b // halves, rows, lane].astype(F32), None), turn(-a * SHIFT / outer))
                for a in range(outer)
            ]
            for q, z in enumerate(dft(x, -1)):
                re, im = times(z, turn(-b * (q + SHIFT) / blocks))
                mid[b, q, 0] = re
                mid[b, q, 1] = jnp.zeros_like(re) if im is None else im

    def inner_forward(qs):
        for q in qs:
            y = [(mid[b, q, 0], mid[b, q, 1]) for b in range(INNER)]
            for r, (re, im) in enumerate(dft(y, -1)):
                k1 = q + outer * r
                cos, sin = twist[0, pl.ds(k1, 1), :], twist[1, pl.ds(k1, 1), :]
                put(row_at(q, r), re * cos - im * sin, im * cos + re * sin)

    def inner_backward(qs):
        for q in qs:
            y = []
            for r in range(INNER):
                k1, rows = q + outer * r, pl.ds(row_at(q, r), PART)
                cos, sin = twist[0, pl.ds(k1, 1), :], twist[1, pl.ds(k1, 1), :]
                re, im = dspec[rows, left], dspec[rows, right]
                y.append((re * cos + im * sin, im * cos - re * sin))
            for b, z in enumerate(dft(y, 1)):
                re, im = times(z, turn(b * (q + SHIFT) / blocks))
                mid[b, q, 0] = re
                mid[b, q, 1] = im

    def put(row, re, im):
        rows = pl.ds(row, re.shape[0])
        for lane, x in ((left, re), (right, im)):
            top = x.astype(BF16)
            high[rows, lane] = top
            low[rows, lane] = (x - top.astype(F32)).astype(BF16)

    def product(rows, table):
        a, b = high[rows, :], low[rows, :]
        dot = functools.partial(jnp.dot, preferred_element_type=F32)
        return dot(a, table[0]) + dot(b, table[0]) + dot(a, table[1])

    @pl.loop(0, nc)
    def _(s):
        pltpu.make_async_copy(frecv.at[s], frecv.at[s], filt_recv.at[s]).wait()

    for i in (3, 4, 7):
        loads[i].wait()

    @pl.loop(0, parts)
    def _(part):
        outer_forward(frecv, part)
        for qs in groups:
            inner_forward(qs)
            fspec[part, group_rows(qs), :] = product(group_rows(qs), fwd)

    def conv_slice(group, p):
        if isinstance(group, int) and group >= parts:
            return pl.ds(pl.multiple_of(p * per, PART), per), pl.ds((group - parts + 1) * LANES, LANES)
        return pl.ds(pl.multiple_of(p * per + group * PART, PART), PART), left

    def conv_copy(group, p):
        src = csend.at[p, conv_slice(group, 0)[0], conv_slice(group, 0)[1]]
        return remote(
            src, crecv.at[conv_slice(group, me)], conv_send.at[group, p], conv_recv.at[group, me], {CTX: p}
        )

    def send_conv(group):
        @pl.loop(0, nc - 1)
        def _(j):
            conv_copy(group, partner(j, me, nc)).start()

        pltpu.make_async_copy(
            csend.at[me, conv_slice(group, 0)[0], conv_slice(group, 0)[1]],
            crecv.at[conv_slice(group, me)],
            conv_recv.at[group, me],
        ).start()

    @pl.loop(0, parts)
    def _(part):
        rows16 = pl.ds(pl.multiple_of(part * PART, PART), PART)

        @pl.loop(0, nc)
        def _(s):
            slot = srecv.at[s, rows16, :]
            pltpu.make_async_copy(slot, slot, sig_recv.at[part, s]).wait()

        outer_forward(srecv, part)

        for qs in groups:
            rows = group_rows(qs)
            inner_forward(qs)
            spec = product(rows, fwd)
            re, im = spec[:, :LANES], spec[:, LANES:]
            fre, fim = fspec[part, rows, left], fspec[part, rows, right]
            put(row_at(qs[0], 0), re * fre - im * fim, re * fim + im * fre)
            dspec[rows, :] = product(rows, bwd)
            inner_backward(qs)

        for b in range(INNER):
            lane = pl.ds(b % halves * LANES, LANES)
            y = [(mid[b, q, 0], mid[b, q, 1]) for q in range(outer)]
            for a, z in enumerate(dft(y, 1)):
                csend[step_s * a + b // halves, rows16, lane] = real_part_times(
                    z, turn(a * SHIFT / outer)
                ).astype(BF16)

        send_conv(part)

    for half in range(1, halves):
        send_conv(parts + half - 1)

    def gate(chunk):
        rows = rows_of(chunk)
        sources = LANES // per

        @pl.loop(0, columns)
        def _(i):
            block = partner(i, me // sources, columns)
            for n in range(sources):
                for group in range(parts) if chunk == 0 else [parts + chunk - 1]:
                    slot = crecv.at[conv_slice(group, block * sources + n)]
                    pltpu.make_async_copy(slot, slot, conv_recv.at[group, block * sources + n]).wait()
            lane = pl.ds(pl.multiple_of(block * LANES, LANES), LANES)
            conv = crecv[lane, rows].astype(F32).T
            gated[rows, lane] = (
                qfeat[rows, lane] * (conv + skip[:, lane] * mixed[rows, lane].astype(F32))
            ).astype(BF16)

    def rows_of(chunk):
        return pl.ds(chunk * LANES, LANES)

    ring_at, pair_at = mt % RING, mt // RING
    across = {TEN: (1 - pair_at) * RING + ring_at}

    def term(chunk, pair, ring):
        column = pl.multiple_of((pair * RING + ring) * share, LANES)
        return jnp.dot(gated[rows_of(chunk), :], wbuf[:, pl.ds(column, share)], preferred_element_type=F32)

    upper, lower = pl.ds(0, PIECE), pl.ds(PIECE, LANES - PIECE)
    further = (2, 1, 3)

    def ring_device(d):
        return {TEN: pair_at * RING + (ring_at + d) % RING}

    def message(kind, c, d):
        src, dst, device = {
            "far": lambda: (xsend.at[c, 0, d], xrecv.at[c, 0, d], ring_device(d)),
            "near": lambda: (xsend.at[c, 1, d], xrecv.at[c, 1, d], ring_device(d)),
            "pair": lambda: (ysend.at[c, d], yrecv.at[c, d], across),
            "then_ring": lambda: (yxsend.at[c, d], yxrecv.at[c, d], ring_device(d)),
            "then_pair": lambda: (xysend.at[c], xyrecv.at[c], across),
        }[kind]()
        k = ("far", "near", "pair", "then_ring", "then_pair").index(kind)
        return remote(src, dst, red_send.at[k, c, d], red_recv.at[k, c, d], device)

    messages = [
        (kind, d)
        for kind, ds in (
            ("far", further),
            ("near", further),
            ("pair", (0, 1, 2, 3)),
            ("then_ring", further),
            ("then_pair", (0,)),
        )
        for d in ds
    ]

    def start_across(c):
        for d in (*further, 0):
            t = term(c, 1 - pair_at, (ring_at + d) % RING)
            ysend[c, d] = t[PIECE:].astype(BF16)
            message("pair", c, d).start()
            if d:
                xsend[c, 0, d] = t[:PIECE].astype(BF16)
                message("far", c, d).start()
            else:
                xown[c, 0] = t[:PIECE]

    def start_along(c):
        for d in (*further, 0):
            t = term(c, pair_at, (ring_at + d) % RING)
            yown[c, d] = t[PIECE:]
            if d:
                xsend[c, 1, d] = t[:PIECE].astype(BF16)
                message("near", c, d).start()
            else:
                xown[c, 1] = t[:PIECE]

    def turn_corner(c):
        for d in further:
            message("far", c, d).wait_recv()
        s = xown[c, 0]
        for d in further:
            s = s + xrecv[c, 0, d].astype(F32)
        xysend[c] = s.astype(BF16)
        message("then_pair", c, 0).start()
        for d in further:
            message("pair", c, d).wait_recv()
            yxsend[c, d] = (yown[c, d] + yrecv[c, d].astype(F32)).astype(BF16)
            message("then_ring", c, d).start()

    def row_copy(chunk, p):
        return remote(
            ssend.at[chunk], srow.at[chunk, mt], row_send.at[chunk, p], row_recv.at[chunk, mt], {TEN: p}
        )

    def end_sums(c):
        squares = []

        def finish(rows, parts_of):
            square = jnp.zeros((rows.size, LANES), F32)
            for i in range(share // LANES):
                lane = pl.ds(i * LANES, LANES)
                s = parts_of[0][:, lane]
                for ref in parts_of[1:]:
                    s = s + ref[:, lane].astype(F32)
                mine[c, rows, lane] = s
                square = square + s * s
            squares.append(jnp.sum(square, axis=1, keepdims=True))

        for d in further:
            message("near", c, d).wait_recv()
        message("then_pair", c, 0).wait_recv()
        finish(upper, [xown.at[c, 1], *(xrecv.at[c, 1, d] for d in further), xyrecv.at[c]])
        message("pair", c, 0).wait_recv()
        for d in further:
            message("then_ring", c, d).wait_recv()
        finish(lower, [yown.at[c, 0], yrecv.at[c, 0], *(yxrecv.at[c, d] for d in further)])
        sums = jnp.concatenate(squares, axis=0)
        ssend[c] = jnp.broadcast_to(sums, (LANES, LANES)).T[:8]
        srow[c, mt] = ssend[c]

        @pl.loop(0, nt - 1, unroll=True)
        def _(j):
            row_copy(c, partner(j, mt, nt)).start()

    def normalize(c):
        @pl.loop(0, nt - 1)
        def _(j):
            p = partner(j, mt, nt)
            slot = srow.at[c, p]
            pltpu.make_async_copy(slot, slot, row_recv.at[c, p]).wait()

        s = srow[c, 0]
        for g in range(1, nt):
            s = s + srow[c, g]
        scale = lax.rsqrt(s * (1.0 / (share * nt)) + 1e-06)
        scale = jnp.broadcast_to(scale[:1], (LANES, LANES)).T
        for i in range(share // LANES):
            lane = pl.ds(i * LANES, LANES)
            out[rows_of(c), lane] = (mine[c, :, lane] * scale * gain[:, lane]).astype(BF16)

    settle_inputs()
    loads[8].wait()
    gate(0)
    loads[5].wait()
    start_across(0)
    start_along(0)
    gate(1)
    start_across(1)
    turn_corner(0)
    start_along(1)
    turn_corner(1)
    settle_conv()
    end_sums(0)
    end_sums(1)
    settle_sums()
    loads[9].wait()
    normalize(0)
    normalize(1)

    settle_rows()


def per_device(
    query_proj, key_proj, value_proj, short_taps, long_filter, skip_weight, out_weight, norm_gain
):
    nc, nt = lax.axis_size(CTX), lax.axis_size(TEN)
    tokens, width = query_proj.shape
    features = out_weight.shape[1]
    share = features // nt
    per = width // nc
    parts = per // PART
    blocks = nc * (tokens // LANES)
    outer = blocks // INNER
    halves = tokens // LANES
    fwd, bwd, twist = (jnp.asarray(x) for x in tables(blocks))
    anywhere = pl.BlockSpec(memory_space=pl.ANY)
    vmem = pl.BlockSpec(memory_space=pltpu.VMEM)
    dma = pltpu.SemaphoreType.DMA
    return pl.pallas_call(
        functools.partial(kernel, nc, nt),
        out_shape=pltpu.VMEM((tokens, share), BF16),
        in_specs=[anywhere] * 11,
        out_specs=vmem,
        scratch_shapes=[
            pltpu.VMEM(short_taps.shape, F32),
            pltpu.VMEM((1, width), F32),
            pltpu.VMEM((1, share), F32),
            pltpu.VMEM(twist.shape, F32),
            pltpu.VMEM((tokens + HALO, width), BF16),
            pltpu.VMEM((tokens + HALO, width), BF16),
            pltpu.VMEM((tokens + HALO, width), BF16),
            pltpu.VMEM((width, features), BF16),
            pltpu.VMEM(fwd.shape, BF16),
            pltpu.VMEM(bwd.shape, BF16),
            pltpu.VMEM((tokens, width), F32),
            pltpu.VMEM((tokens, width), BF16),
            pltpu.VMEM((width, tokens), BF16),
            pltpu.VMEM((nc, per, tokens), BF16),
            pltpu.VMEM((nc, per, tokens), BF16),
            pltpu.VMEM((nc, per, tokens), BF16),
            pltpu.VMEM((width, tokens), BF16),
            pltpu.VMEM((INNER, outer, 2, PART, LANES), F32),
            pltpu.VMEM((blocks * PART, 2 * LANES), BF16),
            pltpu.VMEM((blocks * PART, 2 * LANES), BF16),
            pltpu.VMEM((parts, blocks * PART, 2 * LANES), F32),
            pltpu.VMEM((blocks * PART, 2 * LANES), F32),
            pltpu.VMEM((tokens, width), BF16),
            pltpu.VMEM((halves, 2, RING, PIECE, share), BF16),
            pltpu.VMEM((halves, 2, RING, PIECE, share), BF16),
            pltpu.VMEM((halves, 2, PIECE, share), F32),
            pltpu.VMEM((halves, RING, LANES - PIECE, share), BF16),
            pltpu.VMEM((halves, RING, LANES - PIECE, share), BF16),
            pltpu.VMEM((halves, RING, LANES - PIECE, share), F32),
            pltpu.VMEM((halves, RING, LANES - PIECE, share), BF16),
            pltpu.VMEM((halves, RING, LANES - PIECE, share), BF16),
            pltpu.VMEM((halves, PIECE, share), BF16),
            pltpu.VMEM((halves, PIECE, share), BF16),
            pltpu.VMEM((halves, LANES, share), F32),
            pltpu.VMEM((halves, 8, LANES), F32),
            pltpu.VMEM((halves, nt, 8, LANES), F32),
            dma((10,)),
            dma((3,)),
            dma((3,)),
            dma((nc,)),
            dma((nc,)),
            dma((parts, nc)),
            dma((parts, nc)),
            dma((parts + halves - 1, nc)),
            dma((parts + halves - 1, nc)),
            dma((5, halves, RING)),
            dma((5, halves, RING)),
            dma((halves, nt)),
            dma((halves, nt)),
        ],
        compiler_params=pltpu.CompilerParams(
            collective_id=0, has_side_effects=True, vmem_limit_bytes=56 * 1024 * 1024
        ),
    )(
        query_proj,
        key_proj,
        value_proj,
        long_filter,
        out_weight,
        fwd,
        bwd,
        short_taps,
        skip_weight.reshape(1, width),
        norm_gain.reshape(1, share),
        twist,
    )


def solution(mesh):
    placed = (
        P(CTX, TEN),
        P(CTX, TEN),
        P(CTX, TEN),
        P(None, None, TEN),
        P(TEN, CTX),
        P(TEN),
        P(TEN, None),
        P(TEN),
    )
    return jax.shard_map(
        per_device, mesh=mesh, in_specs=placed, out_specs=P(CTX, TEN), check_vma=False
    )
```

```python
import functools
import math

import jax
import jax.numpy as jnp
import ml_dtypes
import numpy as np
from jax import lax
from jax.experimental import pallas as pl
from jax.experimental.pallas import tpu as pltpu
from jax.sharding import PartitionSpec as P

F32, BF16 = jnp.float32, jnp.bfloat16
CTX, TEN = "context", "tensor"
HALO = 16
LANES = 128
PART = 16
SHIFT = 0.25
GROUP = 2
INNER = 8
RING = 4
PIECE = 48


def times(z, c):
    re, im = z
    cr, ci = float(c.real), float(c.imag)
    cr = 0.0 if abs(cr) < 1e-12 else cr
    ci = 0.0 if abs(ci) < 1e-12 else ci
    if im is None:
        if ci == 0.0:
            return (re if cr == 1.0 else re * cr, None)
        return (re * cr, re * ci)
    if ci == 0.0:
        return z if cr == 1.0 else (re * cr, im * cr)
    if cr == 0.0:
        return (im * -ci, re * ci)
    if abs(abs(cr) - abs(ci)) < 1e-12:
        plus, minus = re + im, re - im
        if (cr > 0) == (ci > 0):
            return (minus * cr, plus * cr)
        return (plus * cr, minus * ci)
    return (re * cr - im * ci, re * ci + im * cr)


def real_part_times(z, c):
    re, im = z
    cr, ci = float(c.real), float(c.imag)
    if im is None or abs(ci) < 1e-12:
        return re if cr == 1.0 else re * cr
    return re * cr - im * ci


def plus_minus(a, b):
    (ar, ai), (br, bi) = a, b
    if ai is None and bi is None:
        return (ar + br, None), (ar - br, None)
    if ai is None:
        return (ar + br, bi), (ar - br, -bi)
    if bi is None:
        return (ar + br, ai), (ar - br, ai)
    return (ar + br, ai + bi), (ar - br, ai - bi)


def dft(x, sign):
    n = len(x)
    if n == 1:
        return list(x)
    even, odd = dft(x[0::2], sign), dft(x[1::2], sign)
    low, high = [], []
    for k in range(n // 2):
        e, o = even[k], odd[k]
        if 4 * k == n and e[1] is not None and o[1] is not None:
            s = float(sign)
            one = (e[0] - o[1], e[1] + o[0])
            two = (e[0] + o[1], e[1] - o[0])
            a, b = (one, two) if s > 0 else (two, one)
        else:
            a, b = plus_minus(e, times(o, turn(sign * k / n)))
        low.append(a)
        high.append(b)
    return low + high


def turn(x):
    return complex(math.cos(2 * math.pi * x), math.sin(2 * math.pi * x))


def im_of(z):
    return jnp.zeros_like(z[0]) if z[1] is None else z[1]


def split_table(x):
    high = x.astype(ml_dtypes.bfloat16)
    low = (x - high.astype(np.float64)).astype(ml_dtypes.bfloat16)
    return np.stack([high, low])


def tables(blocks):
    length = blocks * LANES
    t = np.arange(LANES)
    phase = np.outer(t, t) % LANES / LANES
    forward = np.exp(-2j * np.pi * phase)
    backward = np.exp(2j * np.pi * phase) / length
    pair = lambda w: np.block([[w.real, w.imag], [-w.imag, w.real]])
    twist = np.exp(-2j * np.pi * np.outer(np.arange(blocks) + SHIFT, t) / length)
    return (
        split_table(pair(forward)),
        split_table(pair(backward)),
        np.stack([twist.real, twist.imag]).astype(np.float32),
    )


def kernel(
    nc,
    nt,
    q_hbm,
    k_hbm,
    v_hbm,
    filt_hbm,
    w_hbm,
    fwd_hbm,
    bwd_hbm,
    taps_hbm,
    skip_hbm,
    gain_hbm,
    twist_hbm,
    out,
    taps,
    skip,
    gain,
    twist,
    qbuf,
    kbuf,
    vbuf,
    wbuf,
    fwd,
    bwd,
    qfeat,
    mixed,
    mixed_t,
    frecv,
    srecv,
    csend,
    crecv,
    mid,
    high,
    low,
    fspec,
    dspec,
    gated,
    xsend,
    xrecv,
    xown,
    ysend,
    yrecv,
    yown,
    yxsend,
    yxrecv,
    xysend,
    xyrecv,
    mine,
    ssend,
    srow,
    load_sem,
    halo_send,
    halo_recv,
    filt_send,
    filt_recv,
    sig_send,
    sig_recv,
    conv_send,
    conv_recv,
    red_send,
    red_recv,
    row_send,
    row_recv,
):
    me, mt = lax.axis_index(CTX), lax.axis_index(TEN)
    tokens, width = q_hbm.shape
    per = width // nc
    parts = per // PART
    halves = tokens // LANES
    blocks = nc * halves
    outer = blocks // INNER
    step_s = INNER // halves
    share = out.shape[1]

    def partner(j, mine, n):
        step = n // 2 - (j + 1) // 2
        odd = j % 2
        return (mine + step * (1 - odd) + (n - step) * odd) % n

    def remote(src, dst, send, recv, device):
        return pltpu.make_async_remote_copy(
            src_ref=src,
            dst_ref=dst,
            send_sem=send,
            recv_sem=recv,
            device_id=device,
            device_id_type=pl.DeviceIdType.MESH,
        )

    barrier = pltpu.get_barrier_semaphore()

    @pl.loop(0, nc - 1, unroll=True)
    def _(j):
        pl.semaphore_signal(barrier, inc=1, device_id={CTX: partner(j, me, nc)})

    @pl.loop(0, nt - 1, unroll=True)
    def _(j):
        pl.semaphore_signal(barrier, inc=1, device_id={TEN: partner(j, mt, nt)})

    body = pl.ds(HALO, tokens)
    loads = [
        pltpu.make_async_copy(src, dst, load_sem.at[i])
        for i, (src, dst) in enumerate(
            (
                (k_hbm, kbuf.at[body, :]),
                (v_hbm, vbuf.at[body, :]),
                (q_hbm, qbuf.at[body, :]),
                (fwd_hbm, fwd),
                (bwd_hbm, bwd),
                (w_hbm, wbuf),
                (taps_hbm, taps),
                (twist_hbm, twist),
                (skip_hbm, skip),
                (gain_hbm, gain),
            )
        )
    ]
    for i in (0, 1, 6):
        loads[i].start()

    pl.semaphore_wait(barrier, nc - 1 + nt - 1)

    def settle_inputs():
        @pl.when(me < nc - 1)
        def _():
            for copy in halos:
                copy.wait_send()

        @pl.loop(0, nc - 1)
        def _(j):
            p = partner(j, me, nc)
            filter_copy(p).wait_send()
            for part in range(parts):
                signal_copy(part, p).wait_send()

    def settle_conv():
        @pl.loop(0, nc - 1)
        def _(j):
            for group in range(parts + halves - 1):
                conv_copy(group, partner(j, me, nc)).wait_send()

    def settle_sums():
        for c in range(halves):
            for kind, d in messages:
                message(kind, c, d).wait_send()

    def settle_rows():
        @pl.loop(0, nt - 1)
        def _(j):
            for c in range(halves):
                row_copy(c, partner(j, mt, nt)).wait_send()

    halos = [
        remote(
            src.at[pl.ds(tokens - HALO, HALO), :],
            dst.at[pl.ds(0, HALO), :],
            halo_send.at[i],
            halo_recv.at[i],
            {CTX: (me + 1) % nc},
        )
        for i, (src, dst) in enumerate(((k_hbm, kbuf), (v_hbm, vbuf), (q_hbm, qbuf)))
    ]

    @pl.when(me < nc - 1)
    def _():
        for copy in halos:
            copy.start()

    @pl.when(me == 0)
    def _():
        for buf in (kbuf, vbuf, qbuf):
            buf[pl.ds(0, HALO), :] = jnp.zeros((HALO, width), BF16)

    def filter_copy(p):
        return remote(
            filt_hbm.at[pl.ds(pl.multiple_of(p * per, PART), per), :],
            frecv.at[me],
            filt_send.at[p],
            filt_recv.at[me],
            {CTX: p},
        )

    @pl.loop(0, nc - 1, unroll=True)
    def _(j):
        filter_copy(partner(j, me, nc)).start()

    own_filter = pltpu.make_async_copy(
        filt_hbm.at[pl.ds(pl.multiple_of(me * per, PART), per), :], frecv.at[me], filt_recv.at[me]
    )
    own_filter.start()
    for i in (2, 7, 3, 4, 8, 9, 5):
        loads[i].start()

    def feature(buf, r, row, lane):
        wide = buf[pl.ds(row, LANES + HALO), lane].astype(F32)[HALO - 8 :]
        one = pltpu.roll(wide, 1, 0)[8:]
        two = pltpu.roll(wide, 2, 0)[8:]
        return (
            taps[r, pl.ds(0, 1), lane] * wide[8:]
            + taps[r, pl.ds(1, 1), lane] * one
            + taps[r, pl.ds(2, 1), lane] * two
        )

    columns = width // LANES

    def place(i):
        row = pl.multiple_of(i // columns * LANES, LANES)
        col = pl.multiple_of(i % columns * LANES, LANES)
        return row, col

    for i in (6, 0, 1):
        loads[i].wait()

    @pl.when(me > 0)
    def _():
        for i in (0, 1):
            halos[i].wait_recv()

    @pl.loop(0, halves * columns)
    def _(i):
        row, col = place(i)
        lane = pl.ds(col, LANES)
        product = feature(kbuf, 1, row, lane) * feature(vbuf, 2, row, lane)
        mixed[pl.ds(row, LANES), lane] = product.astype(BF16)
        mixed_t[pl.ds(col, LANES), pl.ds(row, LANES)] = product.T.astype(BF16)

    def signal_copy(part, p):
        return remote(
            mixed_t.at[pl.ds(pl.multiple_of(p * per + part * PART, PART), PART), :],
            srecv.at[me, pl.ds(part * PART, PART), :],
            sig_send.at[part, p],
            sig_recv.at[part, me],
            {CTX: p},
        )

    for part in range(parts):

        @pl.loop(0, nc - 1, unroll=True)
        def _(j):
            signal_copy(part, partner(j, me, nc)).start()

        pltpu.make_async_copy(
            mixed_t.at[pl.ds(pl.multiple_of(me * per + part * PART, PART), PART), :],
            srecv.at[me, pl.ds(part * PART, PART), :],
            sig_recv.at[part, me],
        ).start()

    loads[2].wait()

    @pl.when(me > 0)
    def _():
        halos[2].wait_recv()

    @pl.loop(0, halves * columns)
    def _(i):
        row, col = place(i)
        lane = pl.ds(col, LANES)
        qfeat[pl.ds(row, LANES), lane] = feature(qbuf, 0, row, lane)

    def row_at(q, r):
        return (q * INNER + r) * PART

    together = min(GROUP, outer)
    groups = [range(q, q + together) for q in range(0, outer, together)]

    def group_rows(qs):
        return pl.ds(row_at(qs[0], 0), together * INNER * PART)

    left, right = pl.ds(0, LANES), pl.ds(LANES, LANES)

    def outer_forward(recv, part):
        rows = pl.ds(pl.multiple_of(part * PART, PART), PART)
        for b in range(INNER):
            lane = pl.ds(b % halves * LANES, LANES)
            x = [
                times((recv[step_s * a + b // halves, rows, lane].astype(F32), None), turn(-a * SHIFT / outer))
                for a in range(outer)
            ]
            for q, z in enumerate(dft(x, -1)):
                re, im = times(z, turn(-b * (q + SHIFT) / blocks))
                mid[b, q, 0] = re
                mid[b, q, 1] = jnp.zeros_like(re) if im is None else im

    def inner_forward(qs):
        for q in qs:
            y = [(mid[b, q, 0], mid[b, q, 1]) for b in range(INNER)]
            for r, (re, im) in enumerate(dft(y, -1)):
                k1 = q + outer * r
                cos, sin = twist[0, pl.ds(k1, 1), :], twist[1, pl.ds(k1, 1), :]
                put(row_at(q, r), re * cos - im * sin, im * cos + re * sin)

    def inner_backward(qs):
        for q in qs:
            y = []
            for r in range(INNER):
                k1, rows = q + outer * r, pl.ds(row_at(q, r), PART)
                cos, sin = twist[0, pl.ds(k1, 1), :], twist[1, pl.ds(k1, 1), :]
                re, im = dspec[rows, left], dspec[rows, right]
                y.append((re * cos + im * sin, im * cos - re * sin))
            for b, z in enumerate(dft(y, 1)):
                re, im = times(z, turn(b * (q + SHIFT) / blocks))
                mid[b, q, 0] = re
                mid[b, q, 1] = im

    def put(row, re, im):
        rows = pl.ds(row, re.shape[0])
        for lane, x in ((left, re), (right, im)):
            top = x.astype(BF16)
            high[rows, lane] = top
            low[rows, lane] = (x - top.astype(F32)).astype(BF16)

    def product(rows, table):
        a, b = high[rows, :], low[rows, :]
        dot = functools.partial(jnp.dot, preferred_element_type=F32)
        return dot(a, table[0]) + dot(b, table[0]) + dot(a, table[1])

    @pl.loop(0, nc)
    def _(s):
        pltpu.make_async_copy(frecv.at[s], frecv.at[s], filt_recv.at[s]).wait()

    for i in (3, 4, 7):
        loads[i].wait()

    @pl.loop(0, parts)
    def _(part):
        outer_forward(frecv, part)
        for qs in groups:
            inner_forward(qs)
            fspec[part, group_rows(qs), :] = product(group_rows(qs), fwd)

    def conv_slice(group, p):
        if isinstance(group, int) and group >= parts:
            return pl.ds(pl.multiple_of(p * per, PART), per), pl.ds((group - parts + 1) * LANES, LANES)
        return pl.ds(pl.multiple_of(p * per + group * PART, PART), PART), left

    def conv_copy(group, p):
        src = csend.at[p, conv_slice(group, 0)[0], conv_slice(group, 0)[1]]
        return remote(
            src, crecv.at[conv_slice(group, me)], conv_send.at[group, p], conv_recv.at[group, me], {CTX: p}
        )

    def send_conv(group):
        @pl.loop(0, nc - 1)
        def _(j):
            conv_copy(group, partner(j, me, nc)).start()

        pltpu.make_async_copy(
            csend.at[me, conv_slice(group, 0)[0], conv_slice(group, 0)[1]],
            crecv.at[conv_slice(group, me)],
            conv_recv.at[group, me],
        ).start()

    @pl.loop(0, parts)
    def _(part):
        rows16 = pl.ds(pl.multiple_of(part * PART, PART), PART)

        @pl.loop(0, nc, unroll=True)
        def _(s):
            slot = srecv.at[s, rows16, :]
            pltpu.make_async_copy(slot, slot, sig_recv.at[part, s]).wait()

        outer_forward(srecv, part)

        for qs in groups:
            rows = group_rows(qs)
            inner_forward(qs)
            spec = product(rows, fwd)
            re, im = spec[:, :LANES], spec[:, LANES:]
            fre, fim = fspec[part, rows, left], fspec[part, rows, right]
            put(row_at(qs[0], 0), re * fre - im * fim, re * fim + im * fre)
            dspec[rows, :] = product(rows, bwd)
            inner_backward(qs)

        for b in range(INNER):
            lane = pl.ds(b % halves * LANES, LANES)
            y = [(mid[b, q, 0], mid[b, q, 1]) for q in range(outer)]
            for a, z in enumerate(dft(y, 1)):
                csend[step_s * a + b // halves, rows16, lane] = real_part_times(
                    z, turn(a * SHIFT / outer)
                ).astype(BF16)

        send_conv(part)

    for half in range(1, halves):
        send_conv(parts + half - 1)

    def gate(chunk):
        rows = rows_of(chunk)
        sources = LANES // per

        @pl.loop(0, columns)
        def _(i):
            block = partner(i, me // sources, columns)
            for n in range(sources):
                for group in range(parts) if chunk == 0 else [parts + chunk - 1]:
                    slot = crecv.at[conv_slice(group, block * sources + n)]
                    pltpu.make_async_copy(slot, slot, conv_recv.at[group, block * sources + n]).wait()
            lane = pl.ds(pl.multiple_of(block * LANES, LANES), LANES)
            conv = crecv[lane, rows].astype(F32).T
            gated[rows, lane] = (
                qfeat[rows, lane] * (conv + skip[:, lane] * mixed[rows, lane].astype(F32))
            ).astype(BF16)

    def rows_of(chunk):
        return pl.ds(chunk * LANES, LANES)

    ring_at, pair_at = mt % RING, mt // RING
    across = {TEN: (1 - pair_at) * RING + ring_at}

    def term(chunk, pair, ring):
        column = pl.multiple_of((pair * RING + ring) * share, LANES)
        return jnp.dot(gated[rows_of(chunk), :], wbuf[:, pl.ds(column, share)], preferred_element_type=F32)

    upper, lower = pl.ds(0, PIECE), pl.ds(PIECE, LANES - PIECE)
    further = (2, 1, 3)

    def ring_device(d):
        return {TEN: pair_at * RING + (ring_at + d) % RING}

    def message(kind, c, d):
        src, dst, device = {
            "far": lambda: (xsend.at[c, 0, d], xrecv.at[c, 0, d], ring_device(d)),
            "near": lambda: (xsend.at[c, 1, d], xrecv.at[c, 1, d], ring_device(d)),
            "pair": lambda: (ysend.at[c, d], yrecv.at[c, d], across),
            "then_ring": lambda: (yxsend.at[c, d], yxrecv.at[c, d], ring_device(d)),
            "then_pair": lambda: (xysend.at[c], xyrecv.at[c], across),
        }[kind]()
        k = ("far", "near", "pair", "then_ring", "then_pair").index(kind)
        return remote(src, dst, red_send.at[k, c, d], red_recv.at[k, c, d], device)

    messages = [
        (kind, d)
        for kind, ds in (
            ("far", further),
            ("near", further),
            ("pair", (0, 1, 2, 3)),
            ("then_ring", further),
            ("then_pair", (0,)),
        )
        for d in ds
    ]

    def start_across(c):
        for d in (*further, 0):
            t = term(c, 1 - pair_at, (ring_at + d) % RING)
            ysend[c, d] = t[PIECE:].astype(BF16)
            message("pair", c, d).start()
            if d:
                xsend[c, 0, d] = t[:PIECE].astype(BF16)
                message("far", c, d).start()
            else:
                xown[c, 0] = t[:PIECE]

    def start_along(c):
        for d in (*further, 0):
            t = term(c, pair_at, (ring_at + d) % RING)
            yown[c, d] = t[PIECE:]
            if d:
                xsend[c, 1, d] = t[:PIECE].astype(BF16)
                message("near", c, d).start()
            else:
                xown[c, 1] = t[:PIECE]

    def turn_corner(c):
        for d in further:
            message("far", c, d).wait_recv()
        s = xown[c, 0]
        for d in further:
            s = s + xrecv[c, 0, d].astype(F32)
        xysend[c] = s.astype(BF16)
        message("then_pair", c, 0).start()
        for d in further:
            message("pair", c, d).wait_recv()
            yxsend[c, d] = (yown[c, d] + yrecv[c, d].astype(F32)).astype(BF16)
            message("then_ring", c, d).start()

    def row_copy(chunk, p):
        return remote(
            ssend.at[chunk], srow.at[chunk, mt], row_send.at[chunk, p], row_recv.at[chunk, mt], {TEN: p}
        )

    def end_sums(c):
        squares = []

        def finish(rows, parts_of):
            square = jnp.zeros((rows.size, LANES), F32)
            for i in range(share // LANES):
                lane = pl.ds(i * LANES, LANES)
                s = parts_of[0][:, lane]
                for ref in parts_of[1:]:
                    s = s + ref[:, lane].astype(F32)
                mine[c, rows, lane] = s
                square = square + s * s
            squares.append(jnp.sum(square, axis=1, keepdims=True))

        for d in further:
            message("near", c, d).wait_recv()
        message("then_pair", c, 0).wait_recv()
        finish(upper, [xown.at[c, 1], *(xrecv.at[c, 1, d] for d in further), xyrecv.at[c]])
        message("pair", c, 0).wait_recv()
        for d in further:
            message("then_ring", c, d).wait_recv()
        finish(lower, [yown.at[c, 0], yrecv.at[c, 0], *(yxrecv.at[c, d] for d in further)])
        sums = jnp.concatenate(squares, axis=0)
        ssend[c] = jnp.broadcast_to(sums, (LANES, LANES)).T[:8]
        srow[c, mt] = ssend[c]

        @pl.loop(0, nt - 1, unroll=True)
        def _(j):
            row_copy(c, partner(j, mt, nt)).start()

    def normalize(c):
        @pl.loop(0, nt - 1, unroll=True)
        def _(j):
            p = partner(j, mt, nt)
            slot = srow.at[c, p]
            pltpu.make_async_copy(slot, slot, row_recv.at[c, p]).wait()

        s = srow[c, 0]
        for g in range(1, nt):
            s = s + srow[c, g]
        scale = lax.rsqrt(s * (1.0 / (share * nt)) + 1e-06)
        scale = jnp.broadcast_to(scale[:1], (LANES, LANES)).T
        for i in range(share // LANES):
            lane = pl.ds(i * LANES, LANES)
            out[rows_of(c), lane] = (mine[c, :, lane] * scale * gain[:, lane]).astype(BF16)

    settle_inputs()
    loads[8].wait()
    gate(0)
    loads[5].wait()
    start_across(0)
    start_along(0)
    gate(1)
    start_across(1)
    turn_corner(0)
    start_along(1)
    turn_corner(1)
    settle_conv()
    end_sums(0)
    end_sums(1)
    settle_sums()
    loads[9].wait()
    normalize(0)
    normalize(1)

    settle_rows()


def per_device(
    query_proj, key_proj, value_proj, short_taps, long_filter, skip_weight, out_weight, norm_gain
):
    nc, nt = lax.axis_size(CTX), lax.axis_size(TEN)
    tokens, width = query_proj.shape
    features = out_weight.shape[1]
    share = features // nt
    per = width // nc
    parts = per // PART
    blocks = nc * (tokens // LANES)
    outer = blocks // INNER
    halves = tokens // LANES
    fwd, bwd, twist = (jnp.asarray(x) for x in tables(blocks))
    anywhere = pl.BlockSpec(memory_space=pl.ANY)
    vmem = pl.BlockSpec(memory_space=pltpu.VMEM)
    dma = pltpu.SemaphoreType.DMA
    return pl.pallas_call(
        functools.partial(kernel, nc, nt),
        out_shape=pltpu.VMEM((tokens, share), BF16),
        in_specs=[anywhere] * 11,
        out_specs=vmem,
        scratch_shapes=[
            pltpu.VMEM(short_taps.shape, F32),
            pltpu.VMEM((1, width), F32),
            pltpu.VMEM((1, share), F32),
            pltpu.VMEM(twist.shape, F32),
            pltpu.VMEM((tokens + HALO, width), BF16),
            pltpu.VMEM((tokens + HALO, width), BF16),
            pltpu.VMEM((tokens + HALO, width), BF16),
            pltpu.VMEM((width, features), BF16),
            pltpu.VMEM(fwd.shape, BF16),
            pltpu.VMEM(bwd.shape, BF16),
            pltpu.VMEM((tokens, width), F32),
            pltpu.VMEM((tokens, width), BF16),
            pltpu.VMEM((width, tokens), BF16),
            pltpu.VMEM((nc, per, tokens), BF16),
            pltpu.VMEM((nc, per, tokens), BF16),
            pltpu.VMEM((nc, per, tokens), BF16),
            pltpu.VMEM((width, tokens), BF16),
            pltpu.VMEM((INNER, outer, 2, PART, LANES), F32),
            pltpu.VMEM((blocks * PART, 2 * LANES), BF16),
            pltpu.VMEM((blocks * PART, 2 * LANES), BF16),
            pltpu.VMEM((parts, blocks * PART, 2 * LANES), F32),
            pltpu.VMEM((blocks * PART, 2 * LANES), F32),
            pltpu.VMEM((tokens, width), BF16),
            pltpu.VMEM((halves, 2, RING, PIECE, share), BF16),
            pltpu.VMEM((halves, 2, RING, PIECE, share), BF16),
            pltpu.VMEM((halves, 2, PIECE, share), F32),
            pltpu.VMEM((halves, RING, LANES - PIECE, share), BF16),
            pltpu.VMEM((halves, RING, LANES - PIECE, share), BF16),
            pltpu.VMEM((halves, RING, LANES - PIECE, share), F32),
            pltpu.VMEM((halves, RING, LANES - PIECE, share), BF16),
            pltpu.VMEM((halves, RING, LANES - PIECE, share), BF16),
            pltpu.VMEM((halves, PIECE, share), BF16),
            pltpu.VMEM((halves, PIECE, share), BF16),
            pltpu.VMEM((halves, LANES, share), F32),
            pltpu.VMEM((halves, 8, LANES), F32),
            pltpu.VMEM((halves, nt, 8, LANES), F32),
            dma((10,)),
            dma((3,)),
            dma((3,)),
            dma((nc,)),
            dma((nc,)),
            dma((parts, nc)),
            dma((parts, nc)),
            dma((parts + halves - 1, nc)),
            dma((parts + halves - 1, nc)),
            dma((5, halves, RING)),
            dma((5, halves, RING)),
            dma((halves, nt)),
            dma((halves, nt)),
        ],
        compiler_params=pltpu.CompilerParams(
            collective_id=0, has_side_effects=True, vmem_limit_bytes=56 * 1024 * 1024
        ),
    )(
        query_proj,
        key_proj,
        value_proj,
        long_filter,
        out_weight,
        fwd,
        bwd,
        short_taps,
        skip_weight.reshape(1, width),
        norm_gain.reshape(1, share),
        twist,
    )


def solution(mesh):
    placed = (
        P(CTX, TEN),
        P(CTX, TEN),
        P(CTX, TEN),
        P(None, None, TEN),
        P(TEN, CTX),
        P(TEN),
        P(TEN, None),
        P(TEN),
    )
    return jax.shard_map(
        per_device, mesh=mesh, in_specs=placed, out_specs=P(CTX, TEN), check_vma=False
    )
```
